32 devices in a mesh: grp: 8 (over z, x), seq: 4 (over y, core).
Axes of the slice: x: 2, y: 2, z: 4, core: 2. Of those that a mesh axis runs over, the one named last changes fastest.
Arguments:
- tokens: bfloat16 [4096, 1024], P(('grp', 'seq')), may hold values from -6 to 6
- lengths: int32 [8, 3], P('grp'), may hold values from 1 to 128, 256 in all within a row
- cotangent: float32 [4096, 1024], P(('grp', 'seq')), may hold values from -6 to 6
- norm_gain: bfloat16 [2, 2, 1024], P(None, None, 'grp'), may hold values from 0.5 to 1.5
- norm_bias: bfloat16 [2, 2, 1024], P(None, None, 'grp'), may hold values from -2 to 2
- in_weight: bfloat16 [2, 1024, 3072], P(None, None, 'grp'), may hold values from -0.1875 to 0.1875
- in_bias: bfloat16 [2, 3072], P(None, 'grp'), may hold values from -2 to 2
- conv_weight: bfloat16 [2, 3, 3072], P(None, None, 'grp'), may hold values from -3 to 3
- conv_bias: bfloat16 [2, 3072], P(None, 'grp'), may hold values from -2 to 2
- skip_bias: bfloat16 [2, 1024], P(None, 'grp'), may hold values from -4 to 4
- filt_out: bfloat16 [2, 64, 1024], P(None, None, 'grp'), may hold values from -0.25 to 0.25
- out_weight: bfloat16 [2, 1024, 1024], P(None, None, 'grp'), may hold values from -0.1875 to 0.1875
- up_weight: bfloat16 [2, 1024, 4096], P(None, None, 'grp'), may hold values from -0.1875 to 0.1875
- up_bias: bfloat16 [2, 4096], P(None, 'grp'), may hold values from -2 to 2
- down_weight: bfloat16 [2, 4096, 1024], P(None, None, 'grp'), may hold values from -0.09375 to 0.09375
- branch_bias: bfloat16 [2, 2, 1024], P(None, None, 'grp'), may hold values from -2 to 2
- filt_in: float32 [2, 33, 64], replicated, may hold values from -1 to 1
- filt_mid: float32 [2, 64, 64], replicated, may hold values from -0.75 to 0.75
- filt_bias: float32 [2, 2, 64], replicated, may hold values from -3.140625 to 3.140625
- sine_freq: float32 [2, 2, 64], replicated, may hold values from 0.5 to 3
Outputs:
- activations: float32 [4096, 1024], P(('grp', 'seq'))
- input_grad: float32 [4096, 1024], P(('grp', 'seq'))
- norm_gain_grad: float32 [2, 2, 1024], P(None, None, 'grp')
- norm_bias_grad: float32 [2, 2, 1024], P(None, None, 'grp')
- in_weight_grad: float32 [2, 1024, 3072], P(None, None, 'grp')
- in_bias_grad: float32 [2, 3072], P(None, 'grp')
- conv_weight_grad: float32 [2, 3, 3072], P(None, None, 'grp')
- conv_bias_grad: float32 [2, 3072], P(None, 'grp')
- skip_bias_grad: float32 [2, 1024], P(None, 'grp')
- filt_out_grad: float32 [2, 64, 1024], P(None, None, 'grp')
- out_weight_grad: float32 [2, 1024, 1024], P(None, None, 'grp')
- up_weight_grad: float32 [2, 1024, 4096], P(None, None, 'grp')
- up_bias_grad: float32 [2, 4096], P(None, 'grp')
- down_weight_grad: float32 [2, 4096, 1024], P(None, None, 'grp')
- branch_bias_grad: float32 [2, 2, 1024], P(None, None, 'grp')
- filt_in_grad: float32 [2, 33, 64], replicated
- filt_mid_grad: float32 [2, 64, 64], replicated
- filt_bias_grad: float32 [2, 2, 64], replicated
- sine_freq_grad: float32 [2, 2, 64], replicated
The draws below stay inside these ranges and needn't reach their ends.
Inputs may be any that keep to these rules, and one draw needn't show every extreme that they name: Row g lists the lengths of group g's 3 short sequences in order; they sum to 256, and the longest of each row is 128.
All inputs are finite; a program needn't handle non-finite values.
Results may differ from the reference program's by a relative error of at most 0.022.
Values may be sent and summed in bfloat16 or wider, within the bound.
No kernel may reach another device: no remote copies, remote signals or barrier semaphores. Data moves between devices by JAX's collectives and lax.ppermute only.
A program may use at most 384 MiB of HBM per device.

```python
import math
import jax
import jax.numpy as jnp
import numpy as np
from jax import lax

D = 1024
FF = 4096
FILT = 64
EMB = 33
LAYERS = 2
TOK_DEV = 128
LONG = 256
SHORT_MOST = 128
K = 3
TOKENS = 4096
N_GRP = 8
N_SEQ = 4


def levels(stream_key, dims, cuts, low, largest):
    def one(dim, blocks):
        steps = jax.random.uniform(jax.random.fold_in(jax.random.fold_in(stream_key, 6), dim), (blocks,), jnp.float32, low / len(cuts), largest / len(cuts))
        return jnp.repeat(jnp.exp(steps), dims[dim] // blocks).reshape((-1,) + (1,) * (len(dims) - dim - 1))

    level = one(*cuts[0])
    for cut in cuts[1:]:
        level = level * one(*cut)
    return level


def profile(number_of, total, bound, slope):
    portions = [(1 << 20) // math.isqrt(rank ** slope) + 1 for rank in range(2, number_of + 1)]
    surplus, given = total - bound - (number_of - 1), [1] * (number_of - 1)
    while surplus > 0:
        movable = [i for i in range(number_of - 1) if given[i] < bound]
        whole, remaining = sum([portions[i] for i in movable]), surplus
        for i in movable:
            extra = min(bound - given[i], max(1, remaining * portions[i] // whole), surplus)
            given[i] = given[i] + extra
            surplus = surplus - extra
    return np.array([bound] + given)


def ragged(stream_key, count, total, reach, slope):
    if count == 2:
        one = jax.random.randint(stream_key, (), max(1, total - reach), min(reach, total - 1) + 1)
        return jnp.stack([one, total - one])
    sizes = jnp.asarray(profile(count, total, reach, slope), jnp.int32)
    pairs = (count - 1) // 2
    source_of, taker = sizes[1:1 + 2 * pairs:2], sizes[2:2 + 2 * pairs:2]
    margin = jnp.minimum(source_of - 1, reach - taker)
    shifted = jax.random.randint(jax.random.fold_in(stream_key, 1), (pairs,), 0, 1 << 20) % (margin + 1)
    sizes = sizes.at[1:1 + 2 * pairs:2].set(source_of - shifted).at[2:2 + 2 * pairs:2].set(taker + shifted)
    return sizes[jax.random.permutation(jax.random.fold_in(stream_key, 2), count)]


def centred(stream_key, shape, deviation, bound, split=(), kind=jnp.bfloat16):
    level = levels(stream_key, shape, split, -0.22, 0.18) if split else 1.0
    values = jax.random.normal(stream_key, shape, jnp.float32) * deviation * level
    return jnp.minimum(jnp.maximum(values, -bound), bound).astype(kind)


def setup_inputs(seed: int = 0) -> dict:
    splits = jax.random.split(jax.random.key(seed), 21)
    return {
        "tokens": centred(splits[0], (TOKENS, D), 1.0, 6.0, ((0, 32),)),
        "lengths": jax.vmap(lambda own: ragged(own, K, LONG, SHORT_MOST, 2))(jax.random.split(splits[1], N_GRP)).reshape((N_GRP, K)).astype(jnp.int32),
        "cotangent": centred(splits[2], (TOKENS, D), 1.0, 6.0, ((0, 32),), jnp.float32),
        "norm_gain": jnp.clip(1.0 + 0.1 * jax.random.normal(splits[3], (LAYERS, 2, D), jnp.float32), 0.5, 1.5).astype(jnp.bfloat16),
        "norm_bias": centred(splits[4], (LAYERS, 2, D), 0.3, 2.0, ((2, 8),)),
        "in_weight": centred(splits[5], (LAYERS, D, 3 * D), D ** -0.5, 0.1875, ((2, 8),)),
        "in_bias": centred(splits[6], (LAYERS, 3 * D), 0.3, 2.0, ((1, 8),)),
        "conv_weight": centred(splits[7], (LAYERS, 3, 3 * D), 0.5, 3.0, ((2, 8),)),
        "conv_bias": centred(splits[8], (LAYERS, 3 * D), 0.3, 2.0, ((1, 8),)),
        "skip_bias": centred(splits[9], (LAYERS, D), 1.0, 4.0, ((1, 8),)),
        "filt_out": centred(splits[10], (LAYERS, FILT, D), (0.7 * LONG ** -0.5), 0.25, ((2, 8),)),
        "out_weight": centred(splits[11], (LAYERS, D, D), D ** -0.5, 0.1875, ((2, 8),)),
        "up_weight": centred(splits[12], (LAYERS, D, FF), D ** -0.5, 0.1875, ((2, 8),)),
        "up_bias": centred(splits[13], (LAYERS, FF), 0.3, 2.0, ((1, 8),)),
        "down_weight": centred(splits[14], (LAYERS, FF, D), FF ** -0.5, 0.09375, ((2, 8),)),
        "branch_bias": centred(splits[15], (LAYERS, 2, D), 0.3, 2.0, ((2, 8),)),
        "filt_in": centred(splits[16], (LAYERS, EMB, FILT), EMB ** -0.5, 1.0, (), jnp.float32),
        "filt_mid": centred(splits[17], (LAYERS, FILT, FILT), FILT ** -0.5, 0.75, (), jnp.float32),
        "filt_bias": jnp.clip(jax.random.uniform(splits[18], (LAYERS, 2, FILT), jnp.float32, -3.140625, 3.140625), -3.140625, 3.140625),
        "sine_freq": jnp.clip(jnp.exp(jax.random.uniform(splits[19], (LAYERS, 2, FILT), jnp.float32, math.log(0.5), math.log(3.0))), 0.5, 3.0),
    }


EPS = 1e-05
FAST = math.log(0.01) / 0.3
SLOW = math.log(0.01) / 1.5

@jax.custom_vjp
def low(v):
    return lax.optimization_barrier(v.astype(jnp.bfloat16)).astype(jnp.float32)

@jax.custom_vjp
def low_back(v):
    return v

def low_keep(v):
    return (low(v), None)

def low_pass(kept, grad):
    return (grad,)

def back_keep(v):
    return (v, None)

def back_low(kept, grad):
    return (low(grad),)
low.defvjp(low_keep, low_pass)
low_back.defvjp(back_keep, back_low)

def matmul(left, right):
    return jnp.dot(left, right, precision=lax.Precision.HIGHEST, preferred_element_type=jnp.float32)

def norm_rows(value, gain, shift):
    center = value - lax.optimization_barrier(jnp.mean(value, axis=-1, keepdims=True))
    spread = lax.optimization_barrier(jnp.mean(center * center, axis=-1, keepdims=True))
    return center * lax.rsqrt(spread + EPS) * gain + shift

def positions(length):
    index = jnp.arange(length, dtype=jnp.int32).astype(jnp.float32)
    tpos = index / (length - 1)
    bands = 0.0001 + (15.0 - 0.0001) * jnp.arange(16, dtype=jnp.int32).astype(jnp.float32) / 15.0
    angle = 2.0 * math.pi / length * index[:, None] * bands[None, :]
    return (jnp.concatenate([tpos[:, None], jnp.cos(angle), -jnp.sin(angle)], axis=1), tpos)

def rates(first, count, width):
    channel = (first + jnp.arange(count, dtype=jnp.int32)).astype(jnp.float32)
    return jnp.abs(FAST + (SLOW - FAST) * channel / (width - 1))

def doc_begin(lens, total):
    starts = (total // 2 + jnp.cumsum(lens) - lens).astype(jnp.int32)
    every = jnp.concatenate([jnp.zeros((1,), jnp.int32), starts])
    where_at = jnp.arange(total, dtype=jnp.int32)
    begin = lax.optimization_barrier(jnp.max(jnp.where(every[:, None] <= where_at[None, :], every[:, None], 0), axis=0))
    return (starts, begin)

def causal(signal, filt):
    length = signal.shape[-1]
    size = 2 * length
    spec = jnp.fft.rfft(signal, n=size, axis=-1) * jnp.fft.rfft(filt, n=size, axis=-1)
    return jnp.fft.irfft(spec, n=size, axis=-1)[..., :length]

def mix_group(chan, lens, taps, tap_bias, skip, filt):
    width = chan.shape[1]
    total = chan.shape[2]
    long_len = total // 2
    starts, begin = doc_begin(lens, total)
    where_at = jnp.arange(total, dtype=jnp.int32)
    taps3 = taps.reshape(3, 3, width)
    mixed = tap_bias.reshape(3, width)[:, :, None] + taps3[0][:, :, None] * chan
    for lag in (1, 2):
        moved = jnp.pad(chan, ((0, 0), (0, 0), (lag, 0)))[:, :, :total]
        mixed = mixed + taps3[lag][:, :, None] * jnp.where(where_at - lag >= begin, moved, 0.0)
    prod = mixed[1] * mixed[2]
    head = causal(prod[:, :long_len], filt)
    index = starts[:, None] + jnp.arange(SHORT_MOST, dtype=jnp.int32)[None, :]
    padded = jnp.pad(prod, ((0, 0), (0, SHORT_MOST)))
    windows = jnp.take(padded, index, axis=1)
    local = causal(windows, filt[:, None, :SHORT_MOST])
    keep = jnp.arange(SHORT_MOST, dtype=jnp.int32)[None, :] < lens[:, None]
    local = jnp.where(keep, local, 0.0)
    tail = jnp.zeros_like(padded).at[:, index].add(local)
    conv = jnp.concatenate([head, tail[:, long_len:total]], axis=1)
    return mixed[0] * (conv + skip[:, None] * prod)

def forward(state, lengths, gains, shifts, w_in, b_in, taps, tap_bias, skip, fout, w_out, w_up, b_up, w_down, b_branch, fin, fmid, fbias, freq):
    total = TOK_DEV * N_SEQ
    long_len = total // 2
    feats, tpos = positions(long_len)
    decay = jnp.exp(-rates(0, D, D)[:, None] * tpos[None, :])
    for layer in range(LAYERS):
        normed = low(norm_rows(state, gains[layer, 0], shifts[layer, 0]))
        proj = low(low_back(matmul(normed, w_in[layer]) + b_in[layer]))
        chan = jnp.transpose(proj.reshape(N_GRP, total, 3, D), (0, 2, 3, 1))
        inner = jnp.sin(freq[layer, 0] * (matmul(feats, fin[layer]) + fbias[layer, 0]))
        inner = jnp.sin(freq[layer, 1] * (matmul(inner, fmid[layer]) + fbias[layer, 1]))
        filt = jnp.einsum('tk,kc->ct', inner, fout[layer], precision=lax.Precision.HIGHEST) * decay
        mixed = jax.vmap(mix_group, in_axes=(0, 0, None, None, None, None))(chan, lengths, taps[layer], tap_bias[layer], skip[layer], filt)
        y_tok = low(low_back(jnp.transpose(mixed, (0, 2, 1)).reshape(N_GRP * total, D)))
        mid = state + low_back(matmul(y_tok, w_out[layer]) + b_branch[layer, 0])
        normed2 = low(norm_rows(mid, gains[layer, 1], shifts[layer, 1]))
        pre = low_back(matmul(normed2, w_up[layer]) + b_up[layer])
        hidden = low(jax.nn.gelu(pre, approximate=False))
        state = mid + low_back(matmul(hidden, w_down[layer]) + b_branch[layer, 1])
    return state

def reference(tokens, lengths, cotangent, norm_gain, norm_bias, in_weight, in_bias, conv_weight, conv_bias, skip_bias, filt_out, out_weight, up_weight, up_bias, down_weight, branch_bias, filt_in, filt_mid, filt_bias, sine_freq):
    weights = tuple((w.astype(jnp.float32) for w in (norm_gain, norm_bias, in_weight, in_bias, conv_weight, conv_bias, skip_bias, filt_out, out_weight, up_weight, up_bias, down_weight, branch_bias, filt_in, filt_mid, filt_bias, sine_freq)))

    def run(state, *params):
        return forward(state, lengths, *params)
    result, pull = jax.vjp(run, tokens.astype(jnp.float32), *weights)
    grads = pull(cotangent.astype(jnp.float32))
    return (result, grads[0], grads[1], grads[2], grads[3], grads[4], grads[5], grads[6], grads[7], grads[8], grads[9], grads[10], grads[11], grads[12], grads[13], grads[14], grads[15], grads[16], grads[17])
```

```python
import math

import jax
import jax.numpy as jnp
from jax import lax
from jax.sharding import PartitionSpec as P

EPS = 1e-05
HIGH = lax.Precision.HIGHEST
FAST = math.log(0.01) / 0.3
SLOW = math.log(0.01) / 1.5
F32 = jnp.float32
BF = jnp.bfloat16
INV_SQRT2 = 1.0 / math.sqrt(2.0)
INV_SQRT2PI = 1.0 / math.sqrt(2.0 * math.pi)


def dot(a, b, da, db):
    return lax.dot_general(a, b, (((da,), (db,)), ((), ())), preferred_element_type=F32)


def pick(v, index, axis):
    return lax.dynamic_index_in_dim(v, index, axis, keepdims=False)


class Comm:
    def __init__(self):
        self.n_grp = lax.axis_size("grp")
        self.n_seq = lax.axis_size("seq")
        self.nz = self.n_grp // 2
        self.ny = self.n_seq // 2
        g = lax.axis_index("grp")
        s = lax.axis_index("seq")
        self.g, self.s = g, s
        self.z, self.x = g // 2, g % 2
        self.y, self.c = s // 2, s % 2

    @staticmethod
    def flip(v, axis, size):
        return lax.ppermute(v, axis, [(i, i ^ 1) for i in range(size)])

    @staticmethod
    def turn(v, axis, size, k):
        half = size // 2
        perm = [(2 * i + j, 2 * ((i + k) % half) + j) for i in range(half) for j in range(2)]
        return lax.ppermute(v, axis, perm)

    def _gather(self, v, axis, size, major, minor):
        half = size // 2
        if half > 4:
            return lax.all_gather(v, axis, axis=0, tiled=False)
        parts = [v] + [self.turn(v, axis, size, k) for k in range(1, half)]
        others = [self.flip(p, axis, size) for p in parts]
        if half == 2:
            zero = major == 0
            mine = jnp.stack([jnp.where(zero, parts[0], parts[1]), jnp.where(zero, parts[1], parts[0])])
            them = jnp.stack([jnp.where(zero, others[0], others[1]), jnp.where(zero, others[1], others[0])])
        else:
            order = jnp.mod(major - jnp.arange(half), half)
            mine = jnp.stack([pick(jnp.stack(parts), order[i], 0) for i in range(half)])
            them = jnp.stack([pick(jnp.stack(others), order[i], 0) for i in range(half)])
        first = jnp.where(minor == 0, mine, them)
        second = jnp.where(minor == 0, them, mine)
        return jnp.stack([first, second], axis=1).reshape((size,) + v.shape)

    def gather_seq(self, v):
        return self._gather(v, "seq", self.n_seq, self.y, self.c)

    def gather_grp(self, v):
        half = self.nz
        slab = jnp.zeros((half,) + v.shape, v.dtype)
        zeros = (0,) * v.ndim
        for k in range(half):
            part = v if k == 0 else self.turn(v, "grp", self.n_grp, k)
            slab = lax.dynamic_update_slice(slab, part[None], (jnp.mod(self.z - k, half),) + zeros)
        other = self.flip(slab, "grp", self.n_grp)
        first = jnp.where(self.x == 0, slab, other)
        second = jnp.where(self.x == 0, other, slab)
        return jnp.stack([first, second], axis=1).reshape((self.n_grp,) + v.shape)

    def _scatter(self, v, axis, size, major, minor, kind):
        half = size // 2
        if half > 4:
            return lax.psum_scatter(v.astype(kind), axis, scatter_dimension=0, tiled=False).astype(F32)
        v = v.reshape((half, 2) + v.shape[1:])
        got = self.flip(pick(v, 1 - minor, 1).astype(kind), axis, size)
        mine = pick(v, minor, 1).astype(F32) + got.astype(F32)
        total = pick(mine, major, 0)
        for k in range(1, half):
            sent = pick(mine, jnp.mod(major + k, half), 0).astype(kind)
            total = total + self.turn(sent, axis, size, k).astype(F32)
        return total

    def scatter_seq(self, v, kind=BF):
        return self._scatter(v, "seq", self.n_seq, self.y, self.c, kind)

    def scatter_grp(self, v, kind=BF):
        return self._scatter(v, "grp", self.n_grp, self.z, self.x, kind)

    def sum_all(self, v, axis, size):
        half = size // 2
        if half > 4:
            return lax.psum(v, axis)
        v = v + self.flip(v, axis, size)
        total = v
        for k in range(1, half):
            total = total + self.turn(v, axis, size, k)
        return total


def norm_stats(value):
    center = value - jnp.mean(value, axis=-1, keepdims=True)
    scale = lax.rsqrt(jnp.mean(center * center, axis=-1, keepdims=True) + EPS)
    return center * scale, scale


def norm_back(grad, hat, scale, gain):
    inner = grad * gain
    mean_one = jnp.mean(inner, axis=-1, keepdims=True)
    mean_two = jnp.mean(inner * hat, axis=-1, keepdims=True)
    return scale * (inner - mean_one - hat * mean_two), jnp.sum(grad * hat, axis=0), jnp.sum(grad, axis=0)


def positions(length):
    index = jnp.arange(length, dtype=jnp.int32).astype(F32)
    tpos = index / (length - 1)
    bands = 0.0001 + (15.0 - 0.0001) * jnp.arange(16, dtype=jnp.int32).astype(F32) / 15.0
    angle = 2.0 * math.pi / length * index[:, None] * bands[None, :]
    return (jnp.concatenate([tpos[:, None], jnp.cos(angle), -jnp.sin(angle)], axis=1), tpos)


def odd_table(size, place):
    freq = 2 * jnp.arange(size // 2, dtype=jnp.int32) + 1
    turn = jnp.bitwise_and(freq[:, None] * place[None, :], 2 * size - 1)
    angle = turn.astype(F32) * (math.pi / size)
    return jnp.stack([jnp.cos(angle), -jnp.sin(angle)])


def filter_of(fin, fmid, fbias, freq, fout, feats, decay):
    inner = jnp.sin(freq[0] * (jnp.dot(feats, fin, precision=HIGH) + fbias[0]))
    inner = jnp.sin(freq[1] * (jnp.dot(inner, fmid, precision=HIGH) + fbias[1]))
    return jnp.dot(inner, fout, precision=HIGH) * decay


def lagged(v, lag, mask):
    return jnp.where(mask[None, :, None], jnp.pad(v, ((0, 0), (lag, 0), (0, 0)))[:, : v.shape[1]], 0.0)


def ahead(v, lag):
    return jnp.pad(v, ((0, 0), (0, lag), (0, 0)))[:, lag:]


def times(ar, ai, br, bi):
    return ar * br - ai * bi, ar * bi + ai * br


def times_conj(ar, ai, br, bi):
    return ar * br + ai * bi, ai * br - ar * bi


class Mixer:
    def __init__(self, lens, total, most):
        half = total // 2
        self.half, self.most, self.total, self.count = half, most, total, lens.shape[0]
        starts = half + jnp.cumsum(lens) - lens
        place = jnp.arange(total, dtype=jnp.int32)
        begin = jnp.zeros((total,), jnp.int32)
        for k in range(lens.shape[0]):
            begin = jnp.where(starts[k] <= place, starts[k], begin)
        self.masks = [None] + [place - lag >= begin for lag in (1, 2)]
        self.long = odd_table(2 * half, place[:half]).reshape(2 * half, half).astype(BF)
        self.short0 = odd_table(2 * most, place[:most]).reshape(2 * most, most).astype(BF)
        tail = place[half:]
        tables = []
        for k in range(lens.shape[0]):
            rel = tail - starts[k]
            inside = (rel >= 0) & (rel < lens[k])
            table = odd_table(2 * most, jnp.where(inside, rel, 0))
            tables.append(jnp.where(inside[None, None, :], table, 0.0))
        self.short = jnp.stack(tables).reshape(lens.shape[0] * 2 * most, total - half).astype(BF)

    def split(self, long, short):
        chans = long.shape[-1]
        long = long.reshape(2, self.half, chans)
        short = short.reshape(self.count, 2, self.most, chans)
        return long[0], long[1], short[:, 0], short[:, 1]

    def forth(self, v):
        v = v.astype(BF)
        return self.split(dot(self.long, v[: self.half], 1, 0), dot(self.short, v[self.half :], 1, 0))

    def back(self, spec):
        lr, li, sr, si = spec
        long = jnp.stack([lr, li]).reshape(2 * self.half, -1) * (1.0 / self.half)
        short = jnp.stack([sr, si], axis=1).reshape(self.count * 2 * self.most, -1) * (1.0 / self.most)
        return jnp.concatenate([dot(self.long, long.astype(BF), 0, 0), dot(self.short, short.astype(BF), 0, 0)])

    def filt_spec(self, filt):
        filt = filt.astype(BF)
        long = dot(self.long, filt, 1, 0)
        short = dot(self.short0, filt[: self.most], 1, 0)
        return long[: self.half], long[self.half :], short[: self.most], short[self.most :]

    def filt_back(self, grads):
        lr, li, sr, si = grads
        long = jnp.concatenate([lr, li]) * (1.0 / self.half)
        short = jnp.concatenate([sr, si]) * (1.0 / self.most)
        head = dot(self.short0, short.astype(BF), 0, 0)
        return dot(self.long, long.astype(BF), 0, 0) + jnp.pad(head, ((0, self.half - self.most), (0, 0)))


def body(
    tokens,
    lengths,
    cotangent,
    norm_gain,
    norm_bias,
    in_weight,
    in_bias,
    conv_weight,
    conv_bias,
    skip_bias,
    filt_out,
    out_weight,
    up_weight,
    up_bias,
    down_weight,
    branch_bias,
    filt_in,
    filt_mid,
    filt_bias,
    sine_freq,
):
    comm = Comm()
    n_grp, n_seq, s = comm.n_grp, comm.n_seq, comm.s
    depth = norm_gain.shape[0]
    tok_rows, width = tokens.shape
    total = tok_rows * n_seq
    cols = width // n_grp
    q = cols // n_seq
    ff_shard = up_weight.shape[2]
    f = ff_shard // n_seq
    hid = filt_out.shape[1]
    chans = n_grp * q

    def unit_in(l):
        return pick(in_weight[l].T.reshape(3, n_seq, q, width), s, 1).reshape(3 * q, width)

    def unit_out(l):
        return pick(out_weight[l].reshape(n_grp, n_seq, q, cols), s, 1).reshape(chans, cols).T

    def unit_up(l):
        return lax.dynamic_slice_in_dim(up_weight[l], s * f, f, 1).T

    def unit_down(l):
        return pick(down_weight[l].reshape(n_grp, n_seq, f, cols), s, 1).reshape(n_grp * f, cols).T

    tok_small = [norm_gain, norm_bias, branch_bias]
    seq_small = [
        pick(in_bias.reshape(depth, 3, n_seq, q), s, 2),
        pick(conv_weight.reshape(depth, 3, 3, n_seq, q), s, 3),
        pick(conv_bias.reshape(depth, 3, n_seq, q), s, 2),
        pick(skip_bias.reshape(depth, n_seq, q), s, 1),
        pick(filt_out.reshape(depth, hid, n_seq, q), s, 2),
        pick(up_bias.reshape(depth, n_seq, f), s, 1),
    ]
    shapes = [v.shape for v in tok_small + seq_small]
    sizes = [math.prod(shape) for shape in shapes]
    packed = jnp.concatenate([v.reshape(-1) for v in tok_small + seq_small])
    fill = -packed.shape[0] % 2048
    packed = comm.gather_grp(jnp.pad(packed, (0, fill)).reshape(-1, 128)).reshape(n_grp, -1).astype(F32)
    spread, at = [], 0
    for shape, size in zip(shapes, sizes):
        spread.append(packed[:, at : at + size].reshape((n_grp,) + shape))
        at += size

    def last(v):
        return jnp.moveaxis(v, 0, -2).reshape(v.shape[1:-1] + (n_grp * v.shape[-1],))

    def streams(v):
        v = jnp.moveaxis(v, 0, -3)
        return v.reshape(v.shape[:-3] + (3, n_grp * q))

    gains, shifts, b_branch = (last(v) for v in spread[:3])
    b_in, taps, tap_bias = (streams(v) for v in spread[3:6])
    skip, fout, b_up = (last(v) for v in spread[6:9])

    weights = []
    for l in range(depth):
        w_in = comm.gather_grp(unit_in(l)).reshape(3 * chans, width)
        w_out = comm.gather_grp(unit_out(l)).reshape(width, chans)
        w_up = comm.gather_grp(unit_up(l)).reshape(n_grp * f, width)
        w_down = comm.gather_grp(unit_down(l)).reshape(width, n_grp * f)
        weights.append((w_in, w_out, w_up, w_down))

    lens = lengths[0]
    mixer = Mixer(lens, total, total // 4)
    feats, tpos = positions(total // 2)
    channel = (
        jnp.arange(n_grp, dtype=jnp.int32)[:, None] * cols + s * q + jnp.arange(q, dtype=jnp.int32)[None, :]
    ).reshape(-1).astype(F32)
    rate = jnp.abs(FAST + (SLOW - FAST) * channel / (width - 1))
    decay = jnp.exp(-tpos[:, None] * rate[None, :])

    state = tokens.astype(F32)
    saved = []
    for l in range(depth):
        w_in, w_out, w_up, w_down = weights[l]
        filt, filt_pull = jax.vjp(
            lambda *a: filter_of(*a, feats, decay),
            filt_in[l], filt_mid[l], filt_bias[l], sine_freq[l], fout[l],
        )
        hat1, scale1 = norm_stats(state)
        normed = (hat1 * gains[l, 0] + shifts[l, 0]).astype(BF)
        normed = comm.gather_seq(normed).reshape(total, width)
        proj = dot(normed, w_in, 1, 1) + b_in[l].reshape(-1)
        proj = jnp.transpose(proj.astype(BF).reshape(total, 3, chans), (1, 0, 2))
        chan = proj.astype(F32)
        z = tap_bias[l][:, None, :] + taps[l, 0][:, None, :] * chan
        for lag in (1, 2):
            z = z + taps[l, lag][:, None, :] * lagged(chan, lag, mixer.masks[lag])
        prod = z[1] * z[2]
        h_lr, h_li, h_sr, h_si = mixer.filt_spec(filt)
        x_lr, x_li, x_sr, x_si = mixer.forth(prod)
        conv = mixer.back(times(x_lr, x_li, h_lr, h_li) + times(x_sr, x_si, h_sr, h_si))
        inner = conv + skip[l] * prod
        mixed = (z[0] * inner).astype(BF)
        part = dot(mixed, w_out, 1, 1)
        mid = state + comm.scatter_seq(part.reshape(n_seq, tok_rows, width)) + b_branch[l, 0]
        hat2, scale2 = norm_stats(mid)
        normed2 = (hat2 * gains[l, 1] + shifts[l, 1]).astype(BF)
        normed2 = comm.gather_seq(normed2).reshape(total, width)
        pre = dot(normed2, w_up, 1, 1) + b_up[l]
        cdf = 0.5 * (1.0 + lax.erf(pre * INV_SQRT2))
        hidden = (pre * cdf).astype(BF)
        slope = cdf + pre * (jnp.exp(-0.5 * pre * pre) * INV_SQRT2PI)
        part = dot(hidden, w_down, 1, 1)
        state = mid + comm.scatter_seq(part.reshape(n_seq, tok_rows, width)) + b_branch[l, 1]
        saved.append((filt_pull, hat1, scale1, normed, chan, z, prod, inner, (h_lr, h_li, h_sr, h_si),
                      (x_lr, x_li, x_sr, x_si), mixed, hat2, scale2, normed2, slope, hidden))

    grad = cotangent
    units = [None] * depth
    tok_grads, seq_grads, net_grads = [None] * depth, [None] * depth, [None] * depth

    def chunk(v):
        return comm.scatter_grp(v.astype(BF).reshape((n_grp, v.shape[0] // n_grp) + v.shape[1:])).astype(BF)

    for l in reversed(range(depth)):
        w_in, w_out, w_up, w_down = weights[l]
        (filt_pull, hat1, scale1, normed, chan, z, prod, inner, (h_lr, h_li, h_sr, h_si),
         (x_lr, x_li, x_sr, x_si), mixed, hat2, scale2, normed2, slope, hidden) = saved[l]
        low = grad.astype(BF)
        g_two = jnp.sum(low.astype(F32), axis=0)
        low = comm.gather_seq(low).reshape(total, width)
        u_down = chunk(dot(low, hidden, 0, 0))
        g_pre = (dot(low, w_down, 1, 0) * slope).astype(BF)
        g_up_bias = jnp.sum(g_pre.astype(F32), axis=0)
        part = dot(g_pre, w_up, 1, 0)
        u_up = chunk(dot(g_pre, normed2, 0, 0))
        g_normed2 = comm.scatter_seq(part.reshape(n_seq, tok_rows, width))
        g_mid, gain2, shift2 = norm_back(g_normed2, hat2, scale2, gains[l, 1])
        g_mid = g_mid + grad
        low = g_mid.astype(BF)
        g_one = jnp.sum(low.astype(F32), axis=0)
        low = comm.gather_seq(low).reshape(total, width)
        u_out = chunk(dot(low, mixed, 0, 0))
        g_y = dot(low, w_out, 1, 0).astype(BF).astype(F32)
        g_conv = g_y * z[0]
        g_skip = jnp.sum(g_conv * prod, axis=0)
        y_lr, y_li, y_sr, y_si = mixer.forth(g_conv)
        corr = mixer.back(times_conj(y_lr, y_li, h_lr, h_li) + times_conj(y_sr, y_si, h_sr, h_si))
        f_lr, f_li = times_conj(y_lr, y_li, x_lr, x_li)
        f_sr, f_si = times_conj(y_sr, y_si, x_sr, x_si)
        g_filt = mixer.filt_back((f_lr, f_li, jnp.sum(f_sr, axis=0), jnp.sum(f_si, axis=0)))
        g_prod = corr + skip[l] * g_conv
        g_z = jnp.stack([g_y * inner, g_prod * z[2], g_prod * z[1]])
        g_taps = [jnp.sum(g_z * chan, axis=1)]
        g_proj = taps[l, 0][:, None, :] * g_z
        for lag in (1, 2):
            kept = jnp.where(mixer.masks[lag][None, :, None], g_z, 0.0)
            g_taps.append(jnp.sum(g_z * lagged(chan, lag, mixer.masks[lag]), axis=1))
            g_proj = g_proj + taps[l, lag][:, None, :] * ahead(kept, lag)
        g_proj = jnp.transpose(g_proj.astype(BF), (1, 0, 2)).reshape(total, 3 * chans)
        g_in_bias = jnp.sum(g_proj.astype(F32), axis=0).reshape(3, chans)
        part = dot(g_proj, w_in, 1, 0)
        u_in = chunk(dot(g_proj, normed, 0, 0))
        g_normed = comm.scatter_seq(part.reshape(n_seq, tok_rows, width))
        g_state, gain1, shift1 = norm_back(g_normed, hat1, scale1, gains[l, 0])
        grad = g_mid + g_state
        units[l] = (u_in, u_out, u_up, u_down)
        pulled = filt_pull(g_filt)
        net_grads[l] = pulled[:4]
        tok_grads[l] = (jnp.stack([gain1, gain2]), jnp.stack([shift1, shift2]), jnp.stack([g_one, g_two]))
        seq_grads[l] = (g_in_bias, jnp.stack(g_taps), jnp.sum(g_z, axis=1), g_skip, pulled[4], g_up_bias)

    def whole(place):
        return [comm.gather_seq(units[l][place]).astype(F32) for l in range(depth)]

    in_grad = jnp.stack([
        jnp.transpose(v.reshape(n_seq, 3, q, width), (3, 1, 0, 2)).reshape(width, 3 * cols) for v in whole(0)])
    out_grad = jnp.stack([
        jnp.transpose(v.reshape(n_seq, cols, n_grp, q), (2, 0, 3, 1)).reshape(width, cols) for v in whole(1)])
    up_grad = jnp.stack([jnp.transpose(v, (2, 0, 1)).reshape(width, ff_shard) for v in whole(2)])
    down_grad = jnp.stack([
        jnp.transpose(v.reshape(n_seq, cols, n_grp, f), (2, 0, 3, 1)).reshape(n_grp * ff_shard, cols)
        for v in whole(3)])

    def by_owner(v):
        v = v.reshape(v.shape[:-1] + (n_grp, v.shape[-1] // n_grp))
        return jnp.moveaxis(v, -2, 0).reshape(n_grp, -1)

    def by_owner3(v):
        v = v.reshape(v.shape[:-2] + (n_grp, 3, q))
        return jnp.moveaxis(v, -3, 0).reshape(n_grp, -1)

    tok_all = [jnp.stack(v) for v in zip(*tok_grads)]
    seq_all = [jnp.stack(v) for v in zip(*seq_grads)]
    tok_flat = jnp.concatenate([by_owner(v) for v in tok_all], axis=1)
    seq_flat = jnp.concatenate(
        [by_owner3(v) for v in seq_all[:3]] + [by_owner(v) for v in seq_all[3:]], axis=1)
    tok_len, seq_len = tok_flat.shape[1], seq_flat.shape[1]
    flat = jnp.concatenate([tok_flat, seq_flat], axis=1)
    flat = jnp.pad(flat, ((0, 0), (0, -flat.shape[1] % 1024)))
    small = comm.scatter_grp(flat.reshape(n_grp, -1, 128), F32).reshape(-1)
    tok_sum = comm.sum_all(small[:tok_len].reshape(-1, 128), "seq", n_seq).reshape(-1)
    seq_part = jnp.pad(small[tok_len : tok_len + seq_len], (0, -seq_len % 1024)).reshape(-1, 128)
    seq_sum = comm.gather_seq(seq_part).reshape(n_seq, -1)[:, :seq_len]
    norm_gain_grad, norm_bias_grad, branch_grad = tok_sum.reshape(3, depth, 2, cols)
    pieces, at = [], 0
    for shape in shapes[3:]:
        size = math.prod(shape)
        part = seq_sum[:, at : at + size].reshape((n_seq,) + shape)
        at += size
        part = jnp.moveaxis(part, 0, -2)
        pieces.append(part)
    in_bias_grad = pieces[0].reshape(depth, 3 * cols)
    taps_grad = pieces[1].reshape(depth, 3, 3 * cols)
    tap_bias_grad = pieces[2].reshape(depth, 3 * cols)
    skip_grad = pieces[3].reshape(depth, cols)
    fout_grad = pieces[4].reshape(depth, hid, cols)
    up_bias_grad = pieces[5].reshape(depth, ff_shard)

    nets = [jnp.stack(v) for v in zip(*net_grads)]
    flat = jnp.concatenate([v.reshape(-1) for v in nets])
    flat = jnp.pad(flat, (0, -flat.shape[0] % 1024)).reshape(-1, 128)
    flat = comm.sum_all(comm.sum_all(flat, "seq", n_seq), "grp", n_grp).reshape(-1)
    shared, at = [], 0
    for v in nets:
        shared.append(flat[at : at + v.size].reshape(v.shape))
        at += v.size
    return (
        state, grad, norm_gain_grad, norm_bias_grad, in_grad, in_bias_grad, taps_grad, tap_bias_grad,
        skip_grad, fout_grad, out_grad, up_grad, up_bias_grad, down_grad, branch_grad,
        shared[0], shared[1], shared[2], shared[3],
    )


def solution(mesh):
    tok = P(("grp", "seq"), None)
    last3, last2 = P(None, None, "grp"), P(None, "grp")
    in_specs = (
        tok, P("grp", None), tok, last3, last3, last3, last2, last3, last2, last2,
        last3, last3, last3, last2, last3, last3, P(), P(), P(), P(),
    )
    out_specs = (
        tok, tok, last3, last3, last3, last2, last3, last2, last2, last3,
        last3, last3, last2, last3, last3, P(), P(), P(), P(),
    )
    return jax.shard_map(body, mesh=mesh, in_specs=in_specs, out_specs=out_specs, check_vma=False)
```

```python
import math

import jax
import jax.numpy as jnp
from jax import lax
from jax.experimental import pallas as pl
from jax.experimental.pallas import tpu as pltpu
from jax.sharding import PartitionSpec as P

EPS = 1e-05
HIGH = lax.Precision.HIGHEST
FAST = math.log(0.01) / 0.3
SLOW = math.log(0.01) / 1.5
F32 = jnp.float32
BF = jnp.bfloat16
INV_SQRT2 = 1.0 / math.sqrt(2.0)
INV_SQRT2PI = 1.0 / math.sqrt(2.0 * math.pi)


def dot(a, b, da, db):
    return lax.dot_general(a, b, (((da,), (db,)), ((), ())), preferred_element_type=F32)


def pick(v, index, axis):
    return lax.dynamic_index_in_dim(v, index, axis, keepdims=False)


class Comm:
    def __init__(self):
        self.n_grp = lax.axis_size("grp")
        self.n_seq = lax.axis_size("seq")
        self.nz = self.n_grp // 2
        self.ny = self.n_seq // 2
        g = lax.axis_index("grp")
        s = lax.axis_index("seq")
        self.g, self.s = g, s
        self.z, self.x = g // 2, g % 2
        self.y, self.c = s // 2, s % 2

    @staticmethod
    def flip(v, axis, size):
        return lax.ppermute(v, axis, [(i, i ^ 1) for i in range(size)])

    @staticmethod
    def turn(v, axis, size, k):
        half = size // 2
        perm = [(2 * i + j, 2 * ((i + k) % half) + j) for i in range(half) for j in range(2)]
        return lax.ppermute(v, axis, perm)

    def _gather(self, v, axis, size, major, minor):
        half = size // 2
        if half > 4:
            return lax.all_gather(v, axis, axis=0, tiled=False)
        parts = [v] + [self.turn(v, axis, size, k) for k in range(1, half)]
        others = [self.flip(p, axis, size) for p in parts]
        if half == 2:
            zero = major == 0
            mine = jnp.stack([jnp.where(zero, parts[0], parts[1]), jnp.where(zero, parts[1], parts[0])])
            them = jnp.stack([jnp.where(zero, others[0], others[1]), jnp.where(zero, others[1], others[0])])
        else:
            order = jnp.mod(major - jnp.arange(half), half)
            mine = jnp.stack([pick(jnp.stack(parts), order[i], 0) for i in range(half)])
            them = jnp.stack([pick(jnp.stack(others), order[i], 0) for i in range(half)])
        first = jnp.where(minor == 0, mine, them)
        second = jnp.where(minor == 0, them, mine)
        return jnp.stack([first, second], axis=1).reshape((size,) + v.shape)

    def gather_seq(self, v):
        return self._gather(v, "seq", self.n_seq, self.y, self.c)

    def gather_grp(self, v):
        half = self.nz
        slab = jnp.zeros((half,) + v.shape, v.dtype)
        zeros = (0,) * v.ndim
        for k in range(half):
            part = v if k == 0 else self.turn(v, "grp", self.n_grp, k)
            slab = lax.dynamic_update_slice(slab, part[None], (jnp.mod(self.z - k, half),) + zeros)
        other = self.flip(slab, "grp", self.n_grp)
        first = jnp.where(self.x == 0, slab, other)
        second = jnp.where(self.x == 0, other, slab)
        return jnp.stack([first, second], axis=1).reshape((self.n_grp,) + v.shape)

    def _scatter(self, v, axis, size, major, minor, kind):
        half = size // 2
        if half > 4:
            return lax.psum_scatter(v.astype(kind), axis, scatter_dimension=0, tiled=False).astype(F32)
        v = v.reshape((half, 2) + v.shape[1:])
        got = self.flip(pick(v, 1 - minor, 1).astype(kind), axis, size)
        mine = pick(v, minor, 1).astype(F32) + got.astype(F32)
        total = pick(mine, major, 0)
        for k in range(1, half):
            sent = pick(mine, jnp.mod(major + k, half), 0).astype(kind)
            total = total + self.turn(sent, axis, size, k).astype(F32)
        return total

    def scatter_seq(self, v, kind=BF):
        return self._scatter(v, "seq", self.n_seq, self.y, self.c, kind)

    def scatter_grp(self, v, kind=BF):
        return self._scatter(v, "grp", self.n_grp, self.z, self.x, kind)

    def sum_all(self, v, axis, size):
        half = size // 2
        if half > 4:
            return lax.psum(v, axis)
        v = v + self.flip(v, axis, size)
        total = v
        for k in range(1, half):
            total = total + self.turn(v, axis, size, k)
        return total


def norm_stats(value):
    center = value - jnp.mean(value, axis=-1, keepdims=True)
    scale = lax.rsqrt(jnp.mean(center * center, axis=-1, keepdims=True) + EPS)
    return center * scale, scale


def norm_back(grad, hat, scale, gain):
    inner = grad * gain
    mean_one = jnp.mean(inner, axis=-1, keepdims=True)
    mean_two = jnp.mean(inner * hat, axis=-1, keepdims=True)
    return scale * (inner - mean_one - hat * mean_two), jnp.sum(grad * hat, axis=0), jnp.sum(grad, axis=0)


def positions(length):
    index = jnp.arange(length, dtype=jnp.int32).astype(F32)
    tpos = index / (length - 1)
    bands = 0.0001 + (15.0 - 0.0001) * jnp.arange(16, dtype=jnp.int32).astype(F32) / 15.0
    angle = 2.0 * math.pi / length * index[:, None] * bands[None, :]
    return (jnp.concatenate([tpos[:, None], jnp.cos(angle), -jnp.sin(angle)], axis=1), tpos)


def odd_table(size, place):
    freq = 2 * jnp.arange(size // 2, dtype=jnp.int32) + 1
    turn = jnp.bitwise_and(freq[:, None] * place[None, :], 2 * size - 1)
    angle = turn.astype(F32) * (math.pi / size)
    return jnp.stack([jnp.cos(angle), -jnp.sin(angle)])


def filter_of(fin, fmid, fbias, freq, fout, feats, decay):
    inner = jnp.sin(freq[0] * (jnp.dot(feats, fin, precision=HIGH) + fbias[0]))
    inner = jnp.sin(freq[1] * (jnp.dot(inner, fmid, precision=HIGH) + fbias[1]))
    return jnp.dot(inner, fout, precision=HIGH) * decay


def lagged(v, lag, mask):
    return jnp.where(mask[None, :, None], jnp.pad(v, ((0, 0), (lag, 0), (0, 0)))[:, : v.shape[1]], 0.0)


def ahead(v, lag):
    return jnp.pad(v, ((0, 0), (0, lag), (0, 0)))[:, lag:]


def times(ar, ai, br, bi):
    return ar * br - ai * bi, ar * bi + ai * br


def times_conj(ar, ai, br, bi):
    return ar * br + ai * bi, ai * br - ar * bi


class Mixer:
    def __init__(self, lens, total, most):
        half = total // 2
        self.half, self.most, self.total, self.count = half, most, total, lens.shape[0]
        starts = half + jnp.cumsum(lens) - lens
        place = jnp.arange(total, dtype=jnp.int32)
        begin = jnp.zeros((total,), jnp.int32)
        for k in range(lens.shape[0]):
            begin = jnp.where(starts[k] <= place, starts[k], begin)
        self.masks = [None] + [place - lag >= begin for lag in (1, 2)]
        self.long = odd_table(2 * half, place[:half]).reshape(2 * half, half).astype(BF)
        self.short0 = odd_table(2 * most, place[:most]).reshape(2 * most, most).astype(BF)
        tail = place[half:]
        tables = []
        for k in range(lens.shape[0]):
            rel = tail - starts[k]
            inside = (rel >= 0) & (rel < lens[k])
            table = odd_table(2 * most, jnp.where(inside, rel, 0))
            tables.append(jnp.where(inside[None, None, :], table, 0.0))
        self.short = jnp.stack(tables).reshape(lens.shape[0] * 2 * most, total - half).astype(BF)

    def split(self, long, short):
        chans = long.shape[-1]
        long = long.reshape(2, self.half, chans)
        short = short.reshape(self.count, 2, self.most, chans)
        return long[0], long[1], short[:, 0], short[:, 1]

    def forth(self, v):
        v = v.astype(BF)
        return self.split(dot(self.long, v[: self.half], 1, 0), dot(self.short, v[self.half :], 1, 0))

    def back(self, spec):
        lr, li, sr, si = spec
        long = jnp.stack([lr, li]).reshape(2 * self.half, -1) * (1.0 / self.half)
        short = jnp.stack([sr, si], axis=1).reshape(self.count * 2 * self.most, -1) * (1.0 / self.most)
        return jnp.concatenate([dot(self.long, long.astype(BF), 0, 0), dot(self.short, short.astype(BF), 0, 0)])

    def filt_spec(self, filt):
        filt = filt.astype(BF)
        long = dot(self.long, filt, 1, 0)
        short = dot(self.short0, filt[: self.most], 1, 0)
        return long[: self.half], long[self.half :], short[: self.most], short[self.most :]

    def filt_back(self, grads):
        lr, li, sr, si = grads
        long = jnp.concatenate([lr, li]) * (1.0 / self.half)
        short = jnp.concatenate([sr, si]) * (1.0 / self.most)
        head = dot(self.short0, short.astype(BF), 0, 0)
        return dot(self.long, long.astype(BF), 0, 0) + jnp.pad(head, ((0, self.half - self.most), (0, 0)))


def body_any(
    tokens,
    lengths,
    cotangent,
    norm_gain,
    norm_bias,
    in_weight,
    in_bias,
    conv_weight,
    conv_bias,
    skip_bias,
    filt_out,
    out_weight,
    up_weight,
    up_bias,
    down_weight,
    branch_bias,
    filt_in,
    filt_mid,
    filt_bias,
    sine_freq,
):
    comm = Comm()
    n_grp, n_seq, s = comm.n_grp, comm.n_seq, comm.s
    depth = norm_gain.shape[0]
    tok_rows, width = tokens.shape
    total = tok_rows * n_seq
    cols = width // n_grp
    q = cols // n_seq
    ff_shard = up_weight.shape[2]
    f = ff_shard // n_seq
    hid = filt_out.shape[1]
    chans = n_grp * q

    def unit_in(l):
        return pick(in_weight[l].T.reshape(3, n_seq, q, width), s, 1).reshape(3 * q, width)

    def unit_out(l):
        return pick(out_weight[l].reshape(n_grp, n_seq, q, cols), s, 1).reshape(chans, cols).T

    def unit_up(l):
        return lax.dynamic_slice_in_dim(up_weight[l], s * f, f, 1).T

    def unit_down(l):
        return pick(down_weight[l].reshape(n_grp, n_seq, f, cols), s, 1).reshape(n_grp * f, cols).T

    tok_small = [norm_gain, norm_bias, branch_bias]
    seq_small = [
        pick(in_bias.reshape(depth, 3, n_seq, q), s, 2),
        pick(conv_weight.reshape(depth, 3, 3, n_seq, q), s, 3),
        pick(conv_bias.reshape(depth, 3, n_seq, q), s, 2),
        pick(skip_bias.reshape(depth, n_seq, q), s, 1),
        pick(filt_out.reshape(depth, hid, n_seq, q), s, 2),
        pick(up_bias.reshape(depth, n_seq, f), s, 1),
    ]
    shapes = [v.shape for v in tok_small + seq_small]
    sizes = [math.prod(shape) for shape in shapes]
    packed = jnp.concatenate([v.reshape(-1) for v in tok_small + seq_small])
    fill = -packed.shape[0] % 2048
    packed = comm.gather_grp(jnp.pad(packed, (0, fill)).reshape(-1, 128)).reshape(n_grp, -1).astype(F32)
    spread, at = [], 0
    for shape, size in zip(shapes, sizes):
        spread.append(packed[:, at : at + size].reshape((n_grp,) + shape))
        at += size

    def last(v):
        return jnp.moveaxis(v, 0, -2).reshape(v.shape[1:-1] + (n_grp * v.shape[-1],))

    def streams(v):
        v = jnp.moveaxis(v, 0, -3)
        return v.reshape(v.shape[:-3] + (3, n_grp * q))

    gains, shifts, b_branch = (last(v) for v in spread[:3])
    b_in, taps, tap_bias = (streams(v) for v in spread[3:6])
    skip, fout, b_up = (last(v) for v in spread[6:9])

    weights = []
    for l in range(depth):
        w_in = comm.gather_grp(unit_in(l)).reshape(3 * chans, width)
        w_out = comm.gather_grp(unit_out(l)).reshape(width, chans)
        w_up = comm.gather_grp(unit_up(l)).reshape(n_grp * f, width)
        w_down = comm.gather_grp(unit_down(l)).reshape(width, n_grp * f)
        weights.append((w_in, w_out, w_up, w_down))

    lens = lengths[0]
    mixer = Mixer(lens, total, total // 4)
    feats, tpos = positions(total // 2)
    channel = (
        jnp.arange(n_grp, dtype=jnp.int32)[:, None] * cols + s * q + jnp.arange(q, dtype=jnp.int32)[None, :]
    ).reshape(-1).astype(F32)
    rate = jnp.abs(FAST + (SLOW - FAST) * channel / (width - 1))
    decay = jnp.exp(-tpos[:, None] * rate[None, :])

    state = tokens.astype(F32)
    saved = []
    for l in range(depth):
        w_in, w_out, w_up, w_down = weights[l]
        filt, filt_pull = jax.vjp(
            lambda *a: filter_of(*a, feats, decay),
            filt_in[l], filt_mid[l], filt_bias[l], sine_freq[l], fout[l],
        )
        hat1, scale1 = norm_stats(state)
        normed = (hat1 * gains[l, 0] + shifts[l, 0]).astype(BF)
        normed = comm.gather_seq(normed).reshape(total, width)
        proj = dot(normed, w_in, 1, 1) + b_in[l].reshape(-1)
        proj = jnp.transpose(proj.astype(BF).reshape(total, 3, chans), (1, 0, 2))
        chan = proj.astype(F32)
        z = tap_bias[l][:, None, :] + taps[l, 0][:, None, :] * chan
        for lag in (1, 2):
            z = z + taps[l, lag][:, None, :] * lagged(chan, lag, mixer.masks[lag])
        prod = z[1] * z[2]
        h_lr, h_li, h_sr, h_si = mixer.filt_spec(filt)
        x_lr, x_li, x_sr, x_si = mixer.forth(prod)
        conv = mixer.back(times(x_lr, x_li, h_lr, h_li) + times(x_sr, x_si, h_sr, h_si))
        inner = conv + skip[l] * prod
        mixed = (z[0] * inner).astype(BF)
        part = dot(mixed, w_out, 1, 1)
        mid = state + comm.scatter_seq(part.reshape(n_seq, tok_rows, width)) + b_branch[l, 0]
        hat2, scale2 = norm_stats(mid)
        normed2 = (hat2 * gains[l, 1] + shifts[l, 1]).astype(BF)
        normed2 = comm.gather_seq(normed2).reshape(total, width)
        pre = dot(normed2, w_up, 1, 1) + b_up[l]
        cdf = 0.5 * (1.0 + lax.erf(pre * INV_SQRT2))
        hidden = (pre * cdf).astype(BF)
        slope = cdf + pre * (jnp.exp(-0.5 * pre * pre) * INV_SQRT2PI)
        part = dot(hidden, w_down, 1, 1)
        state = mid + comm.scatter_seq(part.reshape(n_seq, tok_rows, width)) + b_branch[l, 1]
        saved.append((filt_pull, hat1, scale1, normed, chan, z, prod, inner, (h_lr, h_li, h_sr, h_si),
                      (x_lr, x_li, x_sr, x_si), mixed, hat2, scale2, normed2, slope, hidden))

    grad = cotangent
    units = [None] * depth
    tok_grads, seq_grads, net_grads = [None] * depth, [None] * depth, [None] * depth

    def chunk(v):
        return comm.scatter_grp(v.astype(BF).reshape((n_grp, v.shape[0] // n_grp) + v.shape[1:])).astype(BF)

    for l in reversed(range(depth)):
        w_in, w_out, w_up, w_down = weights[l]
        (filt_pull, hat1, scale1, normed, chan, z, prod, inner, (h_lr, h_li, h_sr, h_si),
         (x_lr, x_li, x_sr, x_si), mixed, hat2, scale2, normed2, slope, hidden) = saved[l]
        low = grad.astype(BF)
        g_two = jnp.sum(low.astype(F32), axis=0)
        low = comm.gather_seq(low).reshape(total, width)
        u_down = chunk(dot(low, hidden, 0, 0))
        g_pre = (dot(low, w_down, 1, 0) * slope).astype(BF)
        g_up_bias = jnp.sum(g_pre.astype(F32), axis=0)
        part = dot(g_pre, w_up, 1, 0)
        u_up = chunk(dot(g_pre, normed2, 0, 0))
        g_normed2 = comm.scatter_seq(part.reshape(n_seq, tok_rows, width))
        g_mid, gain2, shift2 = norm_back(g_normed2, hat2, scale2, gains[l, 1])
        g_mid = g_mid + grad
        low = g_mid.astype(BF)
        g_one = jnp.sum(low.astype(F32), axis=0)
        low = comm.gather_seq(low).reshape(total, width)
        u_out = chunk(dot(low, mixed, 0, 0))
        g_y = dot(low, w_out, 1, 0).astype(BF).astype(F32)
        g_conv = g_y * z[0]
        g_skip = jnp.sum(g_conv * prod, axis=0)
        y_lr, y_li, y_sr, y_si = mixer.forth(g_conv)
        corr = mixer.back(times_conj(y_lr, y_li, h_lr, h_li) + times_conj(y_sr, y_si, h_sr, h_si))
        f_lr, f_li = times_conj(y_lr, y_li, x_lr, x_li)
        f_sr, f_si = times_conj(y_sr, y_si, x_sr, x_si)
        g_filt = mixer.filt_back((f_lr, f_li, jnp.sum(f_sr, axis=0), jnp.sum(f_si, axis=0)))
        g_prod = corr + skip[l] * g_conv
        g_z = jnp.stack([g_y * inner, g_prod * z[2], g_prod * z[1]])
        g_taps = [jnp.sum(g_z * chan, axis=1)]
        g_proj = taps[l, 0][:, None, :] * g_z
        for lag in (1, 2):
            kept = jnp.where(mixer.masks[lag][None, :, None], g_z, 0.0)
            g_taps.append(jnp.sum(g_z * lagged(chan, lag, mixer.masks[lag]), axis=1))
            g_proj = g_proj + taps[l, lag][:, None, :] * ahead(kept, lag)
        g_proj = jnp.transpose(g_proj.astype(BF), (1, 0, 2)).reshape(total, 3 * chans)
        g_in_bias = jnp.sum(g_proj.astype(F32), axis=0).reshape(3, chans)
        part = dot(g_proj, w_in, 1, 0)
        u_in = chunk(dot(g_proj, normed, 0, 0))
        g_normed = comm.scatter_seq(part.reshape(n_seq, tok_rows, width))
        g_state, gain1, shift1 = norm_back(g_normed, hat1, scale1, gains[l, 0])
        grad = g_mid + g_state
        units[l] = (u_in, u_out, u_up, u_down)
        pulled = filt_pull(g_filt)
        net_grads[l] = pulled[:4]
        tok_grads[l] = (jnp.stack([gain1, gain2]), jnp.stack([shift1, shift2]), jnp.stack([g_one, g_two]))
        seq_grads[l] = (g_in_bias, jnp.stack(g_taps), jnp.sum(g_z, axis=1), g_skip, pulled[4], g_up_bias)

    def whole(place):
        return [comm.gather_seq(units[l][place]).astype(F32) for l in range(depth)]

    in_grad = jnp.stack([
        jnp.transpose(v.reshape(n_seq, 3, q, width), (3, 1, 0, 2)).reshape(width, 3 * cols) for v in whole(0)])
    out_grad = jnp.stack([
        jnp.transpose(v.reshape(n_seq, cols, n_grp, q), (2, 0, 3, 1)).reshape(width, cols) for v in whole(1)])
    up_grad = jnp.stack([jnp.transpose(v, (2, 0, 1)).reshape(width, ff_shard) for v in whole(2)])
    down_grad = jnp.stack([
        jnp.transpose(v.reshape(n_seq, cols, n_grp, f), (2, 0, 3, 1)).reshape(n_grp * ff_shard, cols)
        for v in whole(3)])

    def by_owner(v):
        v = v.reshape(v.shape[:-1] + (n_grp, v.shape[-1] // n_grp))
        return jnp.moveaxis(v, -2, 0).reshape(n_grp, -1)

    def by_owner3(v):
        v = v.reshape(v.shape[:-2] + (n_grp, 3, q))
        return jnp.moveaxis(v, -3, 0).reshape(n_grp, -1)

    tok_all = [jnp.stack(v) for v in zip(*tok_grads)]
    seq_all = [jnp.stack(v) for v in zip(*seq_grads)]
    tok_flat = jnp.concatenate([by_owner(v) for v in tok_all], axis=1)
    seq_flat = jnp.concatenate(
        [by_owner3(v) for v in seq_all[:3]] + [by_owner(v) for v in seq_all[3:]], axis=1)
    tok_len, seq_len = tok_flat.shape[1], seq_flat.shape[1]
    flat = jnp.concatenate([tok_flat, seq_flat], axis=1)
    flat = jnp.pad(flat, ((0, 0), (0, -flat.shape[1] % 1024)))
    small = comm.scatter_grp(flat.reshape(n_grp, -1, 128), F32).reshape(-1)
    tok_sum = comm.sum_all(small[:tok_len].reshape(-1, 128), "seq", n_seq).reshape(-1)
    seq_part = jnp.pad(small[tok_len : tok_len + seq_len], (0, -seq_len % 1024)).reshape(-1, 128)
    seq_sum = comm.gather_seq(seq_part).reshape(n_seq, -1)[:, :seq_len]
    norm_gain_grad, norm_bias_grad, branch_grad = tok_sum.reshape(3, depth, 2, cols)
    pieces, at = [], 0
    for shape in shapes[3:]:
        size = math.prod(shape)
        part = seq_sum[:, at : at + size].reshape((n_seq,) + shape)
        at += size
        part = jnp.moveaxis(part, 0, -2)
        pieces.append(part)
    in_bias_grad = pieces[0].reshape(depth, 3 * cols)
    taps_grad = pieces[1].reshape(depth, 3, 3 * cols)
    tap_bias_grad = pieces[2].reshape(depth, 3 * cols)
    skip_grad = pieces[3].reshape(depth, cols)
    fout_grad = pieces[4].reshape(depth, hid, cols)
    up_bias_grad = pieces[5].reshape(depth, ff_shard)

    nets = [jnp.stack(v) for v in zip(*net_grads)]
    flat = jnp.concatenate([v.reshape(-1) for v in nets])
    flat = jnp.pad(flat, (0, -flat.shape[0] % 1024)).reshape(-1, 128)
    flat = comm.sum_all(comm.sum_all(flat, "seq", n_seq), "grp", n_grp).reshape(-1)
    shared, at = [], 0
    for v in nets:
        shared.append(flat[at : at + v.size].reshape(v.shape))
        at += v.size
    return (
        state, grad, norm_gain_grad, norm_bias_grad, in_grad, in_bias_grad, taps_grad, tap_bias_grad,
        skip_grad, fout_grad, out_grad, up_grad, up_bias_grad, down_grad, branch_grad,
        shared[0], shared[1], shared[2], shared[3],
    )


ORDER = (0, 2, 1, 3)
VMEM_BYTES = 56 * 2**20
SMALL = 64
SLOT = 24
COST = 1000
UP_AT = 48
TOK = 52


def run(kernel, outs, meta, args, scratch=(), flops=0, alias=None):
    specs, arrays = [], []
    for a in args:
        if isinstance(a, tuple):
            array, block, place = a
            if block is None:
                specs.append(pl.BlockSpec(memory_space=pl.ANY))
            else:
                specs.append(pl.BlockSpec(block, place, pipeline_mode=pl.Buffered(1)))
            arrays.append(array)
        else:
            specs.append(pl.BlockSpec(memory_space=pltpu.VMEM))
            arrays.append(a)
    out_specs, shapes = [], []
    for o in outs:
        shapes.append(jax.ShapeDtypeStruct(o[0], o[1]))
        if len(o) > 2:
            out_specs.append(pl.BlockSpec(o[2], o[3], pipeline_mode=pl.Buffered(1)))
        else:
            out_specs.append(pl.BlockSpec(memory_space=pltpu.VMEM))
    moved = sum(o.size * o.dtype.itemsize for o in shapes) + sum(a.size * a.dtype.itemsize for a in arrays)
    return pl.pallas_call(
        kernel,
        out_shape=shapes,
        grid_spec=pltpu.PrefetchScalarGridSpec(
            num_scalar_prefetch=1,
            grid=(1,),
            in_specs=specs,
            out_specs=out_specs,
            scratch_shapes=[pltpu.VMEM(shape, kind) for shape, kind in scratch],
        ),
        input_output_aliases=alias or {},
        compiler_params=pltpu.CompilerParams(vmem_limit_bytes=VMEM_BYTES),
        cost_estimate=pl.CostEstimate(flops=flops // COST, bytes_accessed=moved // COST, transcendentals=0),
    )(meta, *arrays)


def join(meta, parts, all_ref):
    rows = parts[0].shape[0]
    for k, part in enumerate(parts):
        at = pl.multiple_of((meta[0] ^ ORDER[k]) * rows, rows)
        all_ref[pl.ds(at, rows), :] = part[...]


def owners(meta, refs):
    if len(refs) == 1:
        return [(g, refs[0].at[g]) for g in range(refs[0].shape[0])]
    half = refs[0].shape[0]
    found = []
    for k in range(half):
        at = 2 * lax.rem(meta[1] - k + half, half)
        found.append((at + meta[2], refs[0].at[k]))
        found.append((at + 1 - meta[2], refs[1].at[k]))
    return found


def span(g, size):
    if isinstance(g, int):
        return pl.ds(g * size, size)
    return pl.ds(pl.multiple_of(g * size, size), size)


def place_wide(meta, refs, wide):
    rows = wide.shape[0]
    for g, block in owners(meta, refs):
        wide[:, span(g, block.shape[-1])] = block[:rows, :]


def place_io(meta, refs, wi, wo):
    n_grp = wi.shape[1] // 128
    part = wi.shape[0] // n_grp
    q = part // 3
    for g, block in owners(meta, refs):
        for lb in range(n_grp):
            at = lb * 4 * q
            wi[span(g, part), lb * 128 : (lb + 1) * 128] = block[at : at + part, :]
            wo[lb * q : (lb + 1) * q, span(g, 128)] = block[at + part : at + part + q, :]


def part_out(meta, value, at, send, keep):
    rows = value.shape[0] // 4
    w = value.shape[1]
    even = jnp.stack([value[:rows], value[2 * rows : 3 * rows]])
    odd = jnp.stack([value[rows : 2 * rows], value[3 * rows :]])
    low = meta[4] == 0
    keep[:, :, at : at + w] = jnp.where(low, even, odd)
    send[:, :, at : at + w] = jnp.where(low, odd, even).astype(BF)


def masks_of(meta, total, wide, count):
    place = lax.broadcasted_iota(jnp.int32, (total, wide), 0)
    begin = jnp.zeros((total, wide), jnp.int32)
    for k in range(count):
        begin = jnp.where(place >= meta[5 + k], meta[5 + k], begin)
    return place, [None] + [place - lag >= begin for lag in (1, 2)]


def roll_down(v, lag):
    return pltpu.roll(v, lag, 0)


def stream_z(chan, j, wide, rows5, masks):
    at = j * wide
    v = chan[:, at : at + wide].astype(F32)
    z = rows5[4:5, at : at + wide] + rows5[1:2, at : at + wide] * v
    for lag in (1, 2):
        z = z + rows5[1 + lag : 2 + lag, at : at + wide] * jnp.where(masks[lag], roll_down(v, lag), 0.0)
    return z


def spectra(v, long, short):
    half = v.shape[0] // 2
    low = v.astype(BF)
    return dot(long[...], low[:half], 1, 0), dot(short[...], low[half:], 1, 0)


def filt_spectra(filt, long, short0):
    low = filt.astype(BF)
    return dot(long[...], low, 1, 0), dot(short0[...], low[: short0.shape[1]], 1, 0)


def each(long, short, count):
    half = long.shape[0] // 2
    most = short.shape[0] // count // 2
    pairs = [(long[:half], long[half:])]
    for k in range(count):
        pairs.append((short[2 * k * most : (2 * k + 1) * most], short[(2 * k + 1) * most : (2 * k + 2) * most]))
    return pairs


def unspectra(pairs, long_t, short_t):
    half, most = pairs[0][0].shape[0], pairs[1][0].shape[0]
    long = (jnp.concatenate(pairs[0]) * (1.0 / half)).astype(BF)
    short = (jnp.concatenate([v for pair in pairs[1:] for v in pair]) * (1.0 / most)).astype(BF)
    return jnp.concatenate([dot(long_t[...], long, 1, 0), dot(short_t[...], short, 1, 0)])


def exact(a, b, da, db):
    return lax.dot_general(a, b, (((da,), (db,)), ((), ())), precision=HIGH, preferred_element_type=F32)


def mix_forth_kernel(count, nio, raw, meta, *refs):
    parts, refs = refs[:4], refs[4:]
    io, refs = refs[:nio], refs[nio:]
    (long, long_t, short, short_t, short0, second, decay, fout, rows5, skip, gain, shift,
     every, chan, inner_ref, mixed_ref, send, keep, wi, wo) = refs
    join(meta, parts, every)
    if raw:
        every[...] = (every[...].astype(F32) * gain[...] + shift[...]).astype(BF)
    place_io(meta, io, wi, wo)
    total, wide = mixed_ref.shape
    _, masks = masks_of(meta, total, wide, count)
    z = []
    for j in range(3):
        at = j * wide
        proj = dot(every[...], wi[at : at + wide, :], 1, 1) + rows5[0:1, at : at + wide]
        chan[:, at : at + wide] = proj.astype(BF)
        z.append(stream_z(chan, j, wide, rows5, masks))
    prod = z[1] * z[2]
    filt = exact(second[...], fout[...], 1, 0) * decay[...]
    hs = each(*filt_spectra(filt, long, short0), 1)
    xs = each(*spectra(prod, long, short), count)
    ys = [times(*x, *hs[min(k, 1)]) for k, x in enumerate(xs)]
    inner = unspectra(ys, long_t, short_t) + skip[...] * prod
    inner_ref[...] = inner
    mixed_ref[...] = (z[0] * inner).astype(BF)
    for n in range(4):
        w = wo.shape[1] // 4
        part_out(meta, dot(mixed_ref[...], wo[:, n * w : (n + 1) * w], 1, 0), n * w, send, keep)


def mix_back_kernel(count, nio, meta, *refs):
    parts, refs = refs[:4], refs[4:]
    io, refs = refs[:nio], refs[nio:]
    (long, long_t, short, short_t, short0, short0_t, second, decay, fout, rows5, skip, chan, inner,
     every, g_proj_ref, g_fout, g_second, small, send, keep, wi, wo) = refs
    join(meta, parts, every)
    place_io(meta, io, wi, wo)
    total, wide = inner.shape
    place, masks = masks_of(meta, total, wide, count)
    z = [stream_z(chan, j, wide, rows5, masks) for j in range(3)]
    prod = z[1] * z[2]
    filt = exact(second[...], fout[...], 1, 0) * decay[...]
    hs = each(*filt_spectra(filt, long, short0), 1)
    xs = each(*spectra(prod, long, short), count)
    g_y = dot(every[...], wo[...], 1, 1).astype(BF).astype(F32)
    g_conv = g_y * z[0]
    ys = each(*spectra(g_conv, long, short), count)
    corr = unspectra([times_conj(*y, *hs[min(k, 1)]) for k, y in enumerate(ys)], long_t, short_t)
    g_prod = corr + skip[...] * g_conv
    small[...] = jnp.zeros_like(small)
    small[5:6, :wide] = jnp.sum(g_conv * prod, axis=0, keepdims=True)
    for j, g_z in enumerate((g_y * inner[...], g_prod * z[2], g_prod * z[1])):
        at = j * wide
        v = chan[:, at : at + wide].astype(F32)
        small[4:5, at : at + wide] = jnp.sum(g_z, axis=0, keepdims=True)
        small[1:2, at : at + wide] = jnp.sum(g_z * v, axis=0, keepdims=True)
        g_proj = rows5[1:2, at : at + wide] * g_z
        for lag in (1, 2):
            kept = jnp.where(masks[lag], g_z, 0.0)
            small[1 + lag : 2 + lag, at : at + wide] = jnp.sum(kept * roll_down(v, lag), axis=0, keepdims=True)
            moved = jnp.where(place < total - lag, roll_down(kept, total - lag), 0.0)
            g_proj = g_proj + rows5[1 + lag : 2 + lag, at : at + wide] * moved
        low = g_proj.astype(BF)
        g_proj_ref[:, at : at + wide] = low
        small[0:1, at : at + wide] = jnp.sum(low.astype(F32), axis=0, keepdims=True)
    for n in range(4):
        w = wi.shape[1] // 4
        part_out(meta, dot(g_proj_ref[...], wi[:, n * w : (n + 1) * w], 1, 0), n * w, send, keep)
    fs = [times_conj(*y, *x) for y, x in zip(ys, xs)]
    f_short = fs[1]
    for pair in fs[2:]:
        f_short = (f_short[0] + pair[0], f_short[1] + pair[1])
    half, most = fs[0][0].shape[0], f_short[0].shape[0]
    g_filt = dot(long_t[...], (jnp.concatenate(fs[0]) * (1.0 / half)).astype(BF), 1, 0)
    head = dot(short0_t[...], (jnp.concatenate(f_short) * (1.0 / most)).astype(BF), 1, 0)
    g_filt = jnp.concatenate([g_filt[:most] + head, g_filt[most:]]) * decay[...]
    g_fout[...] = exact(second[...].T, g_filt, 1, 0)
    g_second[...] = exact(g_filt, fout[...], 1, 1)


def mlp_forth_kernel(nup, ndown, meta, *refs):
    parts, refs = refs[:4], refs[4:]
    up, refs = refs[:nup], refs[nup:]
    down, refs = refs[:ndown], refs[ndown:]
    b_up, every, hidden, slope, send, keep, wide_up, wide_down = refs
    join(meta, parts, every)
    place_wide(meta, up, wide_up)
    tile = wide_up.shape[1] // 4
    for n in range(4):
        at = n * tile
        pre = dot(every[...], wide_up[:, at : at + tile], 1, 0) + b_up[:, at : at + tile]
        cdf = 0.5 * (1.0 + lax.erf(pre * INV_SQRT2))
        hidden[:, at : at + tile] = (pre * cdf).astype(BF)
        slope[:, at : at + tile] = (cdf + pre * (jnp.exp(-0.5 * pre * pre) * INV_SQRT2PI)).astype(BF)
    place_wide(meta, down, wide_down)
    tile = wide_down.shape[1] // 4
    for n in range(4):
        part_out(meta, dot(hidden[...], wide_down[:, n * tile : (n + 1) * tile], 1, 0), n * tile, send, keep)


def mlp_back_kernel(nup, ndown, meta, *refs):
    parts, refs = refs[:4], refs[4:]
    up, refs = refs[:nup], refs[nup:]
    down, refs = refs[:ndown], refs[ndown:]
    slope, every, g_pre_ref, g_bias, send, keep, wide_up, wide_down = refs
    join(meta, parts, every)
    place_wide(meta, down, wide_down)
    tile = slope.shape[1] // 4
    for n in range(4):
        at = n * tile
        g_hidden = dot(every[...], wide_down[at : at + tile, :], 1, 1)
        g_pre = (g_hidden * slope[:, at : at + tile].astype(F32)).astype(BF)
        g_pre_ref[:, at : at + tile] = g_pre
        g_bias[:, at : at + tile] = jnp.sum(g_pre.astype(F32), axis=0, keepdims=True)
    place_wide(meta, up, wide_up)
    tile = wide_up.shape[0] // 4
    for n in range(4):
        at = n * tile
        part_out(meta, dot(g_pre_ref[...], wide_up[at : at + tile, :], 1, 1), at, send, keep)


def hat_of(value):
    center = value - jnp.mean(value, axis=-1, keepdims=True)
    scale = lax.rsqrt(jnp.mean(center * center, axis=-1, keepdims=True) + EPS)
    return center * scale, scale


def first_norm_kernel(meta, tokens, cotangent, normed, low, sums):
    hat, _ = hat_of(tokens[...].astype(F32))
    normed[...] = hat.astype(BF)
    rounded = cotangent[...].astype(BF)
    low[...] = rounded
    sums[...] = jnp.zeros_like(sums)
    sums[2:3, :] = jnp.sum(rounded.astype(F32), axis=0, keepdims=True)


def add_norm_kernel(meta, state, keep, got, crossed, bias, gain, shift, new, normed):
    value = state[...].astype(F32) + (keep[0] + got[0].astype(F32) + crossed[...].astype(F32)) + bias[...]
    new[...] = value
    hat, _ = hat_of(value)
    normed[...] = (hat * gain[...] + shift[...]).astype(BF)


def add_kernel(meta, state, keep, got, crossed, bias, new):
    new[...] = state[...] + (keep[0] + got[0].astype(F32) + crossed[...].astype(F32)) + bias[...]


def norm_back_kernel(meta, grad, keep, got, crossed, value, gain, new, low, sums):
    g = keep[0] + got[0].astype(F32) + crossed[...].astype(F32)
    hat, scale = hat_of(value[...].astype(F32))
    inner = g * gain[...]
    mean_one = jnp.mean(inner, axis=-1, keepdims=True)
    mean_two = jnp.mean(inner * hat, axis=-1, keepdims=True)
    total = grad[...] + scale * (inner - mean_one - hat * mean_two)
    new[...] = total
    rounded = total.astype(BF)
    low[...] = rounded
    sums[...] = jnp.zeros_like(sums)
    sums[0:1, :] = jnp.sum(g * hat, axis=0, keepdims=True)
    sums[1:2, :] = jnp.sum(g, axis=0, keepdims=True)
    sums[2:3, :] = jnp.sum(rounded.astype(F32), axis=0, keepdims=True)


def split_io_kernel(meta, g_in, g_out, send, mine):
    n_grp = g_in.shape[1] // 128
    part = g_in.shape[0] // n_grp
    q = part // 3
    for k in range(send.shape[0]):
        for x, target in ((meta[2], mine), (1 - meta[2], send)):
            g = 2 * k + x
            for lb in range(n_grp):
                at = lb * 4 * q
                target[k, at : at + part, :] = g_in[span(g, part), lb * 128 : (lb + 1) * 128]
                target[k, at + part : at + part + q, :] = g_out[lb * q : (lb + 1) * q, span(g, 128)]


def mlp_grads_kernel(meta, every, g_pre, hidden, low, out):
    tile = 256
    rows = every.shape[1]
    for n in range(low.shape[1] // tile):
        w = slice(n * tile, (n + 1) * tile)
        for at, left, right in ((0, every, g_pre), (rows, hidden, low)):
            value = dot(left[...], right[:, w], 0, 0).astype(BF)
            out[2 * n, at : at + rows, :] = value[:, :128]
            out[2 * n + 1, at : at + rows, :] = value[:, 128:]


def io_grads_kernel(meta, g_proj, every, mixed, low, send, mine, g_in, g_out):
    wide = mixed.shape[1]
    for j in range(g_proj.shape[1] // wide):
        w = slice(j * wide, (j + 1) * wide)
        g_in[w, :] = dot(g_proj[:, w], every[...], 0, 0).astype(BF)
    g_out[...] = dot(mixed[...], low[...], 0, 0).astype(BF)
    split_io_kernel(meta, g_in, g_out, send, mine)


def owner_sum_kernel(meta, mine, got, own, *sends):
    half = got.shape[0]
    z = meta[1]
    own[...] = mine[z].astype(F32) + got[z].astype(F32)
    for k, send in enumerate(sends, 1):
        to = lax.rem(z + k, half)
        send[...] = (mine[to].astype(F32) + got[to].astype(F32)).astype(BF)


def last_sum_kernel(meta, own, *refs):
    got, out = refs[:-1], refs[-1]
    total = own[...]
    for v in got:
        total = total + v[...].astype(F32)
    out[...] = total.astype(BF)


def prep_kernel(small, meta, up, down, w_in, w_out, *refs):
    if small:
        in_bias, conv_weight, conv_bias, skip, fout, up_bias, gain, shift, branch = refs[:9]
        refs = refs[9:]
    io_out, up_out, down_out, turned = refs[:4]
    s = meta[0]
    up_out[...] = up[0]
    n_grp, f, lanes = down.shape[1], down.shape[3], down.shape[4]
    q = w_out.shape[3]
    for g in range(n_grp):
        down_out[g * f : (g + 1) * f, :] = down[0, g, 0]
        io_out[g * 4 * q + 3 * q : (g + 1) * 4 * q, :] = w_out[0, g, 0]
    for k in range(3):
        turned[...] = w_in[0, :, k * lanes : (k + 1) * lanes].astype(F32).T
        piece = turned[span(s, q), :].astype(BF)
        for lb in range(n_grp):
            io_out[lb * 4 * q + k * q : lb * 4 * q + (k + 1) * q, :] = piece[:, lb * 128 : (lb + 1) * 128]
    if not small:
        return
    (rows,) = refs[4:]
    depth = up_bias.shape[0]
    rows[...] = jnp.zeros_like(rows)
    b_in, w_tap, b_tap = in_bias[...].astype(F32), conv_weight[...].astype(F32), conv_bias[...].astype(F32)
    skips = skip[...].astype(F32)
    for l in range(depth):
        at = l * SLOT
        outs = fout[l].astype(F32)
        for b in range(3):
            w = slice(b * lanes, (b + 1) * lanes)
            rows[b, at : at + 1, :] = b_in[l : l + 1, w]
            rows[b, at + 1 : at + 4, :] = w_tap[l][:, w]
            rows[b, at + 4 : at + 5, :] = b_tap[l : l + 1, w]
        rows[3, at : at + 4, :] = outs[60:64]
        rows[3, at + 4 : at + 5, :] = skips[l : l + 1]
        for b in range(4):
            rows[b, at + 5 : at + 20, :] = outs[15 * b : 15 * b + 15]
    lane = lax.broadcasted_iota(jnp.int32, (lanes, lanes), 0)
    to = lax.broadcasted_iota(jnp.int32, (lanes, lanes), 1)
    packed = jnp.zeros((2 * SLOT, lanes), F32)
    for b in range(4):
        hit = (lane == s * q + to - b * q) & (to >= b * q) & (to < (b + 1) * q)
        packed = packed + dot(rows[b].astype(BF), jnp.where(hit, 1.0, 0.0).astype(BF), 1, 0)
    ups = up_bias[:, span(s, lanes)].astype(F32)
    tail = [ups, jnp.zeros((TOK - UP_AT - depth, lanes), F32)]
    for v in (gain, shift, branch):
        v = v[...].astype(F32)
        tail += [v[l] for l in range(depth)]
    base = n_grp * 4 * q
    io_out[base : base + SMALL, :] = jnp.concatenate([packed] + tail).astype(BF)


def unpack_kernel(meta, slab, other, e_wide, e_all, tok, rows5, skip, fout, b_up, wide):
    place_wide(meta, (slab, other), wide)
    depth = fout.shape[0]
    tok[...] = wide[TOK:SMALL, :].astype(F32)
    low = wide[: 2 * SLOT, :]
    five = dot(low, e_wide[...], 1, 0)
    for l in range(depth):
        rows5[l] = five[l * SLOT : l * SLOT + 5]
        b_up[l] = wide[UP_AT + l : UP_AT + l + 1, :].astype(F32)
    for b in range(4):
        found = dot(low, e_all[b], 1, 0)
        for l in range(depth):
            at = l * SLOT
            fout[l, 15 * b : 15 * b + 15, :] = found[at + 5 : at + 20]
            if b == 3:
                fout[l, 60:64, :] = found[at : at + 4]
                skip[l] = found[at + 4 : at + 5]


def pack_kernel(depth, meta, *refs):
    ups, refs = refs[:depth], refs[depth:]
    smalls, refs = refs[:depth], refs[depth:]
    fouts, refs = refs[:depth], refs[depth:]
    toks, refs = refs[: 2 * depth + 1], refs[2 * depth + 1 :]
    e_wide, e_all, send, mine, rows, wide = refs
    chans = fouts[0].shape[1]
    rows[...] = jnp.zeros_like(rows)
    for l in range(depth):
        at = l * SLOT
        rows[4, at : at + 5, :] = smalls[l][:5, :]
        for b in range(4):
            rows[b, at + 5 : at + 20, :chans] = fouts[l][15 * b : 15 * b + 15, :]
        rows[3, at : at + 4, :chans] = fouts[l][60:64, :]
        rows[3, at + 4 : at + 5, :chans] = smalls[l][5:6, :chans]
    packed = dot(rows[4].astype(BF), e_wide[...], 1, 1)
    for b in range(4):
        packed = packed + dot(rows[b, :, :chans].astype(BF), e_all[b], 1, 1)
    wide[: 2 * SLOT, :] = packed
    wide[2 * SLOT :, :] = jnp.zeros((SMALL - 2 * SLOT, wide.shape[1]), F32)
    for l in range(depth):
        wide[UP_AT + l : UP_AT + l + 1, :] = ups[l][...]
        for i in range(2):
            v = toks[2 * l + i]
            at = TOK + 2 * l + i
            wide[at : at + 1, :] = v[0:1, :]
            wide[at + 2 * depth : at + 2 * depth + 1, :] = v[1:2, :]
            wide[at + 4 * depth : at + 4 * depth + 1, :] = toks[2 * l + i + 1][2:3, :]
    for k in range(send.shape[0]):
        mine[k] = wide[:, span(2 * k + meta[2], 128)].astype(BF)
        send[k] = wide[:, span(2 * k + 1 - meta[2], 128)].astype(BF)


def finish_small_kernel(q, meta, *refs):
    parts, refs = refs[:4], refs[4:]
    gain, shift, branch, in_bias, conv_weight, conv_bias, skip, fout, up_bias = refs
    depth = fout.shape[0]
    lanes = parts[0].shape[1]
    lane = lax.broadcasted_iota(jnp.int32, (lanes, lanes), 0)
    to = lax.broadcasted_iota(jnp.int32, (lanes, lanes), 1)
    tok = parts[0][...].astype(F32)
    for part in parts[1:]:
        tok = tok + part[...].astype(F32)
    for l in range(depth):
        for t, v in enumerate((gain, shift, branch)):
            at = TOK + 2 * depth * t + 2 * l
            v[l] = tok[at : at + 2]
    for k, part in enumerate(parts):
        up_bias[:, span(meta[0] ^ ORDER[k], lanes)] = part[UP_AT : UP_AT + depth, :].astype(F32)
    for b in range(4):
        found = jnp.zeros((2 * SLOT, lanes), F32)
        for k, part in enumerate(parts):
            s = meta[0] ^ ORDER[k]
            hit = (to - s * q == lane - b * q) & (lane >= b * q) & (lane < (b + 1) * q)
            found = found + dot(part[: 2 * SLOT, :], jnp.where(hit, 1.0, 0.0).astype(BF), 1, 0)
        for l in range(depth):
            at = l * SLOT
            fout[l, 15 * b : 15 * b + 15, :] = found[at + 5 : at + 20]
            if b == 3:
                fout[l, 60:64, :] = found[at : at + 4]
                skip[l : l + 1, :] = found[at + 4 : at + 5]
            else:
                w = slice(b * lanes, (b + 1) * lanes)
                in_bias[l : l + 1, w] = found[at : at + 1]
                conv_weight[l, :, w] = found[at + 1 : at + 4]
                conv_bias[l : l + 1, w] = found[at + 4 : at + 5]


def finish_mlp_kernel(extra, meta, *refs):
    parts, refs = refs[:4], refs[4:]
    up, down = refs[extra:]
    rows = up.shape[1]
    n_grp, f = down.shape[1], down.shape[3]
    for k, part in enumerate(parts):
        s = meta[0] ^ ORDER[k]
        up[0, :, span(s, part.shape[1])] = part[:rows, :].astype(F32)
        for g in range(n_grp):
            down[0, g, s] = part[rows + g * f : rows + (g + 1) * f, :].astype(F32)


def finish_io_kernel(extra, meta, *refs):
    parts, refs = refs[:4], refs[4:]
    g_in, g_out, turned = refs[extra:]
    n_grp, q = g_out.shape[1], g_out.shape[3]
    for k, part in enumerate(parts):
        s = meta[0] ^ ORDER[k]
        for lb in range(n_grp):
            at = lb * 4 * q
            for j in range(3):
                row = pl.ds(pl.multiple_of(j * 4 * q + s * q, q), q)
                turned[row, lb * 128 : (lb + 1) * 128] = part[at + j * q : at + (j + 1) * q, :].astype(F32)
            g_out[0, lb, s] = part[at + 3 * q : at + 4 * q, :].astype(F32)
    for j in range(3):
        g_in[0, :, j * 4 * q : (j + 1) * 4 * q] = turned[j * 4 * q : (j + 1) * 4 * q, :].T


def second_layer(fin, fmid, fbias, freq, feats):
    inner = jnp.sin(freq[0] * (jnp.dot(feats, fin, precision=HIGH) + fbias[0]))
    return jnp.sin(freq[1] * (jnp.dot(inner, fmid, precision=HIGH) + fbias[1]))


def after(value, *others):
    return lax.optimization_barrier((value,) + others)[0]


def body(
    tokens,
    lengths,
    cotangent,
    norm_gain,
    norm_bias,
    in_weight,
    in_bias,
    conv_weight,
    conv_bias,
    skip_bias,
    filt_out,
    out_weight,
    up_weight,
    up_bias,
    down_weight,
    branch_bias,
    filt_in,
    filt_mid,
    filt_bias,
    sine_freq,
):
    comm = Comm()
    n_grp, n_seq, s, nz = comm.n_grp, comm.n_seq, comm.s, comm.nz
    depth = norm_gain.shape[0]
    tok_rows, width = tokens.shape
    total = tok_rows * n_seq
    half, most = total // 2, total // 4
    cols = width // n_grp
    q = cols // n_seq
    ff_shard = up_weight.shape[2]
    f = ff_shard // n_seq
    hid = filt_out.shape[1]
    chans = n_grp * q
    count = lengths.shape[1]
    lens = lengths[0]
    starts = half + jnp.cumsum(lens) - lens
    meta = jnp.concatenate([jnp.stack([s, comm.z, comm.x, comm.y, comm.c]), starts, lens]).astype(jnp.int32)

    down_view = down_weight.reshape(depth, n_grp, n_seq, f, cols)
    out_view = out_weight.reshape(depth, n_grp, n_seq, q, cols)

    def prepare(l, small):
        args = [
            (up_weight, (1, width, f), lambda i, m: (l, 0, m[0])),
            (down_view, (1, n_grp, 1, f, cols), lambda i, m: (l, 0, m[0], 0, 0)),
            (in_weight, (1, width, 3 * cols), lambda i, m: (l, 0, 0)),
            (out_view, (1, n_grp, 1, q, cols), lambda i, m: (l, 0, m[0], 0, 0)),
        ]
        scratch = [((cols, width), F32)]
        rows = width
        if small:
            args += [in_bias, conv_weight, conv_bias, skip_bias, filt_out, up_bias, norm_gain, norm_bias, branch_bias]
            scratch.append(((4, 2 * SLOT, cols), F32))
            rows += SMALL
        outs = [((rows, cols), BF), ((width, f), BF), ((n_grp * f, cols), BF)]
        return run(lambda *r: prep_kernel(small, *r), outs, meta, args, scratch)

    def by_permutes(unit):
        slab = jnp.stack([unit] + [comm.turn(unit, "grp", n_grp, k) for k in range(1, nz)])
        return [slab, comm.flip(slab, "grp", n_grp)]

    first_units = prepare(0, True)
    hat0, low_first, sums_first = run(
        first_norm_kernel,
        [((tok_rows, width), BF), ((tok_rows, width), BF), ((8, width), F32)], meta, [tokens, cotangent])
    ready = list(first_units)
    for l in range(1, depth):
        ready += prepare(l, False)
    chunks, slab = [], None
    for unit in ready:
        if slab is not None:
            unit = after(unit, slab)
        slab = jnp.stack([unit] + [comm.turn(unit, "grp", n_grp, k) for k in range(1, nz)])
        chunks.append([slab, comm.flip(slab, "grp", n_grp)])
    weights = [tuple(chunks[3 * l : 3 * l + 3]) for l in range(depth)]

    lane_from = jnp.arange(n_grp * cols, dtype=jnp.int32)[:, None]
    lane_wide = jnp.arange(3 * chans, dtype=jnp.int32)[None, :]
    lane_chan = jnp.arange(chans, dtype=jnp.int32)[None, :]
    e_wide = ((lane_from // cols == lane_wide // (3 * q)) & (lane_from % cols == lane_wide % (3 * q))).astype(BF)
    e_all = jnp.stack([
        ((lane_from // cols == lane_chan // q) & (lane_from % cols == b * q + lane_chan % q)) for b in range(4)
    ]).astype(BF)
    slab, other = weights[0][0]
    small_block = ((nz, SMALL, cols), lambda i, m: (0, width // SMALL, 0))
    tok_all, rows5, skip, fout, b_up = run(
        unpack_kernel,
        [((6 * depth, width), F32), ((depth, 5, 3 * chans), F32), ((depth, 1, chans), F32),
         ((depth, hid, chans), F32), ((depth, 1, n_grp * f), F32)],
        meta, [(slab,) + small_block, (other,) + small_block, e_wide, e_all], [((SMALL, width), BF)])
    tok_all = tok_all.reshape(3, depth, 2, 1, width)
    gains, shifts, b_branch = tok_all[0], tok_all[1], tok_all[2]

    mixer = Mixer(lens, total, most)
    long, short, short0 = mixer.long, mixer.short, mixer.short0
    long_t, short_t, short0_t = long.T, short.T, short0.T
    feats, tpos = positions(half)
    channel = (
        jnp.arange(n_grp, dtype=jnp.int32)[:, None] * cols + s * q + jnp.arange(q, dtype=jnp.int32)[None, :]
    ).reshape(-1).astype(F32)
    rate = jnp.abs(FAST + (SLOW - FAST) * channel / (width - 1))
    decay = jnp.exp(-tpos[:, None] * rate[None, :])
    seconds, second_pull = jax.vjp(
        lambda *a: jax.vmap(lambda *b: second_layer(*b, feats))(*a), filt_in, filt_mid, filt_bias, sine_freq)

    def gather_parts(v):
        across = comm.turn(v, "seq", n_seq, 1)
        return [v, across, comm.flip(v, "seq", n_seq), comm.flip(across, "seq", n_seq)]

    def scatter_parts(send, keep):
        got = comm.flip(send, "seq", n_seq)
        other = 1 - comm.y
        crossed = (pick(keep, other, 0) + pick(got, other, 0).astype(F32)).astype(BF)
        own = ((1, tok_rows, width), lambda i, m: (m[3], 0, 0))
        return (keep,) + own, (got,) + own, comm.turn(crossed, "seq", n_seq, 1)

    parts_out = [((2, tok_rows, width), BF), ((2, tok_rows, width), F32)]
    io_scratch = [((3 * chans, width), BF), ((chans, width), BF)]
    mlp_scratch = [((width, n_grp * f), BF), ((n_grp * f, width), BF)]
    state = tokens
    saved = []
    normed = hat0
    for l in range(depth):
        w_io, w_up, w_down = weights[l]
        parts = gather_parts(normed)
        if l == 0:
            low_parts = gather_parts(low_first)
            parts[0] = after(parts[0], *low_parts, chunks[1][0])
        else:
            parts[0] = after(parts[0], chunks[4][1], chunks[5][0])
        every, chan, inner, mixed, send, keep = run(
            lambda *r, n=len(w_io), raw=l == 0: mix_forth_kernel(count, n, raw, *r),
            [((total, width), BF), ((total, 3 * chans), BF), ((total, chans), F32), ((total, chans), BF)] + parts_out,
            meta,
            parts + w_io + [long, long_t, short, short_t, short0, seconds[l], decay, fout[l], rows5[l], skip[l],
                            gains[l, 0], shifts[l, 0]],
            io_scratch,
            flops=3 * 10**9,
        )
        got = scatter_parts(send, keep)
        if l == 0:
            state = after(state, chunks[1][1], chunks[2][0])
        mid, normed2 = run(
            add_norm_kernel, [((tok_rows, width), F32), ((tok_rows, width), BF)], meta,
            [state, *got, b_branch[l, 0], gains[l, 1], shifts[l, 1]],
        )
        parts = gather_parts(normed2)
        if l == 0:
            parts[0] = after(parts[0], chunks[2][1], chunks[3][0])
        every2, hidden, slope, send, keep = run(
            lambda *r, n=len(w_up), m=len(w_down): mlp_forth_kernel(n, m, *r),
            [((total, width), BF), ((total, n_grp * f), BF), ((total, n_grp * f), BF)] + parts_out,
            meta, parts + w_up + w_down + [b_up[l]], mlp_scratch,
            flops=4 * 10**9,
        )
        saved.append((state, every, chan, inner, mixed, mid, every2, hidden, slope))
        got = scatter_parts(send, keep)
        if l == 0:
            mid = after(mid, chunks[3][1], chunks[4][0])
        if l + 1 < depth:
            state, normed = run(
                add_norm_kernel, [((tok_rows, width), F32), ((tok_rows, width), BF)], meta,
                [mid, *got, b_branch[l, 1], gains[l + 1, 0], shifts[l + 1, 0]],
            )
        else:
            (state,) = run(add_kernel, [((tok_rows, width), F32)], meta, [mid, *got, b_branch[l, 1]])

    grad = cotangent
    toks = [None] * (2 * depth) + [sums_first]
    g_fouts, g_seconds, smalls, up_biases = ([None] * depth for _ in range(4))

    def owner_turn(mine, got):
        rows = mine.shape[1:]
        own, *sends = run(owner_sum_kernel, [(rows, F32)] + [(rows, BF)] * (nz - 1), meta, [mine, got])
        return [own] + [comm.turn(send, "grp", n_grp, k) for k, send in enumerate(sends, 1)]

    def owner_end(pieces):
        return run(last_sum_kernel, [(pieces[0].shape, BF)], meta, pieces)[0]

    norm_outs = [((tok_rows, width), F32), ((tok_rows, width), BF), ((8, width), F32)]
    mlp_units, io_units, sent = [None] * depth, [None] * depth, []
    for l in reversed(range(depth)):
        w_io, w_up, w_down = weights[l]
        first, every, chan, inner, mixed, mid, every2, hidden, slope = saved[l]
        if l == 0:
            low_parts[0] = after(low_parts[0], io_units[1][1])
        low, g_pre, up_biases[l], send, keep = run(
            lambda *r, n=len(w_up), m=len(w_down): mlp_back_kernel(n, m, *r),
            [((total, width), BF), ((total, n_grp * f), BF), ((1, n_grp * f), F32)] + parts_out,
            meta, low_parts + w_up + w_down + [slope], mlp_scratch,
            flops=4 * 10**9,
        )
        sent.append(send)
        (g_mlp,) = run(
            mlp_grads_kernel, [((n_grp, 2 * width, cols), BF)], meta, [every2, g_pre, hidden, low], flops=4 * 10**9)
        mlp_units[l] = lax.psum_scatter(g_mlp, "grp", scatter_dimension=0, tiled=False)
        grad, low_own, toks[2 * l + 1] = run(
            norm_back_kernel, norm_outs, meta, [grad, *scatter_parts(send, keep), mid, gains[l, 1]])
        low_parts = gather_parts(low_own)
        low, g_proj, g_fouts[l], g_seconds[l], smalls[l], send, keep = run(
            lambda *r, n=len(w_io): mix_back_kernel(count, n, *r),
            [((total, width), BF), ((total, 3 * chans), BF), ((hid, chans), F32), ((half, hid), F32),
             ((8, 3 * chans), F32)] + parts_out,
            meta,
            low_parts + w_io + [long, long_t, short, short_t, short0, short0_t, seconds[l], decay, fout[l], rows5[l],
                                skip[l], chan, inner],
            io_scratch,
            flops=5 * 10**9,
        )
        sent.append(send)
        send_io, mine = run(
            io_grads_kernel, [((nz, width, cols), BF)] * 2, meta, [g_proj, every, mixed, low],
            [((3 * chans, width), BF), ((chans, width), BF)], flops=2 * 10**9)
        io_units[l] = (mine, comm.flip(send_io, "grp", n_grp))
        grad, low_own, toks[2 * l] = run(
            norm_back_kernel, norm_outs, meta, [grad, *scatter_parts(send, keep), first, gains[l, 0]])
        if l:
            low_parts = gather_parts(low_own)

    send, mine = run(
        lambda *r: pack_kernel(depth, *r), [((nz, SMALL, cols), BF)] * 2, meta,
        up_biases + smalls + g_fouts + toks + [e_wide, e_all],
        [((5, 2 * SLOT, 3 * chans), F32), ((SMALL, width), F32)])
    small = owner_end(owner_turn(mine, comm.flip(send, "grp", n_grp)))
    norm_gain_grad, norm_bias_grad, branch_grad, in_bias_grad, taps_grad, tap_bias_grad, skip_grad, fout_grad, up_bias_grad = run(
        lambda *r: finish_small_kernel(q, *r),
        [(v.shape, F32) for v in (norm_gain, norm_bias, branch_bias, in_bias, conv_weight, conv_bias, skip_bias,
                                  filt_out, up_bias)],
        meta, gather_parts(small))

    def finish(kernel, unit, shapes, old, scratch=()):
        outs = []
        for shape in shapes:
            outs.append(((depth,) + shape, F32, (1,) + shape, lambda i, m, l=l, n=len(shape): (l,) + (0,) * n))
        return run(
            lambda *r, n=len(old): kernel(n, *r), outs, meta, gather_parts(unit) + [(v, None, None) for v in old],
            scratch, alias={5: 0, 6: 1} if old else None)

    mlp_shapes = [(width, ff_shard), (n_grp, n_seq, f, cols)]
    io_shapes = [(width, 3 * cols), (n_grp, n_seq, q, cols)]
    mlp_grads, io_grads = [], []
    for l in reversed(range(depth)):
        mine, got = io_units[l]
        pieces = owner_turn(mine, after(got, sent[2]) if l else got)
        if l:
            pieces = [pieces[0]] + [after(v, sent[3]) for v in pieces[1:]]
        io_unit = owner_end(pieces)
        mlp_unit = after(mlp_units[l], sent[3] if l else io_unit, *([] if l else [small]))
        mlp_grads = finish(finish_mlp_kernel, mlp_unit, mlp_shapes, mlp_grads)
        io_grads = finish(finish_io_kernel, io_unit, io_shapes, io_grads, [((3 * cols, width), F32)])
    up_grad, down_grad = mlp_grads
    in_grad, out_grad = io_grads

    net_grads = second_pull(jnp.stack(g_seconds))
    flat = jnp.concatenate([v.reshape(-1) for v in net_grads])
    flat = jnp.pad(flat, (0, -flat.shape[0] % 1024)).reshape(-1, 128)
    flat = comm.sum_all(comm.sum_all(flat, "seq", n_seq), "grp", n_grp).reshape(-1)
    shared, at = [], 0
    for v in net_grads:
        shared.append(flat[at : at + v.size].reshape(v.shape))
        at += v.size
    return (
        state, grad, norm_gain_grad, norm_bias_grad, in_grad, in_bias_grad, taps_grad, tap_bias_grad,
        skip_grad, fout_grad, out_grad.reshape(depth, width, cols), up_grad, up_bias_grad,
        down_grad.reshape(depth, n_grp * ff_shard, cols), branch_grad, shared[0], shared[1], shared[2], shared[3],
    )


def solution(mesh):
    tok = P(("grp", "seq"), None)
    last3, last2 = P(None, None, "grp"), P(None, "grp")
    in_specs = (
        tok, P("grp", None), tok, last3, last3, last3, last2, last3, last2, last2,
        last3, last3, last3, last2, last3, last3, P(), P(), P(), P(),
    )
    out_specs = (
        tok, tok, last3, last3, last3, last2, last3, last2, last2, last3,
        last3, last3, last2, last3, last3, P(), P(), P(), P(),
    )
    small = mesh.shape["seq"] == 4
    return jax.shard_map(body if small else body_any, mesh=mesh, in_specs=in_specs, out_specs=out_specs, check_vma=False)
```

```python
import math

import jax
import jax.numpy as jnp
from jax import lax
from jax.experimental import pallas as pl
from jax.experimental.pallas import tpu as pltpu
from jax.sharding import PartitionSpec as P

EPS = 1e-05
HIGH = lax.Precision.HIGHEST
FAST = math.log(0.01) / 0.3
SLOW = math.log(0.01) / 1.5
F32 = jnp.float32
BF = jnp.bfloat16
INV_SQRT2 = 1.0 / math.sqrt(2.0)
INV_SQRT2PI = 1.0 / math.sqrt(2.0 * math.pi)


def dot(a, b, da, db):
    return lax.dot_general(a, b, (((da,), (db,)), ((), ())), preferred_element_type=F32)


def pick(v, index, axis):
    return lax.dynamic_index_in_dim(v, index, axis, keepdims=False)


class Comm:
    def __init__(self):
        self.n_grp = lax.axis_size("grp")
        self.n_seq = lax.axis_size("seq")
        self.nz = self.n_grp // 2
        self.ny = self.n_seq // 2
        g = lax.axis_index("grp")
        s = lax.axis_index("seq")
        self.g, self.s = g, s
        self.z, self.x = g // 2, g % 2
        self.y, self.c = s // 2, s % 2

    @staticmethod
    def flip(v, axis, size):
        return lax.ppermute(v, axis, [(i, i ^ 1) for i in range(size)])

    @staticmethod
    def turn(v, axis, size, k):
        half = size // 2
        perm = [(2 * i + j, 2 * ((i + k) % half) + j) for i in range(half) for j in range(2)]
        return lax.ppermute(v, axis, perm)

    def _gather(self, v, axis, size, major, minor):
        half = size // 2
        if half > 4:
            return lax.all_gather(v, axis, axis=0, tiled=False)
        parts = [v] + [self.turn(v, axis, size, k) for k in range(1, half)]
        others = [self.flip(p, axis, size) for p in parts]
        if half == 2:
            zero = major == 0
            mine = jnp.stack([jnp.where(zero, parts[0], parts[1]), jnp.where(zero, parts[1], parts[0])])
            them = jnp.stack([jnp.where(zero, others[0], others[1]), jnp.where(zero, others[1], others[0])])
        else:
            order = jnp.mod(major - jnp.arange(half), half)
            mine = jnp.stack([pick(jnp.stack(parts), order[i], 0) for i in range(half)])
            them = jnp.stack([pick(jnp.stack(others), order[i], 0) for i in range(half)])
        first = jnp.where(minor == 0, mine, them)
        second = jnp.where(minor == 0, them, mine)
        return jnp.stack([first, second], axis=1).reshape((size,) + v.shape)

    def gather_seq(self, v):
        return self._gather(v, "seq", self.n_seq, self.y, self.c)

    def gather_grp(self, v):
        half = self.nz
        slab = jnp.zeros((half,) + v.shape, v.dtype)
        zeros = (0,) * v.ndim
        for k in range(half):
            part = v if k == 0 else self.turn(v, "grp", self.n_grp, k)
            slab = lax.dynamic_update_slice(slab, part[None], (jnp.mod(self.z - k, half),) + zeros)
        other = self.flip(slab, "grp", self.n_grp)
        first = jnp.where(self.x == 0, slab, other)
        second = jnp.where(self.x == 0, other, slab)
        return jnp.stack([first, second], axis=1).reshape((self.n_grp,) + v.shape)

    def _scatter(self, v, axis, size, major, minor, kind):
        half = size // 2
        if half > 4:
            return lax.psum_scatter(v.astype(kind), axis, scatter_dimension=0, tiled=False).astype(F32)
        v = v.reshape((half, 2) + v.shape[1:])
        got = self.flip(pick(v, 1 - minor, 1).astype(kind), axis, size)
        mine = pick(v, minor, 1).astype(F32) + got.astype(F32)
        total = pick(mine, major, 0)
        for k in range(1, half):
            sent = pick(mine, jnp.mod(major + k, half), 0).astype(kind)
            total = total + self.turn(sent, axis, size, k).astype(F32)
        return total

    def scatter_seq(self, v, kind=BF):
        return self._scatter(v, "seq", self.n_seq, self.y, self.c, kind)

    def scatter_grp(self, v, kind=BF):
        return self._scatter(v, "grp", self.n_grp, self.z, self.x, kind)

    def sum_all(self, v, axis, size):
        half = size // 2
        if half > 4:
            return lax.psum(v, axis)
        v = v + self.flip(v, axis, size)
        total = v
        for k in range(1, half):
            total = total + self.turn(v, axis, size, k)
        return total


def norm_stats(value):
    center = value - jnp.mean(value, axis=-1, keepdims=True)
    scale = lax.rsqrt(jnp.mean(center * center, axis=-1, keepdims=True) + EPS)
    return center * scale, scale


def norm_back(grad, hat, scale, gain):
    inner = grad * gain
    mean_one = jnp.mean(inner, axis=-1, keepdims=True)
    mean_two = jnp.mean(inner * hat, axis=-1, keepdims=True)
    return scale * (inner - mean_one - hat * mean_two), jnp.sum(grad * hat, axis=0), jnp.sum(grad, axis=0)


def positions(length):
    index = jnp.arange(length, dtype=jnp.int32).astype(F32)
    tpos = index / (length - 1)
    bands = 0.0001 + (15.0 - 0.0001) * jnp.arange(16, dtype=jnp.int32).astype(F32) / 15.0
    angle = 2.0 * math.pi / length * index[:, None] * bands[None, :]
    return (jnp.concatenate([tpos[:, None], jnp.cos(angle), -jnp.sin(angle)], axis=1), tpos)


def odd_table(size, place):
    freq = 2 * jnp.arange(size // 2, dtype=jnp.int32) + 1
    turn = jnp.bitwise_and(freq[:, None] * place[None, :], 2 * size - 1)
    angle = turn.astype(F32) * (math.pi / size)
    return jnp.stack([jnp.cos(angle), -jnp.sin(angle)])


def filter_of(fin, fmid, fbias, freq, fout, feats, decay):
    inner = jnp.sin(freq[0] * (jnp.dot(feats, fin, precision=HIGH) + fbias[0]))
    inner = jnp.sin(freq[1] * (jnp.dot(inner, fmid, precision=HIGH) + fbias[1]))
    return jnp.dot(inner, fout, precision=HIGH) * decay


def lagged(v, lag, mask):
    return jnp.where(mask[None, :, None], jnp.pad(v, ((0, 0), (lag, 0), (0, 0)))[:, : v.shape[1]], 0.0)


def ahead(v, lag):
    return jnp.pad(v, ((0, 0), (0, lag), (0, 0)))[:, lag:]


def times(ar, ai, br, bi):
    return ar * br - ai * bi, ar * bi + ai * br


def times_conj(ar, ai, br, bi):
    return ar * br + ai * bi, ai * br - ar * bi


class Mixer:
    def __init__(self, lens, total, most):
        half = total // 2
        self.half, self.most, self.total, self.count = half, most, total, lens.shape[0]
        starts = half + jnp.cumsum(lens) - lens
        place = jnp.arange(total, dtype=jnp.int32)
        begin = jnp.zeros((total,), jnp.int32)
        for k in range(lens.shape[0]):
            begin = jnp.where(starts[k] <= place, starts[k], begin)
        self.masks = [None] + [place - lag >= begin for lag in (1, 2)]
        self.long = odd_table(2 * half, place[:half]).reshape(2 * half, half).astype(BF)
        self.short0 = odd_table(2 * most, place[:most]).reshape(2 * most, most).astype(BF)
        tail = place[half:]
        tables = []
        for k in range(lens.shape[0]):
            rel = tail - starts[k]
            inside = (rel >= 0) & (rel < lens[k])
            table = odd_table(2 * most, jnp.where(inside, rel, 0))
            tables.append(jnp.where(inside[None, None, :], table, 0.0))
        self.short = jnp.stack(tables).reshape(lens.shape[0] * 2 * most, total - half).astype(BF)

    def split(self, long, short):
        chans = long.shape[-1]
        long = long.reshape(2, self.half, chans)
        short = short.reshape(self.count, 2, self.most, chans)
        return long[0], long[1], short[:, 0], short[:, 1]

    def forth(self, v):
        v = v.astype(BF)
        return self.split(dot(self.long, v[: self.half], 1, 0), dot(self.short, v[self.half :], 1, 0))

    def back(self, spec):
        lr, li, sr, si = spec
        long = jnp.stack([lr, li]).reshape(2 * self.half, -1) * (1.0 / self.half)
        short = jnp.stack([sr, si], axis=1).reshape(self.count * 2 * self.most, -1) * (1.0 / self.most)
        return jnp.concatenate([dot(self.long, long.astype(BF), 0, 0), dot(self.short, short.astype(BF), 0, 0)])

    def filt_spec(self, filt):
        filt = filt.astype(BF)
        long = dot(self.long, filt, 1, 0)
        short = dot(self.short0, filt[: self.most], 1, 0)
        return long[: self.half], long[self.half :], short[: self.most], short[self.most :]

    def filt_back(self, grads):
        lr, li, sr, si = grads
        long = jnp.concatenate([lr, li]) * (1.0 / self.half)
        short = jnp.concatenate([sr, si]) * (1.0 / self.most)
        head = dot(self.short0, short.astype(BF), 0, 0)
        return dot(self.long, long.astype(BF), 0, 0) + jnp.pad(head, ((0, self.half - self.most), (0, 0)))


def body_any(
    tokens,
    lengths,
    cotangent,
    norm_gain,
    norm_bias,
    in_weight,
    in_bias,
    conv_weight,
    conv_bias,
    skip_bias,
    filt_out,
    out_weight,
    up_weight,
    up_bias,
    down_weight,
    branch_bias,
    filt_in,
    filt_mid,
    filt_bias,
    sine_freq,
):
    comm = Comm()
    n_grp, n_seq, s = comm.n_grp, comm.n_seq, comm.s
    depth = norm_gain.shape[0]
    tok_rows, width = tokens.shape
    total = tok_rows * n_seq
    cols = width // n_grp
    q = cols // n_seq
    ff_shard = up_weight.shape[2]
    f = ff_shard // n_seq
    hid = filt_out.shape[1]
    chans = n_grp * q

    def unit_in(l):
        return pick(in_weight[l].T.reshape(3, n_seq, q, width), s, 1).reshape(3 * q, width)

    def unit_out(l):
        return pick(out_weight[l].reshape(n_grp, n_seq, q, cols), s, 1).reshape(chans, cols).T

    def unit_up(l):
        return lax.dynamic_slice_in_dim(up_weight[l], s * f, f, 1).T

    def unit_down(l):
        return pick(down_weight[l].reshape(n_grp, n_seq, f, cols), s, 1).reshape(n_grp * f, cols).T

    tok_small = [norm_gain, norm_bias, branch_bias]
    seq_small = [
        pick(in_bias.reshape(depth, 3, n_seq, q), s, 2),
        pick(conv_weight.reshape(depth, 3, 3, n_seq, q), s, 3),
        pick(conv_bias.reshape(depth, 3, n_seq, q), s, 2),
        pick(skip_bias.reshape(depth, n_seq, q), s, 1),
        pick(filt_out.reshape(depth, hid, n_seq, q), s, 2),
        pick(up_bias.reshape(depth, n_seq, f), s, 1),
    ]
    shapes = [v.shape for v in tok_small + seq_small]
    sizes = [math.prod(shape) for shape in shapes]
    packed = jnp.concatenate([v.reshape(-1) for v in tok_small + seq_small])
    fill = -packed.shape[0] % 2048
    packed = comm.gather_grp(jnp.pad(packed, (0, fill)).reshape(-1, 128)).reshape(n_grp, -1).astype(F32)
    spread, at = [], 0
    for shape, size in zip(shapes, sizes):
        spread.append(packed[:, at : at + size].reshape((n_grp,) + shape))
        at += size

    def last(v):
        return jnp.moveaxis(v, 0, -2).reshape(v.shape[1:-1] + (n_grp * v.shape[-1],))

    def streams(v):
        v = jnp.moveaxis(v, 0, -3)
        return v.reshape(v.shape[:-3] + (3, n_grp * q))

    gains, shifts, b_branch = (last(v) for v in spread[:3])
    b_in, taps, tap_bias = (streams(v) for v in spread[3:6])
    skip, fout, b_up = (last(v) for v in spread[6:9])

    weights = []
    for l in range(depth):
        w_in = comm.gather_grp(unit_in(l)).reshape(3 * chans, width)
        w_out = comm.gather_grp(unit_out(l)).reshape(width, chans)
        w_up = comm.gather_grp(unit_up(l)).reshape(n_grp * f, width)
        w_down = comm.gather_grp(unit_down(l)).reshape(width, n_grp * f)
        weights.append((w_in, w_out, w_up, w_down))

    lens = lengths[0]
    mixer = Mixer(lens, total, total // 4)
    feats, tpos = positions(total // 2)
    channel = (
        jnp.arange(n_grp, dtype=jnp.int32)[:, None] * cols + s * q + jnp.arange(q, dtype=jnp.int32)[None, :]
    ).reshape(-1).astype(F32)
    rate = jnp.abs(FAST + (SLOW - FAST) * channel / (width - 1))
    decay = jnp.exp(-tpos[:, None] * rate[None, :])

    state = tokens.astype(F32)
    saved = []
    for l in range(depth):
        w_in, w_out, w_up, w_down = weights[l]
        filt, filt_pull = jax.vjp(
            lambda *a: filter_of(*a, feats, decay),
            filt_in[l], filt_mid[l], filt_bias[l], sine_freq[l], fout[l],
        )
        hat1, scale1 = norm_stats(state)
        normed = (hat1 * gains[l, 0] + shifts[l, 0]).astype(BF)
        normed = comm.gather_seq(normed).reshape(total, width)
        proj = dot(normed, w_in, 1, 1) + b_in[l].reshape(-1)
        proj = jnp.transpose(proj.astype(BF).reshape(total, 3, chans), (1, 0, 2))
        chan = proj.astype(F32)
        z = tap_bias[l][:, None, :] + taps[l, 0][:, None, :] * chan
        for lag in (1, 2):
            z = z + taps[l, lag][:, None, :] * lagged(chan, lag, mixer.masks[lag])
        prod = z[1] * z[2]
        h_lr, h_li, h_sr, h_si = mixer.filt_spec(filt)
        x_lr, x_li, x_sr, x_si = mixer.forth(prod)
        conv = mixer.back(times(x_lr, x_li, h_lr, h_li) + times(x_sr, x_si, h_sr, h_si))
        inner = conv + skip[l] * prod
        mixed = (z[0] * inner).astype(BF)
        part = dot(mixed, w_out, 1, 1)
        mid = state + comm.scatter_seq(part.reshape(n_seq, tok_rows, width)) + b_branch[l, 0]
        hat2, scale2 = norm_stats(mid)
        normed2 = (hat2 * gains[l, 1] + shifts[l, 1]).astype(BF)
        normed2 = comm.gather_seq(normed2).reshape(total, width)
        pre = dot(normed2, w_up, 1, 1) + b_up[l]
        cdf = 0.5 * (1.0 + lax.erf(pre * INV_SQRT2))
        hidden = (pre * cdf).astype(BF)
        slope = cdf + pre * (jnp.exp(-0.5 * pre * pre) * INV_SQRT2PI)
        part = dot(hidden, w_down, 1, 1)
        state = mid + comm.scatter_seq(part.reshape(n_seq, tok_rows, width)) + b_branch[l, 1]
        saved.append((filt_pull, hat1, scale1, normed, chan, z, prod, inner, (h_lr, h_li, h_sr, h_si),
                      (x_lr, x_li, x_sr, x_si), mixed, hat2, scale2, normed2, slope, hidden))

    grad = cotangent
    units = [None] * depth
    tok_grads, seq_grads, net_grads = [None] * depth, [None] * depth, [None] * depth

    def chunk(v):
        return comm.scatter_grp(v.astype(BF).reshape((n_grp, v.shape[0] // n_grp) + v.shape[1:])).astype(BF)

    for l in reversed(range(depth)):
        w_in, w_out, w_up, w_down = weights[l]
        (filt_pull, hat1, scale1, normed, chan, z, prod, inner, (h_lr, h_li, h_sr, h_si),
         (x_lr, x_li, x_sr, x_si), mixed, hat2, scale2, normed2, slope, hidden) = saved[l]
        low = grad.astype(BF)
        g_two = jnp.sum(low.astype(F32), axis=0)
        low = comm.gather_seq(low).reshape(total, width)
        u_down = chunk(dot(low, hidden, 0, 0))
        g_pre = (dot(low, w_down, 1, 0) * slope).astype(BF)
        g_up_bias = jnp.sum(g_pre.astype(F32), axis=0)
        part = dot(g_pre, w_up, 1, 0)
        u_up = chunk(dot(g_pre, normed2, 0, 0))
        g_normed2 = comm.scatter_seq(part.reshape(n_seq, tok_rows, width))
        g_mid, gain2, shift2 = norm_back(g_normed2, hat2, scale2, gains[l, 1])
        g_mid = g_mid + grad
        low = g_mid.astype(BF)
        g_one = jnp.sum(low.astype(F32), axis=0)
        low = comm.gather_seq(low).reshape(total, width)
        u_out = chunk(dot(low, mixed, 0, 0))
        g_y = dot(low, w_out, 1, 0).astype(BF).astype(F32)
        g_conv = g_y * z[0]
        g_skip = jnp.sum(g_conv * prod, axis=0)
        y_lr, y_li, y_sr, y_si = mixer.forth(g_conv)
        corr = mixer.back(times_conj(y_lr, y_li, h_lr, h_li) + times_conj(y_sr, y_si, h_sr, h_si))
        f_lr, f_li = times_conj(y_lr, y_li, x_lr, x_li)
        f_sr, f_si = times_conj(y_sr, y_si, x_sr, x_si)
        g_filt = mixer.filt_back((f_lr, f_li, jnp.sum(f_sr, axis=0), jnp.sum(f_si, axis=0)))
        g_prod = corr + skip[l] * g_conv
        g_z = jnp.stack([g_y * inner, g_prod * z[2], g_prod * z[1]])
        g_taps = [jnp.sum(g_z * chan, axis=1)]
        g_proj = taps[l, 0][:, None, :] * g_z
        for lag in (1, 2):
            kept = jnp.where(mixer.masks[lag][None, :, None], g_z, 0.0)
            g_taps.append(jnp.sum(g_z * lagged(chan, lag, mixer.masks[lag]), axis=1))
            g_proj = g_proj + taps[l, lag][:, None, :] * ahead(kept, lag)
        g_proj = jnp.transpose(g_proj.astype(BF), (1, 0, 2)).reshape(total, 3 * chans)
        g_in_bias = jnp.sum(g_proj.astype(F32), axis=0).reshape(3, chans)
        part = dot(g_proj, w_in, 1, 0)
        u_in = chunk(dot(g_proj, normed, 0, 0))
        g_normed = comm.scatter_seq(part.reshape(n_seq, tok_rows, width))
        g_state, gain1, shift1 = norm_back(g_normed, hat1, scale1, gains[l, 0])
        grad = g_mid + g_state
        units[l] = (u_in, u_out, u_up, u_down)
        pulled = filt_pull(g_filt)
        net_grads[l] = pulled[:4]
        tok_grads[l] = (jnp.stack([gain1, gain2]), jnp.stack([shift1, shift2]), jnp.stack([g_one, g_two]))
        seq_grads[l] = (g_in_bias, jnp.stack(g_taps), jnp.sum(g_z, axis=1), g_skip, pulled[4], g_up_bias)

    def whole(place):
        return [comm.gather_seq(units[l][place]).astype(F32) for l in range(depth)]

    in_grad = jnp.stack([
        jnp.transpose(v.reshape(n_seq, 3, q, width), (3, 1, 0, 2)).reshape(width, 3 * cols) for v in whole(0)])
    out_grad = jnp.stack([
        jnp.transpose(v.reshape(n_seq, cols, n_grp, q), (2, 0, 3, 1)).reshape(width, cols) for v in whole(1)])
    up_grad = jnp.stack([jnp.transpose(v, (2, 0, 1)).reshape(width, ff_shard) for v in whole(2)])
    down_grad = jnp.stack([
        jnp.transpose(v.reshape(n_seq, cols, n_grp, f), (2, 0, 3, 1)).reshape(n_grp * ff_shard, cols)
        for v in whole(3)])

    def by_owner(v):
        v = v.reshape(v.shape[:-1] + (n_grp, v.shape[-1] // n_grp))
        return jnp.moveaxis(v, -2, 0).reshape(n_grp, -1)

    def by_owner3(v):
        v = v.reshape(v.shape[:-2] + (n_grp, 3, q))
        return jnp.moveaxis(v, -3, 0).reshape(n_grp, -1)

    tok_all = [jnp.stack(v) for v in zip(*tok_grads)]
    seq_all = [jnp.stack(v) for v in zip(*seq_grads)]
    tok_flat = jnp.concatenate([by_owner(v) for v in tok_all], axis=1)
    seq_flat = jnp.concatenate(
        [by_owner3(v) for v in seq_all[:3]] + [by_owner(v) for v in seq_all[3:]], axis=1)
    tok_len, seq_len = tok_flat.shape[1], seq_flat.shape[1]
    flat = jnp.concatenate([tok_flat, seq_flat], axis=1)
    flat = jnp.pad(flat, ((0, 0), (0, -flat.shape[1] % 1024)))
    small = comm.scatter_grp(flat.reshape(n_grp, -1, 128), F32).reshape(-1)
    tok_sum = comm.sum_all(small[:tok_len].reshape(-1, 128), "seq", n_seq).reshape(-1)
    seq_part = jnp.pad(small[tok_len : tok_len + seq_len], (0, -seq_len % 1024)).reshape(-1, 128)
    seq_sum = comm.gather_seq(seq_part).reshape(n_seq, -1)[:, :seq_len]
    norm_gain_grad, norm_bias_grad, branch_grad = tok_sum.reshape(3, depth, 2, cols)
    pieces, at = [], 0
    for shape in shapes[3:]:
        size = math.prod(shape)
        part = seq_sum[:, at : at + size].reshape((n_seq,) + shape)
        at += size
        part = jnp.moveaxis(part, 0, -2)
        pieces.append(part)
    in_bias_grad = pieces[0].reshape(depth, 3 * cols)
    taps_grad = pieces[1].reshape(depth, 3, 3 * cols)
    tap_bias_grad = pieces[2].reshape(depth, 3 * cols)
    skip_grad = pieces[3].reshape(depth, cols)
    fout_grad = pieces[4].reshape(depth, hid, cols)
    up_bias_grad = pieces[5].reshape(depth, ff_shard)

    nets = [jnp.stack(v) for v in zip(*net_grads)]
    flat = jnp.concatenate([v.reshape(-1) for v in nets])
    flat = jnp.pad(flat, (0, -flat.shape[0] % 1024)).reshape(-1, 128)
    flat = comm.sum_all(comm.sum_all(flat, "seq", n_seq), "grp", n_grp).reshape(-1)
    shared, at = [], 0
    for v in nets:
        shared.append(flat[at : at + v.size].reshape(v.shape))
        at += v.size
    return (
        state, grad, norm_gain_grad, norm_bias_grad, in_grad, in_bias_grad, taps_grad, tap_bias_grad,
        skip_grad, fout_grad, out_grad, up_grad, up_bias_grad, down_grad, branch_grad,
        shared[0], shared[1], shared[2], shared[3],
    )


ORDER = (0, 2, 1, 3)
VMEM_BYTES = 56 * 2**20
SMALL = 64
SLOT = 24
COST = 1000
UP_AT = 48
TOK = 52
NET = 112


def run(kernel, outs, meta, args, scratch=(), flops=0, alias=None):
    specs, arrays = [], []
    for a in args:
        if isinstance(a, tuple):
            array, block, place = a
            if block is None:
                specs.append(pl.BlockSpec(memory_space=pl.ANY))
            else:
                specs.append(pl.BlockSpec(block, place, pipeline_mode=pl.Buffered(1)))
            arrays.append(array)
        else:
            specs.append(pl.BlockSpec(memory_space=pltpu.VMEM))
            arrays.append(a)
    out_specs, shapes = [], []
    for o in outs:
        shapes.append(jax.ShapeDtypeStruct(o[0], o[1]))
        if len(o) > 2:
            out_specs.append(pl.BlockSpec(o[2], o[3], pipeline_mode=pl.Buffered(1)))
        else:
            out_specs.append(pl.BlockSpec(memory_space=pltpu.VMEM))
    moved = sum(o.size * o.dtype.itemsize for o in shapes) + sum(a.size * a.dtype.itemsize for a in arrays)
    return pl.pallas_call(
        kernel,
        out_shape=shapes,
        grid_spec=pltpu.PrefetchScalarGridSpec(
            num_scalar_prefetch=1,
            grid=(1,),
            in_specs=specs,
            out_specs=out_specs,
            scratch_shapes=[pltpu.VMEM(shape, kind) for shape, kind in scratch],
        ),
        input_output_aliases=alias or {},
        compiler_params=pltpu.CompilerParams(vmem_limit_bytes=VMEM_BYTES),
        cost_estimate=pl.CostEstimate(flops=flops // COST, bytes_accessed=moved // COST, transcendentals=0),
    )(meta, *arrays)


def join(meta, parts, all_ref):
    rows = parts[0].shape[0]
    for k, part in enumerate(parts):
        at = pl.multiple_of((meta[0] ^ ORDER[k]) * rows, rows)
        all_ref[pl.ds(at, rows), :] = part[...]


def owners(meta, refs):
    if len(refs) == 1:
        return [(g, refs[0].at[g]) for g in range(refs[0].shape[0])]
    half = refs[0].shape[0]
    found = []
    for k in range(half):
        at = 2 * lax.rem(meta[1] - k + half, half)
        found.append((at + meta[2], refs[0].at[k]))
        found.append((at + 1 - meta[2], refs[1].at[k]))
    return found


def span(g, size):
    if isinstance(g, int):
        return pl.ds(g * size, size)
    return pl.ds(pl.multiple_of(g * size, size), size)


def place_wide(meta, refs, wide):
    rows = wide.shape[0]
    for g, block in owners(meta, refs):
        wide[:, span(g, block.shape[-1])] = block[:rows, :]


def place_io(meta, refs, wi, wo):
    n_grp = wi.shape[1] // 128
    part = wi.shape[0] // n_grp
    q = part // 3
    for g, block in owners(meta, refs):
        for lb in range(n_grp):
            at = lb * 4 * q
            wi[span(g, part), lb * 128 : (lb + 1) * 128] = block[at : at + part, :]
            wo[lb * q : (lb + 1) * q, span(g, 128)] = block[at + part : at + part + q, :]


def part_out(meta, value, at, send, keep):
    rows = value.shape[0] // 4
    w = value.shape[1]
    even = jnp.stack([value[:rows], value[2 * rows : 3 * rows]])
    odd = jnp.stack([value[rows : 2 * rows], value[3 * rows :]])
    low = meta[4] == 0
    keep[:, :, at : at + w] = jnp.where(low, even, odd)
    send[:, :, at : at + w] = jnp.where(low, odd, even).astype(BF)


def masks_of(meta, total, wide, count):
    place = lax.broadcasted_iota(jnp.int32, (total, wide), 0)
    begin = jnp.zeros((total, wide), jnp.int32)
    for k in range(count):
        begin = jnp.where(place >= meta[5 + k], meta[5 + k], begin)
    return place, [None] + [place - lag >= begin for lag in (1, 2)]


def roll_down(v, lag):
    return pltpu.roll(v, lag, 0)


def stream_z(chan, j, wide, rows5, masks):
    at = j * wide
    v = chan[:, at : at + wide].astype(F32)
    z = rows5[4:5, at : at + wide] + rows5[1:2, at : at + wide] * v
    for lag in (1, 2):
        z = z + rows5[1 + lag : 2 + lag, at : at + wide] * jnp.where(masks[lag], roll_down(v, lag), 0.0)
    return z


def spectra(v, long, short):
    half = v.shape[0] // 2
    low = v.astype(BF)
    return dot(long[...], low[:half], 1, 0), dot(short[...], low[half:], 1, 0)


def filt_spectra(filt, long, short0):
    low = filt.astype(BF)
    return dot(long[...], low, 1, 0), dot(short0[...], low[: short0.shape[1]], 1, 0)


def each(long, short, count):
    half = long.shape[0] // 2
    most = short.shape[0] // count // 2
    pairs = [(long[:half], long[half:])]
    for k in range(count):
        pairs.append((short[2 * k * most : (2 * k + 1) * most], short[(2 * k + 1) * most : (2 * k + 2) * most]))
    return pairs


def unspectra(pairs, long_t, short_t):
    half, most = pairs[0][0].shape[0], pairs[1][0].shape[0]
    long = (jnp.concatenate(pairs[0]) * (1.0 / half)).astype(BF)
    short = (jnp.concatenate([v for pair in pairs[1:] for v in pair]) * (1.0 / most)).astype(BF)
    return jnp.concatenate([dot(long_t[...], long, 1, 0), dot(short_t[...], short, 1, 0)])


def exact(a, b, da, db):
    return lax.dot_general(a, b, (((da,), (db,)), ((), ())), precision=HIGH, preferred_element_type=F32)


def mix_forth_kernel(count, nio, raw, meta, *refs):
    parts, refs = refs[:4], refs[4:]
    io, refs = refs[:nio], refs[nio:]
    (long, long_t, short, short_t, short0, second, decay, fout, rows5, skip, gain, shift,
     every, chan, inner_ref, mixed_ref, send, keep, wi, wo) = refs
    join(meta, parts, every)
    if raw:
        every[...] = (every[...].astype(F32) * gain[...] + shift[...]).astype(BF)
    place_io(meta, io, wi, wo)
    total, wide = mixed_ref.shape
    _, masks = masks_of(meta, total, wide, count)
    z = []
    for j in range(3):
        at = j * wide
        proj = dot(every[...], wi[at : at + wide, :], 1, 1) + rows5[0:1, at : at + wide]
        chan[:, at : at + wide] = proj.astype(BF)
        z.append(stream_z(chan, j, wide, rows5, masks))
    prod = z[1] * z[2]
    filt = exact(second[...], fout[...], 1, 0) * decay[...]
    hs = each(*filt_spectra(filt, long, short0), 1)
    xs = each(*spectra(prod, long, short), count)
    ys = [times(*x, *hs[min(k, 1)]) for k, x in enumerate(xs)]
    inner = unspectra(ys, long_t, short_t) + skip[...] * prod
    inner_ref[...] = inner
    mixed_ref[...] = (z[0] * inner).astype(BF)
    for n in range(4):
        w = wo.shape[1] // 4
        part_out(meta, dot(mixed_ref[...], wo[:, n * w : (n + 1) * w], 1, 0), n * w, send, keep)


def mix_back_kernel(count, nio, meta, *refs):
    parts, refs = refs[:4], refs[4:]
    io, refs = refs[:nio], refs[nio:]
    (long, long_t, short, short_t, short0, short0_t, second, decay, fout, rows5, skip, chan, inner,
     every, g_proj_ref, g_fout, g_second, small, send, keep, wi, wo) = refs
    join(meta, parts, every)
    place_io(meta, io, wi, wo)
    total, wide = inner.shape
    place, masks = masks_of(meta, total, wide, count)
    z = [stream_z(chan, j, wide, rows5, masks) for j in range(3)]
    prod = z[1] * z[2]
    filt = exact(second[...], fout[...], 1, 0) * decay[...]
    hs = each(*filt_spectra(filt, long, short0), 1)
    xs = each(*spectra(prod, long, short), count)
    g_y = dot(every[...], wo[...], 1, 1).astype(BF).astype(F32)
    g_conv = g_y * z[0]
    ys = each(*spectra(g_conv, long, short), count)
    corr = unspectra([times_conj(*y, *hs[min(k, 1)]) for k, y in enumerate(ys)], long_t, short_t)
    g_prod = corr + skip[...] * g_conv
    small[...] = jnp.zeros_like(small)
    small[5:6, :wide] = jnp.sum(g_conv * prod, axis=0, keepdims=True)
    for j, g_z in enumerate((g_y * inner[...], g_prod * z[2], g_prod * z[1])):
        at = j * wide
        v = chan[:, at : at + wide].astype(F32)
        small[4:5, at : at + wide] = jnp.sum(g_z, axis=0, keepdims=True)
        small[1:2, at : at + wide] = jnp.sum(g_z * v, axis=0, keepdims=True)
        g_proj = rows5[1:2, at : at + wide] * g_z
        for lag in (1, 2):
            kept = jnp.where(masks[lag], g_z, 0.0)
            small[1 + lag : 2 + lag, at : at + wide] = jnp.sum(kept * roll_down(v, lag), axis=0, keepdims=True)
            moved = jnp.where(place < total - lag, roll_down(kept, total - lag), 0.0)
            g_proj = g_proj + rows5[1 + lag : 2 + lag, at : at + wide] * moved
        low = g_proj.astype(BF)
        g_proj_ref[:, at : at + wide] = low
        small[0:1, at : at + wide] = jnp.sum(low.astype(F32), axis=0, keepdims=True)
    for n in range(4):
        w = wi.shape[1] // 4
        part_out(meta, dot(g_proj_ref[...], wi[:, n * w : (n + 1) * w], 1, 0), n * w, send, keep)
    fs = [times_conj(*y, *x) for y, x in zip(ys, xs)]
    f_short = fs[1]
    for pair in fs[2:]:
        f_short = (f_short[0] + pair[0], f_short[1] + pair[1])
    half, most = fs[0][0].shape[0], f_short[0].shape[0]
    g_filt = dot(long_t[...], (jnp.concatenate(fs[0]) * (1.0 / half)).astype(BF), 1, 0)
    head = dot(short0_t[...], (jnp.concatenate(f_short) * (1.0 / most)).astype(BF), 1, 0)
    g_filt = jnp.concatenate([g_filt[:most] + head, g_filt[most:]]) * decay[...]
    g_fout[...] = exact(second[...].T, g_filt, 1, 0)
    g_second[...] = exact(g_filt, fout[...], 1, 1)


def mlp_forth_kernel(nup, ndown, meta, *refs):
    parts, refs = refs[:4], refs[4:]
    up, refs = refs[:nup], refs[nup:]
    down, refs = refs[:ndown], refs[ndown:]
    b_up, every, hidden, slope, send, keep, wide_up, wide_down = refs
    join(meta, parts, every)
    place_wide(meta, up, wide_up)
    tile = wide_up.shape[1] // 4
    for n in range(4):
        at = n * tile
        pre = dot(every[...], wide_up[:, at : at + tile], 1, 0) + b_up[:, at : at + tile]
        cdf = 0.5 * (1.0 + lax.erf(pre * INV_SQRT2))
        hidden[:, at : at + tile] = (pre * cdf).astype(BF)
        slope[:, at : at + tile] = (cdf + pre * (jnp.exp(-0.5 * pre * pre) * INV_SQRT2PI)).astype(BF)
    place_wide(meta, down, wide_down)
    tile = wide_down.shape[1] // 4
    for n in range(4):
        part_out(meta, dot(hidden[...], wide_down[:, n * tile : (n + 1) * tile], 1, 0), n * tile, send, keep)


def mlp_back_kernel(nup, ndown, meta, *refs):
    parts, refs = refs[:4], refs[4:]
    up, refs = refs[:nup], refs[nup:]
    down, refs = refs[:ndown], refs[ndown:]
    slope, every, g_pre_ref, g_bias, send, keep, wide_up, wide_down = refs
    join(meta, parts, every)
    place_wide(meta, down, wide_down)
    tile = slope.shape[1] // 4
    for n in range(4):
        at = n * tile
        g_hidden = dot(every[...], wide_down[at : at + tile, :], 1, 1)
        g_pre = (g_hidden * slope[:, at : at + tile].astype(F32)).astype(BF)
        g_pre_ref[:, at : at + tile] = g_pre
        g_bias[:, at : at + tile] = jnp.sum(g_pre.astype(F32), axis=0, keepdims=True)
    place_wide(meta, up, wide_up)
    tile = wide_up.shape[0] // 4
    for n in range(4):
        at = n * tile
        part_out(meta, dot(g_pre_ref[...], wide_up[at : at + tile, :], 1, 1), at, send, keep)


def hat_of(value):
    center = value - jnp.mean(value, axis=-1, keepdims=True)
    scale = lax.rsqrt(jnp.mean(center * center, axis=-1, keepdims=True) + EPS)
    return center * scale, scale


def first_norm_kernel(meta, tokens, cotangent, normed, low, sums):
    hat, _ = hat_of(tokens[...].astype(F32))
    normed[...] = hat.astype(BF)
    rounded = cotangent[...].astype(BF)
    low[...] = rounded
    sums[...] = jnp.zeros_like(sums)
    sums[2:3, :] = jnp.sum(rounded.astype(F32), axis=0, keepdims=True)


def add_norm_kernel(meta, state, keep, got, crossed, bias, gain, shift, new, normed):
    value = state[...].astype(F32) + (keep[0] + got[0].astype(F32) + crossed[...].astype(F32)) + bias[...]
    new[...] = value
    hat, _ = hat_of(value)
    normed[...] = (hat * gain[...] + shift[...]).astype(BF)


def add_kernel(meta, state, keep, got, crossed, bias, new):
    new[...] = state[...] + (keep[0] + got[0].astype(F32) + crossed[...].astype(F32)) + bias[...]


def norm_back_kernel(meta, grad, keep, got, crossed, value, gain, new, low, sums):
    g = keep[0] + got[0].astype(F32) + crossed[...].astype(F32)
    hat, scale = hat_of(value[...].astype(F32))
    inner = g * gain[...]
    mean_one = jnp.mean(inner, axis=-1, keepdims=True)
    mean_two = jnp.mean(inner * hat, axis=-1, keepdims=True)
    total = grad[...] + scale * (inner - mean_one - hat * mean_two)
    new[...] = total
    rounded = total.astype(BF)
    low[...] = rounded
    sums[...] = jnp.zeros_like(sums)
    sums[0:1, :] = jnp.sum(g * hat, axis=0, keepdims=True)
    sums[1:2, :] = jnp.sum(g, axis=0, keepdims=True)
    sums[2:3, :] = jnp.sum(rounded.astype(F32), axis=0, keepdims=True)


def mlp_grads_kernel(meta, every, g_pre, hidden, low, out):
    tile = 256
    rows = every.shape[1]
    for n in range(low.shape[1] // tile):
        w = slice(n * tile, (n + 1) * tile)
        for at, left, right in ((0, every, g_pre), (rows, hidden, low)):
            value = dot(left[...], right[:, w], 0, 0).astype(BF)
            out[2 * n, at : at + rows, :] = value[:, :128]
            out[2 * n + 1, at : at + rows, :] = value[:, 128:]


def mlp_split_kernel(meta, every, g_pre, hidden, low, send, mine):
    tile = 256
    rows = every.shape[1]
    first = meta[2] == 0
    for at, left, right in ((0, every, g_pre), (rows, hidden, low)):
        for n in range(right.shape[1] // tile):
            value = dot(left[...], right[:, n * tile : (n + 1) * tile], 0, 0).astype(BF)
            one, two = value[:, :128], value[:, 128:]
            mine[n, at : at + rows, :] = jnp.where(first, one, two)
            send[n, at : at + rows, :] = jnp.where(first, two, one)


def io_grads_kernel(split, meta, g_proj, every, mixed, low, *refs):
    outs, (g_in, g_out) = refs[:-2], refs[-2:]
    wide = mixed.shape[1]
    for j in range(g_proj.shape[1] // wide):
        w = slice(j * wide, (j + 1) * wide)
        g_in[w, :] = dot(g_proj[:, w], every[...], 0, 0).astype(BF)
    g_out[...] = dot(mixed[...], low[...], 0, 0).astype(BF)
    n_grp = g_in.shape[1] // 128
    part = g_in.shape[0] // n_grp
    q = part // 3
    if split:
        send, mine = outs
        places = [(2 * k + x, t.at[k]) for k in range(n_grp // 2) for x, t in ((meta[2], mine), (1 - meta[2], send))]
    else:
        places = [(g, outs[0].at[g]) for g in range(n_grp)]
    for g, target in places:
        for lb in range(n_grp):
            at = lb * 4 * q
            target[at : at + part, :] = g_in[span(g, part), lb * 128 : (lb + 1) * 128]
            target[at + part : at + part + q, :] = g_out[lb * q : (lb + 1) * q, span(g, 128)]


def owner_sum_kernel(meta, mine, got, keep, send):
    for k in range(2):
        near = meta[1] ^ (2 * k)
        far = near ^ 1
        keep[k] = mine[near].astype(F32) + got[near].astype(F32)
        send[k] = (mine[far].astype(F32) + got[far].astype(F32)).astype(BF)


def last_sum_kernel(meta, keep, got, crossed, out):
    out[...] = (keep[0] + got[0].astype(F32) + crossed[...].astype(F32)).astype(BF)


def small_last_kernel(meta, *refs):
    pieces, out, held = refs[:-2], refs[-2], refs[-1]
    half = len(pieces)
    for k, v in enumerate(pieces):
        held[lax.rem(meta[1] - k + half, half)] = v[...].astype(F32)
    total = held[0]
    for k in range(1, half):
        total = total + held[k]
    out[...] = total.astype(BF)


def small_turn_kernel(meta, mine, got, own, *sends):
    half = got.shape[0]
    for k, send in enumerate((own,) + sends):
        to = lax.rem(meta[1] + k, half)
        send[...] = (mine[to].astype(F32) + got[to].astype(F32)).astype(BF)


def prep_kernel(small, meta, up, down, w_in, w_out, *refs):
    if small:
        in_bias, conv_weight, conv_bias, skip, fout, up_bias, gain, shift, branch = refs[:9]
        refs = refs[9:]
    io_out, up_out, down_out, turned = refs[:4]
    s = meta[0]
    up_out[...] = up[0]
    n_grp, f, lanes = down.shape[1], down.shape[3], down.shape[4]
    q = w_out.shape[3]
    for g in range(n_grp):
        down_out[g * f : (g + 1) * f, :] = down[0, g, 0]
        io_out[g * 4 * q + 3 * q : (g + 1) * 4 * q, :] = w_out[0, g, 0]
    for k in range(3):
        turned[...] = w_in[0, :, k * lanes : (k + 1) * lanes].astype(F32).T
        piece = turned[span(s, q), :].astype(BF)
        for lb in range(n_grp):
            io_out[lb * 4 * q + k * q : lb * 4 * q + (k + 1) * q, :] = piece[:, lb * 128 : (lb + 1) * 128]
    if not small:
        return
    (rows,) = refs[4:]
    depth = up_bias.shape[0]
    rows[...] = jnp.zeros_like(rows)
    b_in, w_tap, b_tap = in_bias[...].astype(F32), conv_weight[...].astype(F32), conv_bias[...].astype(F32)
    skips = skip[...].astype(F32)
    for l in range(depth):
        at = l * SLOT
        outs = fout[l].astype(F32)
        for b in range(3):
            w = slice(b * lanes, (b + 1) * lanes)
            rows[b, at : at + 1, :] = b_in[l : l + 1, w]
            rows[b, at + 1 : at + 4, :] = w_tap[l][:, w]
            rows[b, at + 4 : at + 5, :] = b_tap[l : l + 1, w]
        rows[3, at : at + 4, :] = outs[60:64]
        rows[3, at + 4 : at + 5, :] = skips[l : l + 1]
        for b in range(4):
            rows[b, at + 5 : at + 20, :] = outs[15 * b : 15 * b + 15]
    lane = lax.broadcasted_iota(jnp.int32, (lanes, lanes), 0)
    to = lax.broadcasted_iota(jnp.int32, (lanes, lanes), 1)
    packed = jnp.zeros((2 * SLOT, lanes), F32)
    for b in range(4):
        hit = (lane == s * q + to - b * q) & (to >= b * q) & (to < (b + 1) * q)
        packed = packed + dot(rows[b].astype(BF), jnp.where(hit, 1.0, 0.0).astype(BF), 1, 0)
    ups = up_bias[:, span(s, lanes)].astype(F32)
    tail = [ups, jnp.zeros((TOK - UP_AT - depth, lanes), F32)]
    for v in (gain, shift, branch):
        v = v[...].astype(F32)
        tail += [v[l] for l in range(depth)]
    base = n_grp * 4 * q
    io_out[base : base + SMALL, :] = jnp.concatenate([packed] + tail).astype(BF)


def unpack_kernel(meta, slab, other, e_wide, e_all, tok, rows5, skip, fout, b_up, wide):
    place_wide(meta, (slab, other), wide)
    depth = fout.shape[0]
    hid = fout.shape[1] // depth
    fout[...] = jnp.zeros_like(fout)
    tok[...] = wide[TOK:SMALL, :].astype(F32)
    low = wide[: 2 * SLOT, :]
    five = dot(low, e_wide[...], 1, 0)
    for l in range(depth):
        rows5[l] = five[l * SLOT : l * SLOT + 5]
        b_up[l] = wide[UP_AT + l : UP_AT + l + 1, :].astype(F32)
    for b in range(4):
        found = dot(low, e_all[b], 1, 0)
        for l in range(depth):
            at, to = l * SLOT, l * hid
            fout[l, to + 15 * b : to + 15 * b + 15, :] = found[at + 5 : at + 20]
            if b == 3:
                fout[l, to + 60 : to + 64, :] = found[at : at + 4]
                skip[l] = found[at + 4 : at + 5]


def net_grads(depth, seconds, net):
    feats_t, one_t, pre0, cos0, freq0, pre1, cos1, freq1, mid = net
    g = seconds[0][...]
    for v in seconds[1:]:
        g = g + v[...]
    lanes = g.shape[1]
    hid = lanes // depth
    g = g * cos1[...]
    g_freq1 = jnp.sum(g * pre1[...], axis=0, keepdims=True)
    g = g * freq1[...]
    g_bias1 = jnp.sum(g, axis=0, keepdims=True)
    full = exact(one_t[...], g, 1, 0)
    lane = lax.broadcasted_iota(jnp.int32, (hid, lanes), 1)
    g_mid = full[:hid]
    for l in range(1, depth):
        g_mid = jnp.where(lane >= l * hid, full[l * hid : (l + 1) * hid], g_mid)
    g = exact(g, mid[...], 1, 1) * cos0[...]
    g_freq0 = jnp.sum(g * pre0[...], axis=0, keepdims=True)
    g = g * freq0[...]
    g_bias0 = jnp.sum(g, axis=0, keepdims=True)
    g_in = exact(feats_t[...], g, 1, 0)
    rows = [g_mid, g_in[:33], g_bias0, g_bias1, g_freq0, g_freq1]
    rows.append(jnp.zeros((NET - hid - 37, lanes), F32))
    return jnp.concatenate(rows)


def pack_kernel(depth, meta, *refs):
    ups, refs = refs[:depth], refs[depth:]
    smalls, refs = refs[:depth], refs[depth:]
    fouts, refs = refs[:depth], refs[depth:]
    toks, refs = refs[: 2 * depth + 1], refs[2 * depth + 1 :]
    seconds, refs = refs[:depth], refs[depth:]
    net, refs = refs[:9], refs[9:]
    e_wide, e_all, send, mine, rows, wide = refs
    chans = fouts[0].shape[1]
    hid = fouts[0].shape[0] // depth
    rows[...] = jnp.zeros_like(rows)
    for l in range(depth):
        at = l * SLOT
        rows[4, at : at + 5, :] = smalls[l][:5, :]
        for b in range(4):
            rows[b, at + 5 : at + 20, :chans] = fouts[l][hid * l + 15 * b : hid * l + 15 * b + 15, :]
        rows[3, at : at + 4, :chans] = fouts[l][hid * l + 60 : hid * l + 64, :]
        rows[3, at + 4 : at + 5, :chans] = smalls[l][5:6, :chans]
    packed = dot(rows[4].astype(BF), e_wide[...], 1, 1)
    for b in range(4):
        packed = packed + dot(rows[b, :, :chans].astype(BF), e_all[b], 1, 1)
    wide[: 2 * SLOT, :] = packed
    wide[2 * SLOT :, :] = jnp.zeros((SMALL - 2 * SLOT, wide.shape[1]), F32)
    for l in range(depth):
        wide[UP_AT + l : UP_AT + l + 1, :] = ups[l][...]
        for i in range(2):
            v = toks[2 * l + i]
            at = TOK + 2 * l + i
            wide[at : at + 1, :] = v[0:1, :]
            wide[at + 2 * depth : at + 2 * depth + 1, :] = v[1:2, :]
            wide[at + 4 * depth : at + 4 * depth + 1, :] = toks[2 * l + i + 1][2:3, :]
    grads = net_grads(depth, seconds, net).astype(BF)
    for k in range(send.shape[0]):
        mine[k, :SMALL] = wide[:, span(2 * k + meta[2], 128)].astype(BF)
        send[k, :SMALL] = wide[:, span(2 * k + 1 - meta[2], 128)].astype(BF)
        mine[k, SMALL:] = grads
        send[k, SMALL:] = grads


def finish_small_kernel(q, meta, *refs):
    parts, refs = refs[:4], refs[4:]
    gain, shift, branch, in_bias, conv_weight, conv_bias, skip, fout, up_bias, g_in, g_mid, g_bias, g_freq, held = refs
    depth = fout.shape[0]
    hid = fout.shape[1]
    lanes = parts[0].shape[1]
    lane = lax.broadcasted_iota(jnp.int32, (lanes, lanes), 0)
    to = lax.broadcasted_iota(jnp.int32, (lanes, lanes), 1)
    for k, part in enumerate(parts):
        held[meta[0] ^ ORDER[k]] = part[...].astype(F32)
    tok = held[0]
    for k in range(1, 4):
        tok = tok + held[k]
    for l in range(depth):
        w = slice(l * hid, (l + 1) * hid)
        at = SMALL + hid
        g_mid[l] = tok[SMALL:at, w]
        g_in[l] = tok[at : at + 33, w]
        g_bias[l] = tok[at + 33 : at + 35, w]
        g_freq[l] = tok[at + 35 : at + 37, w]
    for l in range(depth):
        for t, v in enumerate((gain, shift, branch)):
            at = TOK + 2 * depth * t + 2 * l
            v[l] = tok[at : at + 2]
    for k, part in enumerate(parts):
        up_bias[:, span(meta[0] ^ ORDER[k], lanes)] = part[UP_AT : UP_AT + depth, :].astype(F32)
    for b in range(4):
        found = jnp.zeros((2 * SLOT, lanes), F32)
        for k, part in enumerate(parts):
            s = meta[0] ^ ORDER[k]
            hit = (to - s * q == lane - b * q) & (lane >= b * q) & (lane < (b + 1) * q)
            found = found + dot(part[: 2 * SLOT, :], jnp.where(hit, 1.0, 0.0).astype(BF), 1, 0)
        for l in range(depth):
            at = l * SLOT
            fout[l, 15 * b : 15 * b + 15, :] = found[at + 5 : at + 20]
            if b == 3:
                fout[l, 60:64, :] = found[at : at + 4]
                skip[l : l + 1, :] = found[at + 4 : at + 5]
            else:
                w = slice(b * lanes, (b + 1) * lanes)
                in_bias[l : l + 1, w] = found[at : at + 1]
                conv_weight[l, :, w] = found[at + 1 : at + 4]
                conv_bias[l : l + 1, w] = found[at + 4 : at + 5]


def finish_mlp_kernel(extra, meta, *refs):
    parts, refs = refs[:4], refs[4:]
    up, down = refs[extra:]
    rows = up.shape[1]
    n_grp, f = down.shape[1], down.shape[3]
    for k, part in enumerate(parts):
        s = meta[0] ^ ORDER[k]
        up[0, :, span(s, part.shape[1])] = part[:rows, :].astype(F32)
        for g in range(n_grp):
            down[0, g, s] = part[rows + g * f : rows + (g + 1) * f, :].astype(F32)


def finish_io_kernel(extra, meta, *refs):
    parts, refs = refs[:4], refs[4:]
    g_in, g_out, turned = refs[extra:]
    n_grp, q = g_out.shape[1], g_out.shape[3]
    for k, part in enumerate(parts):
        s = meta[0] ^ ORDER[k]
        for lb in range(n_grp):
            at = lb * 4 * q
            for j in range(3):
                row = pl.ds(pl.multiple_of(j * 4 * q + s * q, q), q)
                turned[row, lb * 128 : (lb + 1) * 128] = part[at + j * q : at + (j + 1) * q, :].astype(F32)
            g_out[0, lb, s] = part[at + 3 * q : at + 4 * q, :].astype(F32)
    for j in range(3):
        g_in[0, :, j * 4 * q : (j + 1) * 4 * q] = turned[j * 4 * q : (j + 1) * 4 * q, :].T


def after(value, *others):
    return lax.optimization_barrier((value,) + others)[0]


def body(
    tokens,
    lengths,
    cotangent,
    norm_gain,
    norm_bias,
    in_weight,
    in_bias,
    conv_weight,
    conv_bias,
    skip_bias,
    filt_out,
    out_weight,
    up_weight,
    up_bias,
    down_weight,
    branch_bias,
    filt_in,
    filt_mid,
    filt_bias,
    sine_freq,
):
    comm = Comm()
    n_grp, n_seq, s, nz = comm.n_grp, comm.n_seq, comm.s, comm.nz
    depth = norm_gain.shape[0]
    tok_rows, width = tokens.shape
    total = tok_rows * n_seq
    half, most = total // 2, total // 4
    cols = width // n_grp
    q = cols // n_seq
    ff_shard = up_weight.shape[2]
    f = ff_shard // n_seq
    hid = filt_out.shape[1]
    chans = n_grp * q
    count = lengths.shape[1]
    lens = lengths[0]
    starts = half + jnp.cumsum(lens) - lens
    meta = jnp.concatenate([jnp.stack([s, comm.z, comm.x, comm.y, comm.c]), starts, lens]).astype(jnp.int32)

    down_view = down_weight.reshape(depth, n_grp, n_seq, f, cols)
    out_view = out_weight.reshape(depth, n_grp, n_seq, q, cols)

    def prepare(l, small):
        args = [
            (up_weight, (1, width, f), lambda i, m: (l, 0, m[0])),
            (down_view, (1, n_grp, 1, f, cols), lambda i, m: (l, 0, m[0], 0, 0)),
            (in_weight, (1, width, 3 * cols), lambda i, m: (l, 0, 0)),
            (out_view, (1, n_grp, 1, q, cols), lambda i, m: (l, 0, m[0], 0, 0)),
        ]
        scratch = [((cols, width), F32)]
        rows = width
        if small:
            args += [in_bias, conv_weight, conv_bias, skip_bias, filt_out, up_bias, norm_gain, norm_bias, branch_bias]
            scratch.append(((4, 2 * SLOT, cols), F32))
            rows += SMALL
        outs = [((rows, cols), BF), ((width, f), BF), ((n_grp * f, cols), BF)]
        return run(lambda *r: prep_kernel(small, *r), outs, meta, args, scratch)

    def by_permutes(unit):
        slab = jnp.stack([unit] + [comm.turn(unit, "grp", n_grp, k) for k in range(1, nz)])
        return [slab, comm.flip(slab, "grp", n_grp)]

    first_units = prepare(0, True)
    hat0, low_first, sums_first = run(
        first_norm_kernel,
        [((tok_rows, width), BF), ((tok_rows, width), BF), ((8, width), F32)], meta, [tokens, cotangent])
    ready = list(first_units)
    for l in range(1, depth):
        ready += prepare(l, False)
    chunks, slab = [], None
    for unit in ready:
        if slab is not None:
            unit = after(unit, slab)
        slab = jnp.stack([unit] + [comm.turn(unit, "grp", n_grp, k) for k in range(1, nz)])
        chunks.append([slab, comm.flip(slab, "grp", n_grp)])
    weights = [tuple(chunks[3 * l : 3 * l + 3]) for l in range(depth)]

    lane_from = jnp.arange(n_grp * cols, dtype=jnp.int32)[:, None]
    lane_wide = jnp.arange(3 * chans, dtype=jnp.int32)[None, :]
    lane_chan = jnp.arange(chans, dtype=jnp.int32)[None, :]
    e_wide = ((lane_from // cols == lane_wide // (3 * q)) & (lane_from % cols == lane_wide % (3 * q))).astype(BF)
    e_all = jnp.stack([
        ((lane_from // cols == lane_chan // q) & (lane_from % cols == b * q + lane_chan % q)) for b in range(4)
    ]).astype(BF)
    slab, other = weights[0][0]
    small_block = ((nz, SMALL, cols), lambda i, m: (0, width // SMALL, 0))
    tok_all, rows5, skip, fout, b_up = run(
        unpack_kernel,
        [((6 * depth, width), F32), ((depth, 5, 3 * chans), F32), ((depth, 1, chans), F32),
         ((depth, depth * hid, chans), F32), ((depth, 1, n_grp * f), F32)],
        meta, [(slab,) + small_block, (other,) + small_block, e_wide, e_all], [((SMALL, width), BF)])
    tok_all = tok_all.reshape(3, depth, 2, 1, width)
    gains, shifts, b_branch = tok_all[0], tok_all[1], tok_all[2]

    mixer = Mixer(lens, total, most)
    long, short, short0 = mixer.long, mixer.short, mixer.short0
    long_t, short_t, short0_t = long.T, short.T, short0.T
    feats, tpos = positions(half)
    channel = (
        jnp.arange(n_grp, dtype=jnp.int32)[:, None] * cols + s * q + jnp.arange(q, dtype=jnp.int32)[None, :]
    ).reshape(-1).astype(F32)
    rate = jnp.abs(FAST + (SLOW - FAST) * channel / (width - 1))
    decay = jnp.exp(-tpos[:, None] * rate[None, :])
    lanes = depth * hid
    bias0, bias1 = (filt_bias[:, i].reshape(1, lanes) for i in range(2))
    freq0, freq1 = (sine_freq[:, i].reshape(1, lanes) for i in range(2))
    mid_all = jnp.zeros((lanes, lanes), F32)
    for l in range(depth):
        mid_all = lax.dynamic_update_slice(mid_all, filt_mid[l], (l * hid, l * hid))
    pre0 = jnp.dot(feats, jnp.transpose(filt_in, (1, 0, 2)).reshape(-1, lanes), precision=HIGH) + bias0
    one, cos0 = jnp.sin(freq0 * pre0), jnp.cos(freq0 * pre0)
    pre1 = jnp.dot(one, mid_all, precision=HIGH) + bias1
    second, cos1 = jnp.sin(freq1 * pre1), jnp.cos(freq1 * pre1)
    feats_t = jnp.pad(feats.T, ((0, -feats.shape[1] % 8), (0, 0)))
    network = [feats_t, one.T, pre0, cos0, freq0, pre1, cos1, freq1, mid_all]

    def gather_parts(v):
        across = comm.turn(v, "seq", n_seq, 1)
        return [v, across, comm.flip(v, "seq", n_seq), comm.flip(across, "seq", n_seq)]

    leaving = []

    def scatter_parts(send, keep):
        got = comm.flip(send, "seq", n_seq)
        other = 1 - comm.y
        crossed = (pick(keep, other, 0) + pick(got, other, 0).astype(F32)).astype(BF)
        own = ((1, tok_rows, width), lambda i, m: (m[3], 0, 0))
        leaving.append(crossed)
        return (keep,) + own, (got,) + own, comm.turn(crossed, "seq", n_seq, 1)

    parts_out = [((2, tok_rows, width), BF), ((2, tok_rows, width), F32)]
    io_scratch = [((3 * chans, width), BF), ((chans, width), BF)]
    mlp_scratch = [((width, n_grp * f), BF), ((n_grp * f, width), BF)]
    state = tokens
    saved = []
    normed = hat0
    for l in range(depth):
        w_io, w_up, w_down = weights[l]
        parts = gather_parts(normed)
        if l == 0:
            low_parts = gather_parts(low_first)
            parts[0] = after(parts[0], *low_parts, chunks[1][0])
        else:
            parts[0] = after(parts[0], chunks[4][1], chunks[5][0])
        every, chan, inner, mixed, send, keep = run(
            lambda *r, n=len(w_io), raw=l == 0: mix_forth_kernel(count, n, raw, *r),
            [((total, width), BF), ((total, 3 * chans), BF), ((total, chans), F32), ((total, chans), BF)] + parts_out,
            meta,
            parts + w_io + [long, long_t, short, short_t, short0, second, decay, fout[l], rows5[l], skip[l],
                            gains[l, 0], shifts[l, 0]],
            io_scratch,
            flops=3 * 10**9,
        )
        got = scatter_parts(send, keep)
        if l == 0:
            state = after(state, chunks[1][1], chunks[2][0])
        mid, normed2 = run(
            add_norm_kernel, [((tok_rows, width), F32), ((tok_rows, width), BF)], meta,
            [state, *got, b_branch[l, 0], gains[l, 1], shifts[l, 1]],
        )
        parts = gather_parts(normed2)
        if l == 0:
            parts[0] = after(parts[0], chunks[2][1], chunks[3][0])
        every2, hidden, slope, send, keep = run(
            lambda *r, n=len(w_up), m=len(w_down): mlp_forth_kernel(n, m, *r),
            [((total, width), BF), ((total, n_grp * f), BF), ((total, n_grp * f), BF)] + parts_out,
            meta, parts + w_up + w_down + [b_up[l]], mlp_scratch,
            flops=4 * 10**9,
        )
        saved.append((state, every, chan, inner, mixed, mid, every2, hidden, slope))
        got = scatter_parts(send, keep)
        if l == 0:
            mid = after(mid, chunks[3][1], chunks[4][0])
        if l + 1 < depth:
            state, normed = run(
                add_norm_kernel, [((tok_rows, width), F32), ((tok_rows, width), BF)], meta,
                [mid, *got, b_branch[l, 1], gains[l + 1, 0], shifts[l + 1, 0]],
            )
        else:
            (state,) = run(add_kernel, [((tok_rows, width), F32)], meta, [mid, *got, b_branch[l, 1]])

    grad = cotangent
    toks = [None] * (2 * depth) + [sums_first]
    g_fouts, g_seconds, smalls, up_biases = ([None] * depth for _ in range(4))

    def hop(v, bit):
        return lax.ppermute(v, "grp", [(i, i ^ bit) for i in range(n_grp)])

    def owner_first(mine, got):
        rows = mine.shape[1:]
        keep, send = run(owner_sum_kernel, [((2,) + rows, F32), ((2,) + rows, BF)], meta, [mine, got])
        return keep, hop(send, 2)

    def owner_second(keep, got):
        return [keep, got, hop((keep[1] + got[1].astype(F32)).astype(BF), 4)]

    def owner_end(pieces):
        keep, got, crossed = pieces
        block = ((1,) + crossed.shape, lambda i, m: (0, 0, 0))
        return run(last_sum_kernel, [(crossed.shape, BF)], meta, [(keep,) + block, (got,) + block, crossed])[0]

    norm_outs = [((tok_rows, width), F32), ((tok_rows, width), BF), ((8, width), F32)]
    for l in reversed(range(depth)):
        w_io, w_up, w_down = weights[l]
        first, every, chan, inner, mixed, mid, every2, hidden, slope = saved[l]
        low, g_pre, up_biases[l], send, keep = run(
            lambda *r, n=len(w_up), m=len(w_down): mlp_back_kernel(n, m, *r),
            [((total, width), BF), ((total, n_grp * f), BF), ((1, n_grp * f), F32)] + parts_out,
            meta, low_parts + w_up + w_down + [slope], mlp_scratch,
            flops=4 * 10**9,
        )
        got = scatter_parts(send, keep)
        operands = [every2, g_pre, hidden, low]
        if l:
            (g_mlp,) = run(mlp_grads_kernel, [((n_grp, 2 * width, cols), BF)], meta, operands)
            grad = after(grad, g_mlp)
        else:
            mlp_send, mlp_mine = run(
                mlp_split_kernel, [((nz, 2 * width, cols), BF)] * 2, meta, operands)
            mlp_got = comm.flip(mlp_send, "grp", n_grp)
            grad = after(grad, mlp_send)
        grad, low_own, toks[2 * l + 1] = run(norm_back_kernel, norm_outs, meta, [grad, *got, mid, gains[l, 1]])
        low_parts = gather_parts(low_own)
        if l:
            mlp_unit = lax.psum_scatter(after(g_mlp, low_own), "grp", scatter_dimension=0, tiled=False)
        low, g_proj, g_fouts[l], g_seconds[l], smalls[l], send, keep = run(
            lambda *r, n=len(w_io): mix_back_kernel(count, n, *r),
            [((total, width), BF), ((total, 3 * chans), BF), ((lanes, chans), F32), ((half, lanes), F32),
             ((8, 3 * chans), F32)] + parts_out,
            meta,
            low_parts + w_io + [long, long_t, short, short_t, short0, short0_t, second, decay, fout[l], rows5[l],
                                skip[l], chan, inner],
            io_scratch,
            flops=5 * 10**9,
        )
        got = scatter_parts(send, keep)
        operands = [g_proj, every, mixed, low]
        scratch = [((3 * chans, width), BF), ((chans, width), BF)]
        if l:
            (g_io,) = run(lambda *r: io_grads_kernel(False, *r), [((n_grp, width, cols), BF)], meta, operands, scratch)
            grad = after(grad, g_io)
        else:
            io_send, io_mine = run(
                lambda *r: io_grads_kernel(True, *r), [((nz, width, cols), BF)] * 2, meta, operands, scratch)
            io_got = comm.flip(io_send, "grp", n_grp)
        grad, low_own, toks[2 * l] = run(norm_back_kernel, norm_outs, meta, [grad, *got, first, gains[l, 0]])
        if l:
            low_parts = gather_parts(low_own)
            io_one = lax.psum_scatter(after(g_io, low_own), "grp", scatter_dimension=0, tiled=False)

    def finish(kernel, parts, shapes, old, scratch=()):
        outs = []
        for shape in shapes:
            outs.append(((depth,) + shape, F32, (1,) + shape, lambda i, m, l=l, n=len(shape): (l,) + (0,) * n))
        return run(
            lambda *r, n=len(old): kernel(n, *r), outs, meta, parts + [(v, None, None) for v in old],
            scratch, alias={5: 0, 6: 1} if old else None)

    mlp_shapes = [(width, ff_shard), (n_grp, n_seq, f, cols)]
    io_shapes = [(width, 3 * cols), (n_grp, n_seq, q, cols)]
    turned = [((3 * cols, width), F32)]

    send, mine = run(
        lambda *r: pack_kernel(depth, *r), [((nz, SMALL + NET, cols), BF)] * 2, meta,
        up_biases + smalls + g_fouts + toks + g_seconds + network + [e_wide, e_all],
        [((5, 2 * SLOT, 3 * chans), F32), ((SMALL, width), F32)])
    mlp_first = owner_first(mlp_mine, after(mlp_got, io_send, low_own))
    io_first = owner_first(io_mine, after(io_got, mlp_first[0], send))
    parts_one = gather_parts(after(mlp_unit, low_own))
    small_got = after(comm.flip(send, "grp", n_grp), parts_one[1])
    small_rows = (SMALL + NET, cols)
    own, *sends = run(small_turn_kernel, [(small_rows, BF)] * nz, meta, [mine, small_got])
    pieces = [own] + [comm.turn(v, "grp", n_grp, k) for k, v in enumerate(sends, 1)]
    mlp_pieces = owner_second(after(mlp_first[0], *pieces[1:]), mlp_first[1])
    io_turn = owner_second(*io_first)
    (small,) = run(small_last_kernel, [(small_rows, BF)], meta, pieces, [((nz,) + small_rows, F32)])
    small_parts = gather_parts(small)

    l = 1
    mlp_grads = finish(finish_mlp_kernel, parts_one, mlp_shapes, [])
    mlp_pieces[0], state, *mlp_grads = lax.optimization_barrier(
        (after(mlp_pieces[0], io_first[1], *small_parts), state, *mlp_grads))
    io_grads = finish(finish_io_kernel, gather_parts(after(io_one, *small_parts)), io_shapes, [], turned)
    io_turn[0], *io_grads = lax.optimization_barrier((io_turn[0], *io_grads))
    l = 0
    mlp_unit = owner_end(mlp_pieces)
    up_grad, down_grad = finish(finish_mlp_kernel, gather_parts(mlp_unit), mlp_shapes, mlp_grads)
    in_grad, out_grad = finish(finish_io_kernel, gather_parts(owner_end(io_turn)), io_shapes, io_grads, turned)
    shared_shapes = [v.shape for v in (filt_in, filt_mid, filt_bias, sine_freq)]
    (norm_gain_grad, norm_bias_grad, branch_grad, in_bias_grad, taps_grad, tap_bias_grad, skip_grad, fout_grad,
     up_bias_grad, *shared) = run(
        lambda *r: finish_small_kernel(q, *r),
        [(v.shape, F32) for v in (norm_gain, norm_bias, branch_bias, in_bias, conv_weight, conv_bias, skip_bias,
                                  filt_out, up_bias)] + [(shape, F32) for shape in shared_shapes],
        meta, small_parts, [((n_seq,) + small_rows, F32)])
    return (
        state, grad, norm_gain_grad, norm_bias_grad, in_grad, in_bias_grad, taps_grad, tap_bias_grad,
        skip_grad, fout_grad, out_grad.reshape(depth, width, cols), up_grad, up_bias_grad,
        down_grad.reshape(depth, n_grp * ff_shard, cols), branch_grad, shared[0], shared[1], shared[2], shared[3],
    )


def solution(mesh):
    tok = P(("grp", "seq"), None)
    last3, last2 = P(None, None, "grp"), P(None, "grp")
    in_specs = (
        tok, P("grp", None), tok, last3, last3, last3, last2, last3, last2, last2,
        last3, last3, last3, last2, last3, last3, P(), P(), P(), P(),
    )
    out_specs = (
        tok, tok, last3, last3, last3, last2, last3, last2, last2, last3,
        last3, last3, last2, last3, last3, P(), P(), P(), P(),
    )
    small = mesh.shape["seq"] == 4 and mesh.shape["grp"] == 8
    return jax.shard_map(body if small else body_any, mesh=mesh, in_specs=in_specs, out_specs=out_specs, check_vma=False)
```

```python
import math

import jax
import jax.numpy as jnp
from jax import lax
from jax.experimental import pallas as pl
from jax.experimental.pallas import tpu as pltpu
from jax.sharding import PartitionSpec as P

EPS = 1e-05
HIGH = lax.Precision.HIGHEST
FAST = math.log(0.01) / 0.3
SLOW = math.log(0.01) / 1.5
F32 = jnp.float32
BF = jnp.bfloat16
INV_SQRT2 = 1.0 / math.sqrt(2.0)
INV_SQRT2PI = 1.0 / math.sqrt(2.0 * math.pi)


def dot(a, b, da, db):
    return lax.dot_general(a, b, (((da,), (db,)), ((), ())), preferred_element_type=F32)


def pick(v, index, axis):
    return lax.dynamic_index_in_dim(v, index, axis, keepdims=False)


class Comm:
    def __init__(self):
        self.n_grp = lax.axis_size("grp")
        self.n_seq = lax.axis_size("seq")
        self.nz = self.n_grp // 2
        self.ny = self.n_seq // 2
        g = lax.axis_index("grp")
        s = lax.axis_index("seq")
        self.g, self.s = g, s
        self.z, self.x = g // 2, g % 2
        self.y, self.c = s // 2, s % 2

    @staticmethod
    def flip(v, axis, size):
        return lax.ppermute(v, axis, [(i, i ^ 1) for i in range(size)])

    @staticmethod
    def turn(v, axis, size, k):
        half = size // 2
        perm = [(2 * i + j, 2 * ((i + k) % half) + j) for i in range(half) for j in range(2)]
        return lax.ppermute(v, axis, perm)

    def _gather(self, v, axis, size, major, minor):
        half = size // 2
        if half > 4:
            return lax.all_gather(v, axis, axis=0, tiled=False)
        parts = [v] + [self.turn(v, axis, size, k) for k in range(1, half)]
        others = [self.flip(p, axis, size) for p in parts]
        if half == 2:
            zero = major == 0
            mine = jnp.stack([jnp.where(zero, parts[0], parts[1]), jnp.where(zero, parts[1], parts[0])])
            them = jnp.stack([jnp.where(zero, others[0], others[1]), jnp.where(zero, others[1], others[0])])
        else:
            order = jnp.mod(major - jnp.arange(half), half)
            mine = jnp.stack([pick(jnp.stack(parts), order[i], 0) for i in range(half)])
            them = jnp.stack([pick(jnp.stack(others), order[i], 0) for i in range(half)])
        first = jnp.where(minor == 0, mine, them)
        second = jnp.where(minor == 0, them, mine)
        return jnp.stack([first, second], axis=1).reshape((size,) + v.shape)

    def gather_seq(self, v):
        return self._gather(v, "seq", self.n_seq, self.y, self.c)

    def gather_grp(self, v):
        half = self.nz
        slab = jnp.zeros((half,) + v.shape, v.dtype)
        zeros = (0,) * v.ndim
        for k in range(half):
            part = v if k == 0 else self.turn(v, "grp", self.n_grp, k)
            slab = lax.dynamic_update_slice(slab, part[None], (jnp.mod(self.z - k, half),) + zeros)
        other = self.flip(slab, "grp", self.n_grp)
        first = jnp.where(self.x == 0, slab, other)
        second = jnp.where(self.x == 0, other, slab)
        return jnp.stack([first, second], axis=1).reshape((self.n_grp,) + v.shape)

    def _scatter(self, v, axis, size, major, minor, kind):
        half = size // 2
        if half > 4:
            return lax.psum_scatter(v.astype(kind), axis, scatter_dimension=0, tiled=False).astype(F32)
        v = v.reshape((half, 2) + v.shape[1:])
        got = self.flip(pick(v, 1 - minor, 1).astype(kind), axis, size)
        mine = pick(v, minor, 1).astype(F32) + got.astype(F32)
        total = pick(mine, major, 0)
        for k in range(1, half):
            sent = pick(mine, jnp.mod(major + k, half), 0).astype(kind)
            total = total + self.turn(sent, axis, size, k).astype(F32)
        return total

    def scatter_seq(self, v, kind=BF):
        return self._scatter(v, "seq", self.n_seq, self.y, self.c, kind)

    def scatter_grp(self, v, kind=BF):
        return self._scatter(v, "grp", self.n_grp, self.z, self.x, kind)

    def sum_all(self, v, axis, size):
        half = size // 2
        if half > 4:
            return lax.psum(v, axis)
        v = v + self.flip(v, axis, size)
        total = v
        for k in range(1, half):
            total = total + self.turn(v, axis, size, k)
        return total


def norm_stats(value):
    center = value - jnp.mean(value, axis=-1, keepdims=True)
    scale = lax.rsqrt(jnp.mean(center * center, axis=-1, keepdims=True) + EPS)
    return center * scale, scale


def norm_back(grad, hat, scale, gain):
    inner = grad * gain
    mean_one = jnp.mean(inner, axis=-1, keepdims=True)
    mean_two = jnp.mean(inner * hat, axis=-1, keepdims=True)
    return scale * (inner - mean_one - hat * mean_two), jnp.sum(grad * hat, axis=0), jnp.sum(grad, axis=0)


def positions(length):
    index = jnp.arange(length, dtype=jnp.int32).astype(F32)
    tpos = index / (length - 1)
    bands = 0.0001 + (15.0 - 0.0001) * jnp.arange(16, dtype=jnp.int32).astype(F32) / 15.0
    angle = 2.0 * math.pi / length * index[:, None] * bands[None, :]
    return (jnp.concatenate([tpos[:, None], jnp.cos(angle), -jnp.sin(angle)], axis=1), tpos)


def odd_table(size, place):
    freq = 2 * jnp.arange(size // 2, dtype=jnp.int32) + 1
    turn = jnp.bitwise_and(freq[:, None] * place[None, :], 2 * size - 1)
    angle = turn.astype(F32) * (math.pi / size)
    return jnp.stack([jnp.cos(angle), -jnp.sin(angle)])


def filter_of(fin, fmid, fbias, freq, fout, feats, decay):
    inner = jnp.sin(freq[0] * (jnp.dot(feats, fin, precision=HIGH) + fbias[0]))
    inner = jnp.sin(freq[1] * (jnp.dot(inner, fmid, precision=HIGH) + fbias[1]))
    return jnp.dot(inner, fout, precision=HIGH) * decay


def lagged(v, lag, mask):
    return jnp.where(mask[None, :, None], jnp.pad(v, ((0, 0), (lag, 0), (0, 0)))[:, : v.shape[1]], 0.0)


def ahead(v, lag):
    return jnp.pad(v, ((0, 0), (0, lag), (0, 0)))[:, lag:]


def times(ar, ai, br, bi):
    return ar * br - ai * bi, ar * bi + ai * br


def times_conj(ar, ai, br, bi):
    return ar * br + ai * bi, ai * br - ar * bi


class Mixer:
    def __init__(self, lens, total, most):
        half = total // 2
        self.half, self.most, self.total, self.count = half, most, total, lens.shape[0]
        starts = half + jnp.cumsum(lens) - lens
        place = jnp.arange(total, dtype=jnp.int32)
        begin = jnp.zeros((total,), jnp.int32)
        for k in range(lens.shape[0]):
            begin = jnp.where(starts[k] <= place, starts[k], begin)
        self.masks = [None] + [place - lag >= begin for lag in (1, 2)]
        self.long = odd_table(2 * half, place[:half]).reshape(2 * half, half).astype(BF)
        self.short0 = odd_table(2 * most, place[:most]).reshape(2 * most, most).astype(BF)
        tail = place[half:]
        tables = []
        for k in range(lens.shape[0]):
            rel = tail - starts[k]
            inside = (rel >= 0) & (rel < lens[k])
            table = odd_table(2 * most, jnp.where(inside, rel, 0))
            tables.append(jnp.where(inside[None, None, :], table, 0.0))
        self.short = jnp.stack(tables).reshape(lens.shape[0] * 2 * most, total - half).astype(BF)

    def split(self, long, short):
        chans = long.shape[-1]
        long = long.reshape(2, self.half, chans)
        short = short.reshape(self.count, 2, self.most, chans)
        return long[0], long[1], short[:, 0], short[:, 1]

    def forth(self, v):
        v = v.astype(BF)
        return self.split(dot(self.long, v[: self.half], 1, 0), dot(self.short, v[self.half :], 1, 0))

    def back(self, spec):
        lr, li, sr, si = spec
        long = jnp.stack([lr, li]).reshape(2 * self.half, -1) * (1.0 / self.half)
        short = jnp.stack([sr, si], axis=1).reshape(self.count * 2 * self.most, -1) * (1.0 / self.most)
        return jnp.concatenate([dot(self.long, long.astype(BF), 0, 0), dot(self.short, short.astype(BF), 0, 0)])

    def filt_spec(self, filt):
        filt = filt.astype(BF)
        long = dot(self.long, filt, 1, 0)
        short = dot(self.short0, filt[: self.most], 1, 0)
        return long[: self.half], long[self.half :], short[: self.most], short[self.most :]

    def filt_back(self, grads):
        lr, li, sr, si = grads
        long = jnp.concatenate([lr, li]) * (1.0 / self.half)
        short = jnp.concatenate([sr, si]) * (1.0 / self.most)
        head = dot(self.short0, short.astype(BF), 0, 0)
        return dot(self.long, long.astype(BF), 0, 0) + jnp.pad(head, ((0, self.half - self.most), (0, 0)))


def body_any(
    tokens,
    lengths,
    cotangent,
    norm_gain,
    norm_bias,
    in_weight,
    in_bias,
    conv_weight,
    conv_bias,
    skip_bias,
    filt_out,
    out_weight,
    up_weight,
    up_bias,
    down_weight,
    branch_bias,
    filt_in,
    filt_mid,
    filt_bias,
    sine_freq,
):
    comm = Comm()
    n_grp, n_seq, s = comm.n_grp, comm.n_seq, comm.s
    depth = norm_gain.shape[0]
    tok_rows, width = tokens.shape
    total = tok_rows * n_seq
    cols = width // n_grp
    q = cols // n_seq
    ff_shard = up_weight.shape[2]
    f = ff_shard // n_seq
    hid = filt_out.shape[1]
    chans = n_grp * q

    def unit_in(l):
        return pick(in_weight[l].T.reshape(3, n_seq, q, width), s, 1).reshape(3 * q, width)

    def unit_out(l):
        return pick(out_weight[l].reshape(n_grp, n_seq, q, cols), s, 1).reshape(chans, cols).T

    def unit_up(l):
        return lax.dynamic_slice_in_dim(up_weight[l], s * f, f, 1).T

    def unit_down(l):
        return pick(down_weight[l].reshape(n_grp, n_seq, f, cols), s, 1).reshape(n_grp * f, cols).T

    tok_small = [norm_gain, norm_bias, branch_bias]
    seq_small = [
        pick(in_bias.reshape(depth, 3, n_seq, q), s, 2),
        pick(conv_weight.reshape(depth, 3, 3, n_seq, q), s, 3),
        pick(conv_bias.reshape(depth, 3, n_seq, q), s, 2),
        pick(skip_bias.reshape(depth, n_seq, q), s, 1),
        pick(filt_out.reshape(depth, hid, n_seq, q), s, 2),
        pick(up_bias.reshape(depth, n_seq, f), s, 1),
    ]
    shapes = [v.shape for v in tok_small + seq_small]
    sizes = [math.prod(shape) for shape in shapes]
    packed = jnp.concatenate([v.reshape(-1) for v in tok_small + seq_small])
    fill = -packed.shape[0] % 2048
    packed = comm.gather_grp(jnp.pad(packed, (0, fill)).reshape(-1, 128)).reshape(n_grp, -1).astype(F32)
    spread, at = [], 0
    for shape, size in zip(shapes, sizes):
        spread.append(packed[:, at : at + size].reshape((n_grp,) + shape))
        at += size

    def last(v):
        return jnp.moveaxis(v, 0, -2).reshape(v.shape[1:-1] + (n_grp * v.shape[-1],))

    def streams(v):
        v = jnp.moveaxis(v, 0, -3)
        return v.reshape(v.shape[:-3] + (3, n_grp * q))

    gains, shifts, b_branch = (last(v) for v in spread[:3])
    b_in, taps, tap_bias = (streams(v) for v in spread[3:6])
    skip, fout, b_up = (last(v) for v in spread[6:9])

    weights = []
    for l in range(depth):
        w_in = comm.gather_grp(unit_in(l)).reshape(3 * chans, width)
        w_out = comm.gather_grp(unit_out(l)).reshape(width, chans)
        w_up = comm.gather_grp(unit_up(l)).reshape(n_grp * f, width)
        w_down = comm.gather_grp(unit_down(l)).reshape(width, n_grp * f)
        weights.append((w_in, w_out, w_up, w_down))

    lens = lengths[0]
    mixer = Mixer(lens, total, total // 4)
    feats, tpos = positions(total // 2)
    channel = (
        jnp.arange(n_grp, dtype=jnp.int32)[:, None] * cols + s * q + jnp.arange(q, dtype=jnp.int32)[None, :]
    ).reshape(-1).astype(F32)
    rate = jnp.abs(FAST + (SLOW - FAST) * channel / (width - 1))
    decay = jnp.exp(-tpos[:, None] * rate[None, :])

    state = tokens.astype(F32)
    saved = []
    for l in range(depth):
        w_in, w_out, w_up, w_down = weights[l]
        filt, filt_pull = jax.vjp(
            lambda *a: filter_of(*a, feats, decay),
            filt_in[l], filt_mid[l], filt_bias[l], sine_freq[l], fout[l],
        )
        hat1, scale1 = norm_stats(state)
        normed = (hat1 * gains[l, 0] + shifts[l, 0]).astype(BF)
        normed = comm.gather_seq(normed).reshape(total, width)
        proj = dot(normed, w_in, 1, 1) + b_in[l].reshape(-1)
        proj = jnp.transpose(proj.astype(BF).reshape(total, 3, chans), (1, 0, 2))
        chan = proj.astype(F32)
        z = tap_bias[l][:, None, :] + taps[l, 0][:, None, :] * chan
        for lag in (1, 2):
            z = z + taps[l, lag][:, None, :] * lagged(chan, lag, mixer.masks[lag])
        prod = z[1] * z[2]
        h_lr, h_li, h_sr, h_si = mixer.filt_spec(filt)
        x_lr, x_li, x_sr, x_si = mixer.forth(prod)
        conv = mixer.back(times(x_lr, x_li, h_lr, h_li) + times(x_sr, x_si, h_sr, h_si))
        inner = conv + skip[l] * prod
        mixed = (z[0] * inner).astype(BF)
        part = dot(mixed, w_out, 1, 1)
        mid = state + comm.scatter_seq(part.reshape(n_seq, tok_rows, width)) + b_branch[l, 0]
        hat2, scale2 = norm_stats(mid)
        normed2 = (hat2 * gains[l, 1] + shifts[l, 1]).astype(BF)
        normed2 = comm.gather_seq(normed2).reshape(total, width)
        pre = dot(normed2, w_up, 1, 1) + b_up[l]
        cdf = 0.5 * (1.0 + lax.erf(pre * INV_SQRT2))
        hidden = (pre * cdf).astype(BF)
        slope = cdf + pre * (jnp.exp(-0.5 * pre * pre) * INV_SQRT2PI)
        part = dot(hidden, w_down, 1, 1)
        state = mid + comm.scatter_seq(part.reshape(n_seq, tok_rows, width)) + b_branch[l, 1]
        saved.append((filt_pull, hat1, scale1, normed, chan, z, prod, inner, (h_lr, h_li, h_sr, h_si),
                      (x_lr, x_li, x_sr, x_si), mixed, hat2, scale2, normed2, slope, hidden))

    grad = cotangent
    units = [None] * depth
    tok_grads, seq_grads, net_grads = [None] * depth, [None] * depth, [None] * depth

    def chunk(v):
        return comm.scatter_grp(v.astype(BF).reshape((n_grp, v.shape[0] // n_grp) + v.shape[1:])).astype(BF)

    for l in reversed(range(depth)):
        w_in, w_out, w_up, w_down = weights[l]
        (filt_pull, hat1, scale1, normed, chan, z, prod, inner, (h_lr, h_li, h_sr, h_si),
         (x_lr, x_li, x_sr, x_si), mixed, hat2, scale2, normed2, slope, hidden) = saved[l]
        low = grad.astype(BF)
        g_two = jnp.sum(low.astype(F32), axis=0)
        low = comm.gather_seq(low).reshape(total, width)
        u_down = chunk(dot(low, hidden, 0, 0))
        g_pre = (dot(low, w_down, 1, 0) * slope).astype(BF)
        g_up_bias = jnp.sum(g_pre.astype(F32), axis=0)
        part = dot(g_pre, w_up, 1, 0)
        u_up = chunk(dot(g_pre, normed2, 0, 0))
        g_normed2 = comm.scatter_seq(part.reshape(n_seq, tok_rows, width))
        g_mid, gain2, shift2 = norm_back(g_normed2, hat2, scale2, gains[l, 1])
        g_mid = g_mid + grad
        low = g_mid.astype(BF)
        g_one = jnp.sum(low.astype(F32), axis=0)
        low = comm.gather_seq(low).reshape(total, width)
        u_out = chunk(dot(low, mixed, 0, 0))
        g_y = dot(low, w_out, 1, 0).astype(BF).astype(F32)
        g_conv = g_y * z[0]
        g_skip = jnp.sum(g_conv * prod, axis=0)
        y_lr, y_li, y_sr, y_si = mixer.forth(g_conv)
        corr = mixer.back(times_conj(y_lr, y_li, h_lr, h_li) + times_conj(y_sr, y_si, h_sr, h_si))
        f_lr, f_li = times_conj(y_lr, y_li, x_lr, x_li)
        f_sr, f_si = times_conj(y_sr, y_si, x_sr, x_si)
        g_filt = mixer.filt_back((f_lr, f_li, jnp.sum(f_sr, axis=0), jnp.sum(f_si, axis=0)))
        g_prod = corr + skip[l] * g_conv
        g_z = jnp.stack([g_y * inner, g_prod * z[2], g_prod * z[1]])
        g_taps = [jnp.sum(g_z * chan, axis=1)]
        g_proj = taps[l, 0][:, None, :] * g_z
        for lag in (1, 2):
            kept = jnp.where(mixer.masks[lag][None, :, None], g_z, 0.0)
            g_taps.append(jnp.sum(g_z * lagged(chan, lag, mixer.masks[lag]), axis=1))
            g_proj = g_proj + taps[l, lag][:, None, :] * ahead(kept, lag)
        g_proj = jnp.transpose(g_proj.astype(BF), (1, 0, 2)).reshape(total, 3 * chans)
        g_in_bias = jnp.sum(g_proj.astype(F32), axis=0).reshape(3, chans)
        part = dot(g_proj, w_in, 1, 0)
        u_in = chunk(dot(g_proj, normed, 0, 0))
        g_normed = comm.scatter_seq(part.reshape(n_seq, tok_rows, width))
        g_state, gain1, shift1 = norm_back(g_normed, hat1, scale1, gains[l, 0])
        grad = g_mid + g_state
        units[l] = (u_in, u_out, u_up, u_down)
        pulled = filt_pull(g_filt)
        net_grads[l] = pulled[:4]
        tok_grads[l] = (jnp.stack([gain1, gain2]), jnp.stack([shift1, shift2]), jnp.stack([g_one, g_two]))
        seq_grads[l] = (g_in_bias, jnp.stack(g_taps), jnp.sum(g_z, axis=1), g_skip, pulled[4], g_up_bias)

    def whole(place):
        return [comm.gather_seq(units[l][place]).astype(F32) for l in range(depth)]

    in_grad = jnp.stack([
        jnp.transpose(v.reshape(n_seq, 3, q, width), (3, 1, 0, 2)).reshape(width, 3 * cols) for v in whole(0)])
    out_grad = jnp.stack([
        jnp.transpose(v.reshape(n_seq, cols, n_grp, q), (2, 0, 3, 1)).reshape(width, cols) for v in whole(1)])
    up_grad = jnp.stack([jnp.transpose(v, (2, 0, 1)).reshape(width, ff_shard) for v in whole(2)])
    down_grad = jnp.stack([
        jnp.transpose(v.reshape(n_seq, cols, n_grp, f), (2, 0, 3, 1)).reshape(n_grp * ff_shard, cols)
        for v in whole(3)])

    def by_owner(v):
        v = v.reshape(v.shape[:-1] + (n_grp, v.shape[-1] // n_grp))
        return jnp.moveaxis(v, -2, 0).reshape(n_grp, -1)

    def by_owner3(v):
        v = v.reshape(v.shape[:-2] + (n_grp, 3, q))
        return jnp.moveaxis(v, -3, 0).reshape(n_grp, -1)

    tok_all = [jnp.stack(v) for v in zip(*tok_grads)]
    seq_all = [jnp.stack(v) for v in zip(*seq_grads)]
    tok_flat = jnp.concatenate([by_owner(v) for v in tok_all], axis=1)
    seq_flat = jnp.concatenate(
        [by_owner3(v) for v in seq_all[:3]] + [by_owner(v) for v in seq_all[3:]], axis=1)
    tok_len, seq_len = tok_flat.shape[1], seq_flat.shape[1]
    flat = jnp.concatenate([tok_flat, seq_flat], axis=1)
    flat = jnp.pad(flat, ((0, 0), (0, -flat.shape[1] % 1024)))
    small = comm.scatter_grp(flat.reshape(n_grp, -1, 128), F32).reshape(-1)
    tok_sum = comm.sum_all(small[:tok_len].reshape(-1, 128), "seq", n_seq).reshape(-1)
    seq_part = jnp.pad(small[tok_len : tok_len + seq_len], (0, -seq_len % 1024)).reshape(-1, 128)
    seq_sum = comm.gather_seq(seq_part).reshape(n_seq, -1)[:, :seq_len]
    norm_gain_grad, norm_bias_grad, branch_grad = tok_sum.reshape(3, depth, 2, cols)
    pieces, at = [], 0
    for shape in shapes[3:]:
        size = math.prod(shape)
        part = seq_sum[:, at : at + size].reshape((n_seq,) + shape)
        at += size
        part = jnp.moveaxis(part, 0, -2)
        pieces.append(part)
    in_bias_grad = pieces[0].reshape(depth, 3 * cols)
    taps_grad = pieces[1].reshape(depth, 3, 3 * cols)
    tap_bias_grad = pieces[2].reshape(depth, 3 * cols)
    skip_grad = pieces[3].reshape(depth, cols)
    fout_grad = pieces[4].reshape(depth, hid, cols)
    up_bias_grad = pieces[5].reshape(depth, ff_shard)

    nets = [jnp.stack(v) for v in zip(*net_grads)]
    flat = jnp.concatenate([v.reshape(-1) for v in nets])
    flat = jnp.pad(flat, (0, -flat.shape[0] % 1024)).reshape(-1, 128)
    flat = comm.sum_all(comm.sum_all(flat, "seq", n_seq), "grp", n_grp).reshape(-1)
    shared, at = [], 0
    for v in nets:
        shared.append(flat[at : at + v.size].reshape(v.shape))
        at += v.size
    return (
        state, grad, norm_gain_grad, norm_bias_grad, in_grad, in_bias_grad, taps_grad, tap_bias_grad,
        skip_grad, fout_grad, out_grad, up_grad, up_bias_grad, down_grad, branch_grad,
        shared[0], shared[1], shared[2], shared[3],
    )


ORDER = (0, 2, 1, 3)
VMEM_BYTES = 56 * 2**20
SMALL = 64
SLOT = 24
COST = 1000
UP_AT = 48
TOK = 52
NET = 112


def run(kernel, outs, meta, args, scratch=(), flops=0, alias=None):
    specs, arrays = [], []
    for a in args:
        if isinstance(a, tuple):
            array, block, place = a
            if block is None:
                specs.append(pl.BlockSpec(memory_space=pl.ANY))
            else:
                specs.append(pl.BlockSpec(block, place, pipeline_mode=pl.Buffered(1)))
            arrays.append(array)
        else:
            specs.append(pl.BlockSpec(memory_space=pltpu.VMEM))
            arrays.append(a)
    out_specs, shapes = [], []
    for o in outs:
        shapes.append(jax.ShapeDtypeStruct(o[0], o[1]))
        if len(o) > 2:
            out_specs.append(pl.BlockSpec(o[2], o[3], pipeline_mode=pl.Buffered(1)))
        else:
            out_specs.append(pl.BlockSpec(memory_space=pltpu.VMEM))
    moved = sum(o.size * o.dtype.itemsize for o in shapes) + sum(a.size * a.dtype.itemsize for a in arrays)
    return pl.pallas_call(
        kernel,
        out_shape=shapes,
        grid_spec=pltpu.PrefetchScalarGridSpec(
            num_scalar_prefetch=1,
            grid=(1,),
            in_specs=specs,
            out_specs=out_specs,
            scratch_shapes=[pltpu.VMEM(shape, kind) for shape, kind in scratch],
        ),
        input_output_aliases=alias or {},
        compiler_params=pltpu.CompilerParams(vmem_limit_bytes=VMEM_BYTES),
        cost_estimate=pl.CostEstimate(flops=flops // COST, bytes_accessed=moved // COST, transcendentals=0),
    )(meta, *arrays)


def join(meta, parts, all_ref):
    rows = parts[0].shape[0]
    for k, part in enumerate(parts):
        at = pl.multiple_of((meta[0] ^ ORDER[k]) * rows, rows)
        all_ref[pl.ds(at, rows), :] = part[...]


def owners(meta, refs):
    if len(refs) == 1:
        return [(g, refs[0].at[g]) for g in range(refs[0].shape[0])]
    half = refs[0].shape[0]
    found = []
    for k in range(half):
        at = 2 * lax.rem(meta[1] - k + half, half)
        found.append((at + meta[2], refs[0].at[k]))
        found.append((at + 1 - meta[2], refs[1].at[k]))
    return found


def span(g, size):
    if isinstance(g, int):
        return pl.ds(g * size, size)
    return pl.ds(pl.multiple_of(g * size, size), size)


def place_wide(meta, refs, wide):
    rows = wide.shape[0]
    for g, block in owners(meta, refs):
        wide[:, span(g, block.shape[-1])] = block[:rows, :]


def place_io(meta, refs, wi, wo):
    n_grp = wi.shape[1] // 128
    part = wi.shape[0] // n_grp
    q = part // 3
    for g, block in owners(meta, refs):
        for lb in range(n_grp):
            at = lb * 4 * q
            wi[span(g, part), lb * 128 : (lb + 1) * 128] = block[at : at + part, :]
            wo[lb * q : (lb + 1) * q, span(g, 128)] = block[at + part : at + part + q, :]


def part_out(meta, value, at, send, keep):
    rows = value.shape[0] // 4
    w = value.shape[1]
    even = jnp.stack([value[:rows], value[2 * rows : 3 * rows]])
    odd = jnp.stack([value[rows : 2 * rows], value[3 * rows :]])
    low = meta[4] == 0
    keep[:, :, at : at + w] = jnp.where(low, even, odd)
    send[:, :, at : at + w] = jnp.where(low, odd, even).astype(BF)


def masks_of(meta, total, wide, count):
    place = lax.broadcasted_iota(jnp.int32, (total, wide), 0)
    begin = jnp.zeros((total, wide), jnp.int32)
    for k in range(count):
        begin = jnp.where(place >= meta[5 + k], meta[5 + k], begin)
    return place, [None] + [place - lag >= begin for lag in (1, 2)]


def roll_down(v, lag):
    return pltpu.roll(v, lag, 0)


def stream_z(chan, j, wide, rows5, masks):
    at = j * wide
    v = chan[:, at : at + wide].astype(F32)
    z = rows5[4:5, at : at + wide] + rows5[1:2, at : at + wide] * v
    for lag in (1, 2):
        z = z + rows5[1 + lag : 2 + lag, at : at + wide] * jnp.where(masks[lag], roll_down(v, lag), 0.0)
    return z


def spectra(v, long, short):
    half = v.shape[0] // 2
    low = v.astype(BF)
    return dot(long[...], low[:half], 1, 0), dot(short[...], low[half:], 1, 0)


def filt_spectra(filt, long, short0):
    low = filt.astype(BF)
    return dot(long[...], low, 1, 0), dot(short0[...], low[: short0.shape[1]], 1, 0)


def each(long, short, count):
    half = long.shape[0] // 2
    most = short.shape[0] // count // 2
    pairs = [(long[:half], long[half:])]
    for k in range(count):
        pairs.append((short[2 * k * most : (2 * k + 1) * most], short[(2 * k + 1) * most : (2 * k + 2) * most]))
    return pairs


def unspectra(pairs, long_t, short_t):
    half, most = pairs[0][0].shape[0], pairs[1][0].shape[0]
    long = (jnp.concatenate(pairs[0]) * (1.0 / half)).astype(BF)
    short = (jnp.concatenate([v for pair in pairs[1:] for v in pair]) * (1.0 / most)).astype(BF)
    return jnp.concatenate([dot(long_t[...], long, 1, 0), dot(short_t[...], short, 1, 0)])


def exact(a, b, da, db):
    return lax.dot_general(a, b, (((da,), (db,)), ((), ())), precision=HIGH, preferred_element_type=F32)


def mix_forth_kernel(count, nio, raw, meta, *refs):
    parts, refs = refs[:4], refs[4:]
    io, refs = refs[:nio], refs[nio:]
    (long, long_t, short, short_t, short0, second, decay, fout, rows5, skip, gain, shift,
     every, chan, inner_ref, mixed_ref, send, keep, wi, wo) = refs
    join(meta, parts, every)
    if raw:
        every[...] = (every[...].astype(F32) * gain[...] + shift[...]).astype(BF)
    place_io(meta, io, wi, wo)
    total, wide = mixed_ref.shape
    _, masks = masks_of(meta, total, wide, count)
    z = []
    for j in range(3):
        at = j * wide
        proj = dot(every[...], wi[at : at + wide, :], 1, 1) + rows5[0:1, at : at + wide]
        chan[:, at : at + wide] = proj.astype(BF)
        z.append(stream_z(chan, j, wide, rows5, masks))
    prod = z[1] * z[2]
    filt = exact(second[...], fout[...], 1, 0) * decay[...]
    hs = each(*filt_spectra(filt, long, short0), 1)
    xs = each(*spectra(prod, long, short), count)
    ys = [times(*x, *hs[min(k, 1)]) for k, x in enumerate(xs)]
    inner = unspectra(ys, long_t, short_t) + skip[...] * prod
    inner_ref[...] = inner
    mixed_ref[...] = (z[0] * inner).astype(BF)
    for n in range(4):
        w = wo.shape[1] // 4
        part_out(meta, dot(mixed_ref[...], wo[:, n * w : (n + 1) * w], 1, 0), n * w, send, keep)


def mix_back_kernel(count, nio, meta, *refs):
    parts, refs = refs[:4], refs[4:]
    io, refs = refs[:nio], refs[nio:]
    (long, long_t, short, short_t, short0, short0_t, second, decay, fout, rows5, skip, chan, inner,
     every, g_proj_ref, g_fout, g_second, small, send, keep, wi, wo) = refs
    join(meta, parts, every)
    place_io(meta, io, wi, wo)
    total, wide = inner.shape
    place, masks = masks_of(meta, total, wide, count)
    z = [stream_z(chan, j, wide, rows5, masks) for j in range(3)]
    prod = z[1] * z[2]
    filt = exact(second[...], fout[...], 1, 0) * decay[...]
    hs = each(*filt_spectra(filt, long, short0), 1)
    xs = each(*spectra(prod, long, short), count)
    g_y = dot(every[...], wo[...], 1, 1).astype(BF).astype(F32)
    g_conv = g_y * z[0]
    ys = each(*spectra(g_conv, long, short), count)
    corr = unspectra([times_conj(*y, *hs[min(k, 1)]) for k, y in enumerate(ys)], long_t, short_t)
    g_prod = corr + skip[...] * g_conv
    small[...] = jnp.zeros_like(small)
    small[5:6, :wide] = jnp.sum(g_conv * prod, axis=0, keepdims=True)
    for j, g_z in enumerate((g_y * inner[...], g_prod * z[2], g_prod * z[1])):
        at = j * wide
        v = chan[:, at : at + wide].astype(F32)
        small[4:5, at : at + wide] = jnp.sum(g_z, axis=0, keepdims=True)
        small[1:2, at : at + wide] = jnp.sum(g_z * v, axis=0, keepdims=True)
        g_proj = rows5[1:2, at : at + wide] * g_z
        for lag in (1, 2):
            kept = jnp.where(masks[lag], g_z, 0.0)
            small[1 + lag : 2 + lag, at : at + wide] = jnp.sum(kept * roll_down(v, lag), axis=0, keepdims=True)
            moved = jnp.where(place < total - lag, roll_down(kept, total - lag), 0.0)
            g_proj = g_proj + rows5[1 + lag : 2 + lag, at : at + wide] * moved
        low = g_proj.astype(BF)
        g_proj_ref[:, at : at + wide] = low
        small[0:1, at : at + wide] = jnp.sum(low.astype(F32), axis=0, keepdims=True)
    for n in range(4):
        w = wi.shape[1] // 4
        part_out(meta, dot(g_proj_ref[...], wi[:, n * w : (n + 1) * w], 1, 0), n * w, send, keep)
    fs = [times_conj(*y, *x) for y, x in zip(ys, xs)]
    f_short = fs[1]
    for pair in fs[2:]:
        f_short = (f_short[0] + pair[0], f_short[1] + pair[1])
    half, most = fs[0][0].shape[0], f_short[0].shape[0]
    g_filt = dot(long_t[...], (jnp.concatenate(fs[0]) * (1.0 / half)).astype(BF), 1, 0)
    head = dot(short0_t[...], (jnp.concatenate(f_short) * (1.0 / most)).astype(BF), 1, 0)
    g_filt = jnp.concatenate([g_filt[:most] + head, g_filt[most:]]) * decay[...]
    g_fout[...] = exact(second[...].T, g_filt, 1, 0)
    g_second[...] = exact(g_filt, fout[...], 1, 1)


def mlp_forth_kernel(nup, ndown, meta, *refs):
    parts, refs = refs[:4], refs[4:]
    up, refs = refs[:nup], refs[nup:]
    down, refs = refs[:ndown], refs[ndown:]
    b_up, every, hidden, slope, send, keep, wide_up, wide_down = refs
    join(meta, parts, every)
    place_wide(meta, up, wide_up)
    tile = wide_up.shape[1] // 4
    for n in range(4):
        at = n * tile
        pre = dot(every[...], wide_up[:, at : at + tile], 1, 0) + b_up[:, at : at + tile]
        cdf = 0.5 * (1.0 + lax.erf(pre * INV_SQRT2))
        hidden[:, at : at + tile] = (pre * cdf).astype(BF)
        slope[:, at : at + tile] = (cdf + pre * (jnp.exp(-0.5 * pre * pre) * INV_SQRT2PI)).astype(BF)
    place_wide(meta, down, wide_down)
    tile = wide_down.shape[1] // 4
    for n in range(4):
        part_out(meta, dot(hidden[...], wide_down[:, n * tile : (n + 1) * tile], 1, 0), n * tile, send, keep)


def mlp_back_kernel(nup, ndown, meta, *refs):
    parts, refs = refs[:4], refs[4:]
    up, refs = refs[:nup], refs[nup:]
    down, refs = refs[:ndown], refs[ndown:]
    slope, every, g_pre_ref, g_bias, send, keep, wide_up, wide_down = refs
    join(meta, parts, every)
    place_wide(meta, down, wide_down)
    tile = slope.shape[1] // 4
    for n in range(4):
        at = n * tile
        g_hidden = dot(every[...], wide_down[at : at + tile, :], 1, 1)
        g_pre = (g_hidden * slope[:, at : at + tile].astype(F32)).astype(BF)
        g_pre_ref[:, at : at + tile] = g_pre
        g_bias[:, at : at + tile] = jnp.sum(g_pre.astype(F32), axis=0, keepdims=True)
    place_wide(meta, up, wide_up)
    tile = wide_up.shape[0] // 4
    for n in range(4):
        at = n * tile
        part_out(meta, dot(g_pre_ref[...], wide_up[at : at + tile, :], 1, 1), at, send, keep)


def hat_of(value):
    center = value - jnp.mean(value, axis=-1, keepdims=True)
    scale = lax.rsqrt(jnp.mean(center * center, axis=-1, keepdims=True) + EPS)
    return center * scale, scale


def first_norm_kernel(meta, tokens, cotangent, normed, low, sums):
    hat, _ = hat_of(tokens[...].astype(F32))
    normed[...] = hat.astype(BF)
    rounded = cotangent[...].astype(BF)
    low[...] = rounded
    sums[...] = jnp.zeros_like(sums)
    sums[2:3, :] = jnp.sum(rounded.astype(F32), axis=0, keepdims=True)


def add_norm_kernel(meta, state, keep, got, crossed, bias, gain, shift, new, normed):
    value = state[...].astype(F32) + (keep[0] + got[0].astype(F32) + crossed[...].astype(F32)) + bias[...]
    new[...] = value
    hat, _ = hat_of(value)
    normed[...] = (hat * gain[...] + shift[...]).astype(BF)


def add_kernel(meta, state, keep, got, crossed, bias, new):
    new[...] = state[...] + (keep[0] + got[0].astype(F32) + crossed[...].astype(F32)) + bias[...]


def norm_back_kernel(meta, grad, keep, got, crossed, value, gain, new, low, sums):
    g = keep[0] + got[0].astype(F32) + crossed[...].astype(F32)
    hat, scale = hat_of(value[...].astype(F32))
    inner = g * gain[...]
    mean_one = jnp.mean(inner, axis=-1, keepdims=True)
    mean_two = jnp.mean(inner * hat, axis=-1, keepdims=True)
    total = grad[...] + scale * (inner - mean_one - hat * mean_two)
    new[...] = total
    rounded = total.astype(BF)
    low[...] = rounded
    sums[...] = jnp.zeros_like(sums)
    sums[0:1, :] = jnp.sum(g * hat, axis=0, keepdims=True)
    sums[1:2, :] = jnp.sum(g, axis=0, keepdims=True)
    sums[2:3, :] = jnp.sum(rounded.astype(F32), axis=0, keepdims=True)


def mlp_grads_kernel(meta, every, g_pre, hidden, low, out):
    tile = 256
    rows = every.shape[1]
    for n in range(low.shape[1] // tile):
        w = slice(n * tile, (n + 1) * tile)
        for at, left, right in ((0, every, g_pre), (rows, hidden, low)):
            value = dot(left[...], right[:, w], 0, 0).astype(BF)
            out[2 * n, at : at + rows, :] = value[:, :128]
            out[2 * n + 1, at : at + rows, :] = value[:, 128:]


def mlp_split_kernel(meta, every, g_pre, hidden, low, send, mine):
    tile = 256
    rows = every.shape[1]
    first = meta[2] == 0
    for at, left, right in ((0, every, g_pre), (rows, hidden, low)):
        for n in range(right.shape[1] // tile):
            value = dot(left[...], right[:, n * tile : (n + 1) * tile], 0, 0).astype(BF)
            one, two = value[:, :128], value[:, 128:]
            mine[n, at : at + rows, :] = jnp.where(first, one, two)
            send[n, at : at + rows, :] = jnp.where(first, two, one)


def io_grads_kernel(split, meta, g_proj, every, mixed, low, *refs):
    outs, (g_in, g_out) = refs[:-2], refs[-2:]
    wide = mixed.shape[1]
    for j in range(g_proj.shape[1] // wide):
        w = slice(j * wide, (j + 1) * wide)
        g_in[w, :] = dot(g_proj[:, w], every[...], 0, 0).astype(BF)
    g_out[...] = dot(mixed[...], low[...], 0, 0).astype(BF)
    n_grp = g_in.shape[1] // 128
    part = g_in.shape[0] // n_grp
    q = part // 3
    if split:
        send, mine = outs
        places = [(2 * k + x, t.at[k]) for k in range(n_grp // 2) for x, t in ((meta[2], mine), (1 - meta[2], send))]
    else:
        places = [(g, outs[0].at[g]) for g in range(n_grp)]
    for g, target in places:
        for lb in range(n_grp):
            at = lb * 4 * q
            target[at : at + part, :] = g_in[span(g, part), lb * 128 : (lb + 1) * 128]
            target[at + part : at + part + q, :] = g_out[lb * q : (lb + 1) * q, span(g, 128)]


def owner_sum_kernel(meta, mine, got, keep, send):
    for k in range(2):
        near = meta[1] ^ (2 * k)
        far = near ^ 1
        keep[k] = mine[near].astype(F32) + got[near].astype(F32)
        send[k] = (mine[far].astype(F32) + got[far].astype(F32)).astype(BF)


def last_sum_kernel(meta, keep, got, crossed, out):
    out[...] = (keep[0] + got[0].astype(F32) + crossed[...].astype(F32)).astype(BF)


def small_last_kernel(meta, *refs):
    pieces, out, held = refs[:-2], refs[-2], refs[-1]
    half = len(pieces)
    for k, v in enumerate(pieces):
        held[lax.rem(meta[1] - k + half, half)] = v[...].astype(F32)
    total = held[0]
    for k in range(1, half):
        total = total + held[k]
    out[...] = total.astype(BF)


def small_turn_kernel(meta, mine, got, own, *sends):
    half = got.shape[0]
    for k, send in enumerate((own,) + sends):
        to = lax.rem(meta[1] + k, half)
        send[...] = (mine[to].astype(F32) + got[to].astype(F32)).astype(BF)


def prep_kernel(small, meta, up, down, w_in, w_out, *refs):
    if small:
        in_bias, conv_weight, conv_bias, skip, fout, up_bias, gain, shift, branch = refs[:9]
        refs = refs[9:]
    io_out, up_out, down_out, turned = refs[:4]
    s = meta[0]
    up_out[...] = up[0]
    n_grp, f, lanes = down.shape[1], down.shape[3], down.shape[4]
    q = w_out.shape[3]
    for g in range(n_grp):
        down_out[g * f : (g + 1) * f, :] = down[0, g, 0]
        io_out[g * 4 * q + 3 * q : (g + 1) * 4 * q, :] = w_out[0, g, 0]
    for k in range(3):
        turned[...] = w_in[0, :, k * lanes : (k + 1) * lanes].astype(F32).T
        piece = turned[span(s, q), :].astype(BF)
        for lb in range(n_grp):
            io_out[lb * 4 * q + k * q : lb * 4 * q + (k + 1) * q, :] = piece[:, lb * 128 : (lb + 1) * 128]
    if not small:
        return
    (rows,) = refs[4:]
    depth = up_bias.shape[0]
    rows[...] = jnp.zeros_like(rows)
    b_in, w_tap, b_tap = in_bias[...].astype(F32), conv_weight[...].astype(F32), conv_bias[...].astype(F32)
    skips = skip[...].astype(F32)
    for l in range(depth):
        at = l * SLOT
        outs = fout[l].astype(F32)
        for b in range(3):
            w = slice(b * lanes, (b + 1) * lanes)
            rows[b, at : at + 1, :] = b_in[l : l + 1, w]
            rows[b, at + 1 : at + 4, :] = w_tap[l][:, w]
            rows[b, at + 4 : at + 5, :] = b_tap[l : l + 1, w]
        rows[3, at : at + 4, :] = outs[60:64]
        rows[3, at + 4 : at + 5, :] = skips[l : l + 1]
        for b in range(4):
            rows[b, at + 5 : at + 20, :] = outs[15 * b : 15 * b + 15]
    lane = lax.broadcasted_iota(jnp.int32, (lanes, lanes), 0)
    to = lax.broadcasted_iota(jnp.int32, (lanes, lanes), 1)
    packed = jnp.zeros((2 * SLOT, lanes), F32)
    for b in range(4):
        hit = (lane == s * q + to - b * q) & (to >= b * q) & (to < (b + 1) * q)
        packed = packed + dot(rows[b].astype(BF), jnp.where(hit, 1.0, 0.0).astype(BF), 1, 0)
    ups = up_bias[:, span(s, lanes)].astype(F32)
    tail = [ups, jnp.zeros((TOK - UP_AT - depth, lanes), F32)]
    for v in (gain, shift, branch):
        v = v[...].astype(F32)
        tail += [v[l] for l in range(depth)]
    base = n_grp * 4 * q
    io_out[base : base + SMALL, :] = jnp.concatenate([packed] + tail).astype(BF)


def unpack_kernel(meta, slab, other, e_wide, e_all, tok, rows5, skip, fout, b_up, wide):
    place_wide(meta, (slab, other), wide)
    depth = fout.shape[0]
    hid = fout.shape[1] // depth
    fout[...] = jnp.zeros_like(fout)
    tok[...] = wide[TOK:SMALL, :].astype(F32)
    low = wide[: 2 * SLOT, :]
    five = dot(low, e_wide[...], 1, 0)
    for l in range(depth):
        rows5[l] = five[l * SLOT : l * SLOT + 5]
        b_up[l] = wide[UP_AT + l : UP_AT + l + 1, :].astype(F32)
    for b in range(4):
        found = dot(low, e_all[b], 1, 0)
        for l in range(depth):
            at, to = l * SLOT, l * hid
            fout[l, to + 15 * b : to + 15 * b + 15, :] = found[at + 5 : at + 20]
            if b == 3:
                fout[l, to + 60 : to + 64, :] = found[at : at + 4]
                skip[l] = found[at + 4 : at + 5]


def net_grads(depth, seconds, net):
    feats_t, one_t, pre0, cos0, freq0, pre1, cos1, freq1, mid = net
    g = seconds[0][...]
    for v in seconds[1:]:
        g = g + v[...]
    lanes = g.shape[1]
    hid = lanes // depth
    g = g * cos1[...]
    g_freq1 = jnp.sum(g * pre1[...], axis=0, keepdims=True)
    g = g * freq1[...]
    g_bias1 = jnp.sum(g, axis=0, keepdims=True)
    full = exact(one_t[...], g, 1, 0)
    lane = lax.broadcasted_iota(jnp.int32, (hid, lanes), 1)
    g_mid = full[:hid]
    for l in range(1, depth):
        g_mid = jnp.where(lane >= l * hid, full[l * hid : (l + 1) * hid], g_mid)
    g = exact(g, mid[...], 1, 1) * cos0[...]
    g_freq0 = jnp.sum(g * pre0[...], axis=0, keepdims=True)
    g = g * freq0[...]
    g_bias0 = jnp.sum(g, axis=0, keepdims=True)
    g_in = exact(feats_t[...], g, 1, 0)
    rows = [g_mid, g_in[:33], g_bias0, g_bias1, g_freq0, g_freq1]
    rows.append(jnp.zeros((NET - hid - 37, lanes), F32))
    return jnp.concatenate(rows)


def pack_kernel(depth, meta, *refs):
    ups, refs = refs[:depth], refs[depth:]
    smalls, refs = refs[:depth], refs[depth:]
    fouts, refs = refs[:depth], refs[depth:]
    toks, refs = refs[: 2 * depth + 1], refs[2 * depth + 1 :]
    seconds, refs = refs[:depth], refs[depth:]
    net, refs = refs[:9], refs[9:]
    e_wide, e_all, send, mine, rows, wide = refs
    chans = fouts[0].shape[1]
    hid = fouts[0].shape[0] // depth
    rows[...] = jnp.zeros_like(rows)
    for l in range(depth):
        at = l * SLOT
        rows[4, at : at + 5, :] = smalls[l][:5, :]
        for b in range(4):
            rows[b, at + 5 : at + 20, :chans] = fouts[l][hid * l + 15 * b : hid * l + 15 * b + 15, :]
        rows[3, at : at + 4, :chans] = fouts[l][hid * l + 60 : hid * l + 64, :]
        rows[3, at + 4 : at + 5, :chans] = smalls[l][5:6, :chans]
    packed = dot(rows[4].astype(BF), e_wide[...], 1, 1)
    for b in range(4):
        packed = packed + dot(rows[b, :, :chans].astype(BF), e_all[b], 1, 1)
    wide[: 2 * SLOT, :] = packed
    wide[2 * SLOT :, :] = jnp.zeros((SMALL - 2 * SLOT, wide.shape[1]), F32)
    for l in range(depth):
        wide[UP_AT + l : UP_AT + l + 1, :] = ups[l][...]
        for i in range(2):
            v = toks[2 * l + i]
            at = TOK + 2 * l + i
            wide[at : at + 1, :] = v[0:1, :]
            wide[at + 2 * depth : at + 2 * depth + 1, :] = v[1:2, :]
            wide[at + 4 * depth : at + 4 * depth + 1, :] = toks[2 * l + i + 1][2:3, :]
    grads = net_grads(depth, seconds, net).astype(BF)
    for k in range(send.shape[0]):
        mine[k, :SMALL] = wide[:, span(2 * k + meta[2], 128)].astype(BF)
        send[k, :SMALL] = wide[:, span(2 * k + 1 - meta[2], 128)].astype(BF)
        mine[k, SMALL:] = grads
        send[k, SMALL:] = grads


def finish_small_kernel(q, meta, *refs):
    parts, refs = refs[:4], refs[4:]
    gain, shift, branch, in_bias, conv_weight, conv_bias, skip, fout, up_bias, g_in, g_mid, g_bias, g_freq, held = refs
    depth = fout.shape[0]
    hid = fout.shape[1]
    lanes = parts[0].shape[1]
    lane = lax.broadcasted_iota(jnp.int32, (lanes, lanes), 0)
    to = lax.broadcasted_iota(jnp.int32, (lanes, lanes), 1)
    for k, part in enumerate(parts):
        held[meta[0] ^ ORDER[k]] = part[...].astype(F32)
    tok = held[0]
    for k in range(1, 4):
        tok = tok + held[k]
    for l in range(depth):
        w = slice(l * hid, (l + 1) * hid)
        at = SMALL + hid
        g_mid[l] = tok[SMALL:at, w]
        g_in[l] = tok[at : at + 33, w]
        g_bias[l] = tok[at + 33 : at + 35, w]
        g_freq[l] = tok[at + 35 : at + 37, w]
    for l in range(depth):
        for t, v in enumerate((gain, shift, branch)):
            at = TOK + 2 * depth * t + 2 * l
            v[l] = tok[at : at + 2]
    for k, part in enumerate(parts):
        up_bias[:, span(meta[0] ^ ORDER[k], lanes)] = part[UP_AT : UP_AT + depth, :].astype(F32)
    for b in range(4):
        found = jnp.zeros((2 * SLOT, lanes), F32)
        for k, part in enumerate(parts):
            s = meta[0] ^ ORDER[k]
            hit = (to - s * q == lane - b * q) & (lane >= b * q) & (lane < (b + 1) * q)
            found = found + dot(part[: 2 * SLOT, :], jnp.where(hit, 1.0, 0.0).astype(BF), 1, 0)
        for l in range(depth):
            at = l * SLOT
            fout[l, 15 * b : 15 * b + 15, :] = found[at + 5 : at + 20]
            if b == 3:
                fout[l, 60:64, :] = found[at : at + 4]
                skip[l : l + 1, :] = found[at + 4 : at + 5]
            else:
                w = slice(b * lanes, (b + 1) * lanes)
                in_bias[l : l + 1, w] = found[at : at + 1]
                conv_weight[l, :, w] = found[at + 1 : at + 4]
                conv_bias[l : l + 1, w] = found[at + 4 : at + 5]


def finish_mlp_kernel(extra, meta, *refs):
    parts, refs = refs[:4], refs[4:]
    up, down = refs[extra:]
    rows = up.shape[1]
    n_grp, f = down.shape[1], down.shape[3]
    for k, part in enumerate(parts):
        s = meta[0] ^ ORDER[k]
        up[0, :, span(s, part.shape[1])] = part[:rows, :].astype(F32)
        for g in range(n_grp):
            down[0, g, s] = part[rows + g * f : rows + (g + 1) * f, :].astype(F32)


def finish_io_kernel(extra, meta, *refs):
    parts, refs = refs[:4], refs[4:]
    g_in, g_out, turned = refs[extra:]
    n_grp, q = g_out.shape[1], g_out.shape[3]
    for k, part in enumerate(parts):
        s = meta[0] ^ ORDER[k]
        for lb in range(n_grp):
            at = lb * 4 * q
            for j in range(3):
                row = pl.ds(pl.multiple_of(j * 4 * q + s * q, q), q)
                turned[row, lb * 128 : (lb + 1) * 128] = part[at + j * q : at + (j + 1) * q, :].astype(F32)
            g_out[0, lb, s] = part[at + 3 * q : at + 4 * q, :].astype(F32)
    for j in range(3):
        g_in[0, :, j * 4 * q : (j + 1) * 4 * q] = turned[j * 4 * q : (j + 1) * 4 * q, :].T


def after(value, *others):
    return lax.optimization_barrier((value,) + others)[0]


def body(
    tokens,
    lengths,
    cotangent,
    norm_gain,
    norm_bias,
    in_weight,
    in_bias,
    conv_weight,
    conv_bias,
    skip_bias,
    filt_out,
    out_weight,
    up_weight,
    up_bias,
    down_weight,
    branch_bias,
    filt_in,
    filt_mid,
    filt_bias,
    sine_freq,
):
    comm = Comm()
    n_grp, n_seq, s, nz = comm.n_grp, comm.n_seq, comm.s, comm.nz
    depth = norm_gain.shape[0]
    tok_rows, width = tokens.shape
    total = tok_rows * n_seq
    half, most = total // 2, total // 4
    cols = width // n_grp
    q = cols // n_seq
    ff_shard = up_weight.shape[2]
    f = ff_shard // n_seq
    hid = filt_out.shape[1]
    chans = n_grp * q
    count = lengths.shape[1]
    lens = lengths[0]
    starts = half + jnp.cumsum(lens) - lens
    meta = jnp.concatenate([jnp.stack([s, comm.z, comm.x, comm.y, comm.c]), starts, lens]).astype(jnp.int32)

    down_view = down_weight.reshape(depth, n_grp, n_seq, f, cols)
    out_view = out_weight.reshape(depth, n_grp, n_seq, q, cols)

    def prepare(l, small):
        args = [
            (up_weight, (1, width, f), lambda i, m: (l, 0, m[0])),
            (down_view, (1, n_grp, 1, f, cols), lambda i, m: (l, 0, m[0], 0, 0)),
            (in_weight, (1, width, 3 * cols), lambda i, m: (l, 0, 0)),
            (out_view, (1, n_grp, 1, q, cols), lambda i, m: (l, 0, m[0], 0, 0)),
        ]
        scratch = [((cols, width), F32)]
        rows = width
        if small:
            args += [in_bias, conv_weight, conv_bias, skip_bias, filt_out, up_bias, norm_gain, norm_bias, branch_bias]
            scratch.append(((4, 2 * SLOT, cols), F32))
            rows += SMALL
        outs = [((rows, cols), BF), ((width, f), BF), ((n_grp * f, cols), BF)]
        return run(lambda *r: prep_kernel(small, *r), outs, meta, args, scratch)

    def by_permutes(unit):
        slab = jnp.stack([unit] + [comm.turn(unit, "grp", n_grp, k) for k in range(1, nz)])
        return [slab, comm.flip(slab, "grp", n_grp)]

    first_units = prepare(0, True)
    hat0, low_first, sums_first = run(
        first_norm_kernel,
        [((tok_rows, width), BF), ((tok_rows, width), BF), ((8, width), F32)], meta, [tokens, cotangent])
    ready = list(first_units)
    for l in range(1, depth):
        ready += prepare(l, False)
    chunks, slab = [], None
    for unit in ready:
        if slab is not None:
            unit = after(unit, slab)
        slab = jnp.stack([unit] + [comm.turn(unit, "grp", n_grp, k) for k in range(1, nz)])
        chunks.append([slab, comm.flip(slab, "grp", n_grp)])
    weights = [tuple(chunks[3 * l : 3 * l + 3]) for l in range(depth)]

    lane_from = jnp.arange(n_grp * cols, dtype=jnp.int32)[:, None]
    lane_wide = jnp.arange(3 * chans, dtype=jnp.int32)[None, :]
    lane_chan = jnp.arange(chans, dtype=jnp.int32)[None, :]
    e_wide = ((lane_from // cols == lane_wide // (3 * q)) & (lane_from % cols == lane_wide % (3 * q))).astype(BF)
    e_all = jnp.stack([
        ((lane_from // cols == lane_chan // q) & (lane_from % cols == b * q + lane_chan % q)) for b in range(4)
    ]).astype(BF)
    slab, other = weights[0][0]
    small_block = ((nz, SMALL, cols), lambda i, m: (0, width // SMALL, 0))
    tok_all, rows5, skip, fout, b_up = run(
        unpack_kernel,
        [((6 * depth, width), F32), ((depth, 5, 3 * chans), F32), ((depth, 1, chans), F32),
         ((depth, depth * hid, chans), F32), ((depth, 1, n_grp * f), F32)],
        meta, [(slab,) + small_block, (other,) + small_block, e_wide, e_all], [((SMALL, width), BF)])
    tok_all = tok_all.reshape(3, depth, 2, 1, width)
    gains, shifts, b_branch = tok_all[0], tok_all[1], tok_all[2]

    mixer = Mixer(lens, total, most)
    long, short, short0 = mixer.long, mixer.short, mixer.short0
    long_t, short_t, short0_t = long.T, short.T, short0.T
    feats, tpos = positions(half)
    channel = (
        jnp.arange(n_grp, dtype=jnp.int32)[:, None] * cols + s * q + jnp.arange(q, dtype=jnp.int32)[None, :]
    ).reshape(-1).astype(F32)
    rate = jnp.abs(FAST + (SLOW - FAST) * channel / (width - 1))
    decay = jnp.exp(-tpos[:, None] * rate[None, :])
    lanes = depth * hid
    bias0, bias1 = (filt_bias[:, i].reshape(1, lanes) for i in range(2))
    freq0, freq1 = (sine_freq[:, i].reshape(1, lanes) for i in range(2))
    mid_all = jnp.zeros((lanes, lanes), F32)
    for l in range(depth):
        mid_all = lax.dynamic_update_slice(mid_all, filt_mid[l], (l * hid, l * hid))
    pre0 = jnp.dot(feats, jnp.transpose(filt_in, (1, 0, 2)).reshape(-1, lanes), precision=HIGH) + bias0
    one, cos0 = jnp.sin(freq0 * pre0), jnp.cos(freq0 * pre0)
    pre1 = jnp.dot(one, mid_all, precision=HIGH) + bias1
    second, cos1 = jnp.sin(freq1 * pre1), jnp.cos(freq1 * pre1)
    feats_t = jnp.pad(feats.T, ((0, -feats.shape[1] % 8), (0, 0)))
    network = [feats_t, one.T, pre0, cos0, freq0, pre1, cos1, freq1, mid_all]

    def gather_parts(v):
        across = comm.turn(v, "seq", n_seq, 1)
        return [v, across, comm.flip(v, "seq", n_seq), comm.flip(across, "seq", n_seq)]

    leaving = []

    def scatter_parts(send, keep):
        got = comm.flip(send, "seq", n_seq)
        other = 1 - comm.y
        crossed = (pick(keep, other, 0) + pick(got, other, 0).astype(F32)).astype(BF)
        own = ((1, tok_rows, width), lambda i, m: (m[3], 0, 0))
        leaving.append(crossed)
        return (keep,) + own, (got,) + own, comm.turn(crossed, "seq", n_seq, 1)

    parts_out = [((2, tok_rows, width), BF), ((2, tok_rows, width), F32)]
    io_scratch = [((3 * chans, width), BF), ((chans, width), BF)]
    mlp_scratch = [((width, n_grp * f), BF), ((n_grp * f, width), BF)]
    state = tokens
    saved = []
    normed = hat0
    for l in range(depth):
        w_io, w_up, w_down = weights[l]
        parts = gather_parts(normed)
        if l == 0:
            low_parts = gather_parts(low_first)
            parts[0] = after(parts[0], *low_parts, chunks[1][0])
        else:
            parts[0] = after(parts[0], chunks[4][0])
        every, chan, inner, mixed, send, keep = run(
            lambda *r, n=len(w_io), raw=l == 0: mix_forth_kernel(count, n, raw, *r),
            [((total, width), BF), ((total, 3 * chans), BF), ((total, chans), F32), ((total, chans), BF)] + parts_out,
            meta,
            parts + w_io + [long, long_t, short, short_t, short0, second, decay, fout[l], rows5[l], skip[l],
                            gains[l, 0], shifts[l, 0]],
            io_scratch,
            flops=3 * 10**9,
        )
        if l:
            send = after(send, chunks[4][1], chunks[5][0])
        got = scatter_parts(send, keep)
        if l == 0:
            state = after(state, chunks[1][1], chunks[2][0])
        mid, normed2 = run(
            add_norm_kernel, [((tok_rows, width), F32), ((tok_rows, width), BF)], meta,
            [state, *got, b_branch[l, 0], gains[l, 1], shifts[l, 1]],
        )
        parts = gather_parts(normed2)
        if l == 0:
            parts[0] = after(parts[0], chunks[2][1], chunks[3][0])
        every2, hidden, slope, send, keep = run(
            lambda *r, n=len(w_up), m=len(w_down): mlp_forth_kernel(n, m, *r),
            [((total, width), BF), ((total, n_grp * f), BF), ((total, n_grp * f), BF)] + parts_out,
            meta, parts + w_up + w_down + [b_up[l]], mlp_scratch,
            flops=4 * 10**9,
        )
        saved.append((state, every, chan, inner, mixed, mid, every2, hidden, slope))
        got = scatter_parts(send, keep)
        if l == 0:
            mid = after(mid, chunks[3][1], chunks[4][0])
        if l + 1 < depth:
            state, normed = run(
                add_norm_kernel, [((tok_rows, width), F32), ((tok_rows, width), BF)], meta,
                [mid, *got, b_branch[l, 1], gains[l + 1, 0], shifts[l + 1, 0]],
            )
        else:
            (state,) = run(add_kernel, [((tok_rows, width), F32)], meta, [mid, *got, b_branch[l, 1]])

    grad = cotangent
    toks = [None] * (2 * depth) + [sums_first]
    g_fouts, g_seconds, smalls, up_biases = ([None] * depth for _ in range(4))

    def hop(v, bit):
        return lax.ppermute(v, "grp", [(i, i ^ bit) for i in range(n_grp)])

    def owner_first(mine, got):
        rows = mine.shape[1:]
        keep, send = run(owner_sum_kernel, [((2,) + rows, F32), ((2,) + rows, BF)], meta, [mine, got])
        return keep, hop(send, 2)

    def owner_second(keep, got):
        return [keep, got, hop((keep[1] + got[1].astype(F32)).astype(BF), 4)]

    def owner_end(pieces):
        keep, got, crossed = pieces
        block = ((1,) + crossed.shape, lambda i, m: (0, 0, 0))
        return run(last_sum_kernel, [(crossed.shape, BF)], meta, [(keep,) + block, (got,) + block, crossed])[0]

    norm_outs = [((tok_rows, width), F32), ((tok_rows, width), BF), ((8, width), F32)]
    for l in reversed(range(depth)):
        w_io, w_up, w_down = weights[l]
        first, every, chan, inner, mixed, mid, every2, hidden, slope = saved[l]
        low, g_pre, up_biases[l], send, keep = run(
            lambda *r, n=len(w_up), m=len(w_down): mlp_back_kernel(n, m, *r),
            [((total, width), BF), ((total, n_grp * f), BF), ((1, n_grp * f), F32)] + parts_out,
            meta, low_parts + w_up + w_down + [slope], mlp_scratch,
            flops=4 * 10**9,
        )
        got = scatter_parts(send, keep)
        operands = [every2, g_pre, hidden, low]
        if l:
            (g_mlp,) = run(mlp_grads_kernel, [((n_grp, 2 * width, cols), BF)], meta, operands)
            grad = after(grad, g_mlp)
        else:
            mlp_send, mlp_mine = run(
                mlp_split_kernel, [((nz, 2 * width, cols), BF)] * 2, meta, operands)
            mlp_got = comm.flip(mlp_send, "grp", n_grp)
            grad = after(grad, mlp_send)
        grad, low_own, toks[2 * l + 1] = run(norm_back_kernel, norm_outs, meta, [grad, *got, mid, gains[l, 1]])
        low_parts = gather_parts(low_own)
        if l:
            mlp_unit = lax.psum_scatter(after(g_mlp, low_own), "grp", scatter_dimension=0, tiled=False)
        low, g_proj, g_fouts[l], g_seconds[l], smalls[l], send, keep = run(
            lambda *r, n=len(w_io): mix_back_kernel(count, n, *r),
            [((total, width), BF), ((total, 3 * chans), BF), ((lanes, chans), F32), ((half, lanes), F32),
             ((8, 3 * chans), F32)] + parts_out,
            meta,
            low_parts + w_io + [long, long_t, short, short_t, short0, short0_t, second, decay, fout[l], rows5[l],
                                skip[l], chan, inner],
            io_scratch,
            flops=5 * 10**9,
        )
        got = scatter_parts(send, keep)
        operands = [g_proj, every, mixed, low]
        scratch = [((3 * chans, width), BF), ((chans, width), BF)]
        if l:
            (g_io,) = run(lambda *r: io_grads_kernel(False, *r), [((n_grp, width, cols), BF)], meta, operands, scratch)
            grad = after(grad, g_io)
        else:
            io_send, io_mine = run(
                lambda *r: io_grads_kernel(True, *r), [((nz, width, cols), BF)] * 2, meta, operands, scratch)
            io_got = comm.flip(io_send, "grp", n_grp)
        grad, low_own, toks[2 * l] = run(norm_back_kernel, norm_outs, meta, [grad, *got, first, gains[l, 0]])
        if l:
            low_parts = gather_parts(low_own)
            io_one = lax.psum_scatter(after(g_io, low_own), "grp", scatter_dimension=0, tiled=False)

    def finish(kernel, parts, shapes, old, scratch=()):
        outs = []
        for shape in shapes:
            outs.append(((depth,) + shape, F32, (1,) + shape, lambda i, m, l=l, n=len(shape): (l,) + (0,) * n))
        return run(
            lambda *r, n=len(old): kernel(n, *r), outs, meta, parts + [(v, None, None) for v in old],
            scratch, alias={5: 0, 6: 1} if old else None)

    mlp_shapes = [(width, ff_shard), (n_grp, n_seq, f, cols)]
    io_shapes = [(width, 3 * cols), (n_grp, n_seq, q, cols)]
    turned = [((3 * cols, width), F32)]

    send, mine = run(
        lambda *r: pack_kernel(depth, *r), [((nz, SMALL + NET, cols), BF)] * 2, meta,
        up_biases + smalls + g_fouts + toks + g_seconds + network + [e_wide, e_all],
        [((5, 2 * SLOT, 3 * chans), F32), ((SMALL, width), F32)])
    mlp_first = owner_first(mlp_mine, after(mlp_got, io_send, low_own))
    io_first = owner_first(io_mine, after(io_got, mlp_first[0], send))
    parts_one = gather_parts(after(mlp_unit, low_own))
    small_got = after(comm.flip(send, "grp", n_grp), parts_one[1])
    small_rows = (SMALL + NET, cols)
    own, *sends = run(small_turn_kernel, [(small_rows, BF)] * nz, meta, [mine, small_got])
    pieces = [own] + [comm.turn(v, "grp", n_grp, k) for k, v in enumerate(sends, 1)]
    mlp_pieces = owner_second(after(mlp_first[0], *pieces[1:]), mlp_first[1])
    io_turn = owner_second(*io_first)
    (small,) = run(small_last_kernel, [(small_rows, BF)], meta, pieces, [((nz,) + small_rows, F32)])
    small_parts = gather_parts(small)

    l = 1
    mlp_grads = finish(finish_mlp_kernel, parts_one, mlp_shapes, [])
    mlp_pieces[0], state, *mlp_grads = lax.optimization_barrier(
        (after(mlp_pieces[0], io_first[1], *small_parts), state, *mlp_grads))
    io_grads = finish(finish_io_kernel, gather_parts(after(io_one, *small_parts)), io_shapes, [], turned)
    io_turn[0], *io_grads = lax.optimization_barrier((io_turn[0], *io_grads))
    shared_shapes = [v.shape for v in (filt_in, filt_mid, filt_bias, sine_freq)]
    small_grads = run(
        lambda *r: finish_small_kernel(q, *r),
        [(v.shape, F32) for v in (norm_gain, norm_bias, branch_bias, in_bias, conv_weight, conv_bias, skip_bias,
                                  filt_out, up_bias)] + [(shape, F32) for shape in shared_shapes],
        meta, small_parts, [((n_seq,) + small_rows, F32)])
    io_turn[0], *small_grads = lax.optimization_barrier((io_turn[0], *small_grads))
    (norm_gain_grad, norm_bias_grad, branch_grad, in_bias_grad, taps_grad, tap_bias_grad, skip_grad, fout_grad,
     up_bias_grad, *shared) = small_grads
    l = 0
    mlp_unit = owner_end(mlp_pieces)
    up_grad, down_grad = finish(finish_mlp_kernel, gather_parts(mlp_unit), mlp_shapes, mlp_grads)
    in_grad, out_grad = finish(finish_io_kernel, gather_parts(owner_end(io_turn)), io_shapes, io_grads, turned)
    return (
        state, grad, norm_gain_grad, norm_bias_grad, in_grad, in_bias_grad, taps_grad, tap_bias_grad,
        skip_grad, fout_grad, out_grad.reshape(depth, width, cols), up_grad, up_bias_grad,
        down_grad.reshape(depth, n_grp * ff_shard, cols), branch_grad, shared[0], shared[1], shared[2], shared[3],
    )


def solution(mesh):
    tok = P(("grp", "seq"), None)
    last3, last2 = P(None, None, "grp"), P(None, "grp")
    in_specs = (
        tok, P("grp", None), tok, last3, last3, last3, last2, last3, last2, last2,
        last3, last3, last3, last2, last3, last3, P(), P(), P(), P(),
    )
    out_specs = (
        tok, tok, last3, last3, last3, last2, last3, last2, last2, last3,
        last3, last3, last2, last3, last3, P(), P(), P(), P(),
    )
    small = mesh.shape["seq"] == 4 and mesh.shape["grp"] == 8
    return jax.shard_map(body if small else body_any, mesh=mesh, in_specs=in_specs, out_specs=out_specs, check_vma=False)
```

```python
import math

import jax
import jax.numpy as jnp
from jax import lax
from jax.experimental import pallas as pl
from jax.experimental.pallas import tpu as pltpu
from jax.sharding import PartitionSpec as P

EPS = 1e-05
HIGH = lax.Precision.HIGHEST
FAST = math.log(0.01) / 0.3
SLOW = math.log(0.01) / 1.5
F32 = jnp.float32
BF = jnp.bfloat16
INV_SQRT2 = 1.0 / math.sqrt(2.0)
INV_SQRT2PI = 1.0 / math.sqrt(2.0 * math.pi)


def dot(a, b, da, db):
    return lax.dot_general(a, b, (((da,), (db,)), ((), ())), preferred_element_type=F32)


def pick(v, index, axis):
    return lax.dynamic_index_in_dim(v, index, axis, keepdims=False)


class Comm:
    def __init__(self):
        self.n_grp = lax.axis_size("grp")
        self.n_seq = lax.axis_size("seq")
        self.nz = self.n_grp // 2
        self.ny = self.n_seq // 2
        g = lax.axis_index("grp")
        s = lax.axis_index("seq")
        self.g, self.s = g, s
        self.z, self.x = g // 2, g % 2
        self.y, self.c = s // 2, s % 2

    @staticmethod
    def flip(v, axis, size):
        return lax.ppermute(v, axis, [(i, i ^ 1) for i in range(size)])

    @staticmethod
    def turn(v, axis, size, k):
        half = size // 2
        perm = [(2 * i + j, 2 * ((i + k) % half) + j) for i in range(half) for j in range(2)]
        return lax.ppermute(v, axis, perm)

    def _gather(self, v, axis, size, major, minor):
        half = size // 2
        if half > 4:
            return lax.all_gather(v, axis, axis=0, tiled=False)
        parts = [v] + [self.turn(v, axis, size, k) for k in range(1, half)]
        others = [self.flip(p, axis, size) for p in parts]
        if half == 2:
            zero = major == 0
            mine = jnp.stack([jnp.where(zero, parts[0], parts[1]), jnp.where(zero, parts[1], parts[0])])
            them = jnp.stack([jnp.where(zero, others[0], others[1]), jnp.where(zero, others[1], others[0])])
        else:
            order = jnp.mod(major - jnp.arange(half), half)
            mine = jnp.stack([pick(jnp.stack(parts), order[i], 0) for i in range(half)])
            them = jnp.stack([pick(jnp.stack(others), order[i], 0) for i in range(half)])
        first = jnp.where(minor == 0, mine, them)
        second = jnp.where(minor == 0, them, mine)
        return jnp.stack([first, second], axis=1).reshape((size,) + v.shape)

    def gather_seq(self, v):
        return self._gather(v, "seq", self.n_seq, self.y, self.c)

    def gather_grp(self, v):
        half = self.nz
        slab = jnp.zeros((half,) + v.shape, v.dtype)
        zeros = (0,) * v.ndim
        for k in range(half):
            part = v if k == 0 else self.turn(v, "grp", self.n_grp, k)
            slab = lax.dynamic_update_slice(slab, part[None], (jnp.mod(self.z - k, half),) + zeros)
        other = self.flip(slab, "grp", self.n_grp)
        first = jnp.where(self.x == 0, slab, other)
        second = jnp.where(self.x == 0, other, slab)
        return jnp.stack([first, second], axis=1).reshape((self.n_grp,) + v.shape)

    def _scatter(self, v, axis, size, major, minor, kind):
        half = size // 2
        if half > 4:
            return lax.psum_scatter(v.astype(kind), axis, scatter_dimension=0, tiled=False).astype(F32)
        v = v.reshape((half, 2) + v.shape[1:])
        got = self.flip(pick(v, 1 - minor, 1).astype(kind), axis, size)
        mine = pick(v, minor, 1).astype(F32) + got.astype(F32)
        total = pick(mine, major, 0)
        for k in range(1, half):
            sent = pick(mine, jnp.mod(major + k, half), 0).astype(kind)
            total = total + self.turn(sent, axis, size, k).astype(F32)
        return total

    def scatter_seq(self, v, kind=BF):
        return self._scatter(v, "seq", self.n_seq, self.y, self.c, kind)

    def scatter_grp(self, v, kind=BF):
        return self._scatter(v, "grp", self.n_grp, self.z, self.x, kind)

    def sum_all(self, v, axis, size):
        half = size // 2
        if half > 4:
            return lax.psum(v, axis)
        v = v + self.flip(v, axis, size)
        total = v
        for k in range(1, half):
            total = total + self.turn(v, axis, size, k)
        return total


def norm_stats(value):
    center = value - jnp.mean(value, axis=-1, keepdims=True)
    scale = lax.rsqrt(jnp.mean(center * center, axis=-1, keepdims=True) + EPS)
    return center * scale, scale


def norm_back(grad, hat, scale, gain):
    inner = grad * gain
    mean_one = jnp.mean(inner, axis=-1, keepdims=True)
    mean_two = jnp.mean(inner * hat, axis=-1, keepdims=True)
    return scale * (inner - mean_one - hat * mean_two), jnp.sum(grad * hat, axis=0), jnp.sum(grad, axis=0)


def positions(length):
    index = jnp.arange(length, dtype=jnp.int32).astype(F32)
    tpos = index / (length - 1)
    bands = 0.0001 + (15.0 - 0.0001) * jnp.arange(16, dtype=jnp.int32).astype(F32) / 15.0
    angle = 2.0 * math.pi / length * index[:, None] * bands[None, :]
    return (jnp.concatenate([tpos[:, None], jnp.cos(angle), -jnp.sin(angle)], axis=1), tpos)


def odd_table(size, place):
    freq = 2 * jnp.arange(size // 2, dtype=jnp.int32) + 1
    turn = jnp.bitwise_and(freq[:, None] * place[None, :], 2 * size - 1)
    angle = turn.astype(F32) * (math.pi / size)
    return jnp.stack([jnp.cos(angle), -jnp.sin(angle)])


def filter_of(fin, fmid, fbias, freq, fout, feats, decay):
    inner = jnp.sin(freq[0] * (jnp.dot(feats, fin, precision=HIGH) + fbias[0]))
    inner = jnp.sin(freq[1] * (jnp.dot(inner, fmid, precision=HIGH) + fbias[1]))
    return jnp.dot(inner, fout, precision=HIGH) * decay


def lagged(v, lag, mask):
    return jnp.where(mask[None, :, None], jnp.pad(v, ((0, 0), (lag, 0), (0, 0)))[:, : v.shape[1]], 0.0)


def ahead(v, lag):
    return jnp.pad(v, ((0, 0), (0, lag), (0, 0)))[:, lag:]


def times(ar, ai, br, bi):
    return ar * br - ai * bi, ar * bi + ai * br


def times_conj(ar, ai, br, bi):
    return ar * br + ai * bi, ai * br - ar * bi


class Mixer:
    def __init__(self, lens, total, most):
        half = total // 2
        self.half, self.most, self.total, self.count = half, most, total, lens.shape[0]
        starts = half + jnp.cumsum(lens) - lens
        place = jnp.arange(total, dtype=jnp.int32)
        begin = jnp.zeros((total,), jnp.int32)
        for k in range(lens.shape[0]):
            begin = jnp.where(starts[k] <= place, starts[k], begin)
        self.masks = [None] + [place - lag >= begin for lag in (1, 2)]
        self.long = odd_table(2 * half, place[:half]).reshape(2 * half, half).astype(BF)
        self.short0 = odd_table(2 * most, place[:most]).reshape(2 * most, most).astype(BF)
        tail = place[half:]
        tables = []
        for k in range(lens.shape[0]):
            rel = tail - starts[k]
            inside = (rel >= 0) & (rel < lens[k])
            table = odd_table(2 * most, jnp.where(inside, rel, 0))
            tables.append(jnp.where(inside[None, None, :], table, 0.0))
        self.short = jnp.stack(tables).reshape(lens.shape[0] * 2 * most, total - half).astype(BF)

    def split(self, long, short):
        chans = long.shape[-1]
        long = long.reshape(2, self.half, chans)
        short = short.reshape(self.count, 2, self.most, chans)
        return long[0], long[1], short[:, 0], short[:, 1]

    def forth(self, v):
        v = v.astype(BF)
        return self.split(dot(self.long, v[: self.half], 1, 0), dot(self.short, v[self.half :], 1, 0))

    def back(self, spec):
        lr, li, sr, si = spec
        long = jnp.stack([lr, li]).reshape(2 * self.half, -1) * (1.0 / self.half)
        short = jnp.stack([sr, si], axis=1).reshape(self.count * 2 * self.most, -1) * (1.0 / self.most)
        return jnp.concatenate([dot(self.long, long.astype(BF), 0, 0), dot(self.short, short.astype(BF), 0, 0)])

    def filt_spec(self, filt):
        filt = filt.astype(BF)
        long = dot(self.long, filt, 1, 0)
        short = dot(self.short0, filt[: self.most], 1, 0)
        return long[: self.half], long[self.half :], short[: self.most], short[self.most :]

    def filt_back(self, grads):
        lr, li, sr, si = grads
        long = jnp.concatenate([lr, li]) * (1.0 / self.half)
        short = jnp.concatenate([sr, si]) * (1.0 / self.most)
        head = dot(self.short0, short.astype(BF), 0, 0)
        return dot(self.long, long.astype(BF), 0, 0) + jnp.pad(head, ((0, self.half - self.most), (0, 0)))


def body_any(
    tokens,
    lengths,
    cotangent,
    norm_gain,
    norm_bias,
    in_weight,
    in_bias,
    conv_weight,
    conv_bias,
    skip_bias,
    filt_out,
    out_weight,
    up_weight,
    up_bias,
    down_weight,
    branch_bias,
    filt_in,
    filt_mid,
    filt_bias,
    sine_freq,
):
    comm = Comm()
    n_grp, n_seq, s = comm.n_grp, comm.n_seq, comm.s
    depth = norm_gain.shape[0]
    tok_rows, width = tokens.shape
    total = tok_rows * n_seq
    cols = width // n_grp
    q = cols // n_seq
    ff_shard = up_weight.shape[2]
    f = ff_shard // n_seq
    hid = filt_out.shape[1]
    chans = n_grp * q

    def unit_in(l):
        return pick(in_weight[l].T.reshape(3, n_seq, q, width), s, 1).reshape(3 * q, width)

    def unit_out(l):
        return pick(out_weight[l].reshape(n_grp, n_seq, q, cols), s, 1).reshape(chans, cols).T

    def unit_up(l):
        return lax.dynamic_slice_in_dim(up_weight[l], s * f, f, 1).T

    def unit_down(l):
        return pick(down_weight[l].reshape(n_grp, n_seq, f, cols), s, 1).reshape(n_grp * f, cols).T

    tok_small = [norm_gain, norm_bias, branch_bias]
    seq_small = [
        pick(in_bias.reshape(depth, 3, n_seq, q), s, 2),
        pick(conv_weight.reshape(depth, 3, 3, n_seq, q), s, 3),
        pick(conv_bias.reshape(depth, 3, n_seq, q), s, 2),
        pick(skip_bias.reshape(depth, n_seq, q), s, 1),
        pick(filt_out.reshape(depth, hid, n_seq, q), s, 2),
        pick(up_bias.reshape(depth, n_seq, f), s, 1),
    ]
    shapes = [v.shape for v in tok_small + seq_small]
    sizes = [math.prod(shape) for shape in shapes]
    packed = jnp.concatenate([v.reshape(-1) for v in tok_small + seq_small])
    fill = -packed.shape[0] % 2048
    packed = comm.gather_grp(jnp.pad(packed, (0, fill)).reshape(-1, 128)).reshape(n_grp, -1).astype(F32)
    spread, at = [], 0
    for shape, size in zip(shapes, sizes):
        spread.append(packed[:, at : at + size].reshape((n_grp,) + shape))
        at += size

    def last(v):
        return jnp.moveaxis(v, 0, -2).reshape(v.shape[1:-1] + (n_grp * v.shape[-1],))

    def streams(v):
        v = jnp.moveaxis(v, 0, -3)
        return v.reshape(v.shape[:-3] + (3, n_grp * q))

    gains, shifts, b_branch = (last(v) for v in spread[:3])
    b_in, taps, tap_bias = (streams(v) for v in spread[3:6])
    skip, fout, b_up = (last(v) for v in spread[6:9])

    weights = []
    for l in range(depth):
        w_in = comm.gather_grp(unit_in(l)).reshape(3 * chans, width)
        w_out = comm.gather_grp(unit_out(l)).reshape(width, chans)
        w_up = comm.gather_grp(unit_up(l)).reshape(n_grp * f, width)
        w_down = comm.gather_grp(unit_down(l)).reshape(width, n_grp * f)
        weights.append((w_in, w_out, w_up, w_down))

    lens = lengths[0]
    mixer = Mixer(lens, total, total // 4)
    feats, tpos = positions(total // 2)
    channel = (
        jnp.arange(n_grp, dtype=jnp.int32)[:, None] * cols + s * q + jnp.arange(q, dtype=jnp.int32)[None, :]
    ).reshape(-1).astype(F32)
    rate = jnp.abs(FAST + (SLOW - FAST) * channel / (width - 1))
    decay = jnp.exp(-tpos[:, None] * rate[None, :])

    state = tokens.astype(F32)
    saved = []
    for l in range(depth):
        w_in, w_out, w_up, w_down = weights[l]
        filt, filt_pull = jax.vjp(
            lambda *a: filter_of(*a, feats, decay),
            filt_in[l], filt_mid[l], filt_bias[l], sine_freq[l], fout[l],
        )
        hat1, scale1 = norm_stats(state)
        normed = (hat1 * gains[l, 0] + shifts[l, 0]).astype(BF)
        normed = comm.gather_seq(normed).reshape(total, width)
        proj = dot(normed, w_in, 1, 1) + b_in[l].reshape(-1)
        proj = jnp.transpose(proj.astype(BF).reshape(total, 3, chans), (1, 0, 2))
        chan = proj.astype(F32)
        z = tap_bias[l][:, None, :] + taps[l, 0][:, None, :] * chan
        for lag in (1, 2):
            z = z + taps[l, lag][:, None, :] * lagged(chan, lag, mixer.masks[lag])
        prod = z[1] * z[2]
        h_lr, h_li, h_sr, h_si = mixer.filt_spec(filt)
        x_lr, x_li, x_sr, x_si = mixer.forth(prod)
        conv = mixer.back(times(x_lr, x_li, h_lr, h_li) + times(x_sr, x_si, h_sr, h_si))
        inner = conv + skip[l] * prod
        mixed = (z[0] * inner).astype(BF)
        part = dot(mixed, w_out, 1, 1)
        mid = state + comm.scatter_seq(part.reshape(n_seq, tok_rows, width)) + b_branch[l, 0]
        hat2, scale2 = norm_stats(mid)
        normed2 = (hat2 * gains[l, 1] + shifts[l, 1]).astype(BF)
        normed2 = comm.gather_seq(normed2).reshape(total, width)
        pre = dot(normed2, w_up, 1, 1) + b_up[l]
        cdf = 0.5 * (1.0 + lax.erf(pre * INV_SQRT2))
        hidden = (pre * cdf).astype(BF)
        slope = cdf + pre * (jnp.exp(-0.5 * pre * pre) * INV_SQRT2PI)
        part = dot(hidden, w_down, 1, 1)
        state = mid + comm.scatter_seq(part.reshape(n_seq, tok_rows, width)) + b_branch[l, 1]
        saved.append((filt_pull, hat1, scale1, normed, chan, z, prod, inner, (h_lr, h_li, h_sr, h_si),
                      (x_lr, x_li, x_sr, x_si), mixed, hat2, scale2, normed2, slope, hidden))

    grad = cotangent
    units = [None] * depth
    tok_grads, seq_grads, net_grads = [None] * depth, [None] * depth, [None] * depth

    def chunk(v):
        return comm.scatter_grp(v.astype(BF).reshape((n_grp, v.shape[0] // n_grp) + v.shape[1:])).astype(BF)

    for l in reversed(range(depth)):
        w_in, w_out, w_up, w_down = weights[l]
        (filt_pull, hat1, scale1, normed, chan, z, prod, inner, (h_lr, h_li, h_sr, h_si),
         (x_lr, x_li, x_sr, x_si), mixed, hat2, scale2, normed2, slope, hidden) = saved[l]
        low = grad.astype(BF)
        g_two = jnp.sum(low.astype(F32), axis=0)
        low = comm.gather_seq(low).reshape(total, width)
        u_down = chunk(dot(low, hidden, 0, 0))
        g_pre = (dot(low, w_down, 1, 0) * slope).astype(BF)
        g_up_bias = jnp.sum(g_pre.astype(F32), axis=0)
        part = dot(g_pre, w_up, 1, 0)
        u_up = chunk(dot(g_pre, normed2, 0, 0))
        g_normed2 = comm.scatter_seq(part.reshape(n_seq, tok_rows, width))
        g_mid, gain2, shift2 = norm_back(g_normed2, hat2, scale2, gains[l, 1])
        g_mid = g_mid + grad
        low = g_mid.astype(BF)
        g_one = jnp.sum(low.astype(F32), axis=0)
        low = comm.gather_seq(low).reshape(total, width)
        u_out = chunk(dot(low, mixed, 0, 0))
        g_y = dot(low, w_out, 1, 0).astype(BF).astype(F32)
        g_conv = g_y * z[0]
        g_skip = jnp.sum(g_conv * prod, axis=0)
        y_lr, y_li, y_sr, y_si = mixer.forth(g_conv)
        corr = mixer.back(times_conj(y_lr, y_li, h_lr, h_li) + times_conj(y_sr, y_si, h_sr, h_si))
        f_lr, f_li = times_conj(y_lr, y_li, x_lr, x_li)
        f_sr, f_si = times_conj(y_sr, y_si, x_sr, x_si)
        g_filt = mixer.filt_back((f_lr, f_li, jnp.sum(f_sr, axis=0), jnp.sum(f_si, axis=0)))
        g_prod = corr + skip[l] * g_conv
        g_z = jnp.stack([g_y * inner, g_prod * z[2], g_prod * z[1]])
        g_taps = [jnp.sum(g_z * chan, axis=1)]
        g_proj = taps[l, 0][:, None, :] * g_z
        for lag in (1, 2):
            kept = jnp.where(mixer.masks[lag][None, :, None], g_z, 0.0)
            g_taps.append(jnp.sum(g_z * lagged(chan, lag, mixer.masks[lag]), axis=1))
            g_proj = g_proj + taps[l, lag][:, None, :] * ahead(kept, lag)
        g_proj = jnp.transpose(g_proj.astype(BF), (1, 0, 2)).reshape(total, 3 * chans)
        g_in_bias = jnp.sum(g_proj.astype(F32), axis=0).reshape(3, chans)
        part = dot(g_proj, w_in, 1, 0)
        u_in = chunk(dot(g_proj, normed, 0, 0))
        g_normed = comm.scatter_seq(part.reshape(n_seq, tok_rows, width))
        g_state, gain1, shift1 = norm_back(g_normed, hat1, scale1, gains[l, 0])
        grad = g_mid + g_state
        units[l] = (u_in, u_out, u_up, u_down)
        pulled = filt_pull(g_filt)
        net_grads[l] = pulled[:4]
        tok_grads[l] = (jnp.stack([gain1, gain2]), jnp.stack([shift1, shift2]), jnp.stack([g_one, g_two]))
        seq_grads[l] = (g_in_bias, jnp.stack(g_taps), jnp.sum(g_z, axis=1), g_skip, pulled[4], g_up_bias)

    def whole(place):
        return [comm.gather_seq(units[l][place]).astype(F32) for l in range(depth)]

    in_grad = jnp.stack([
        jnp.transpose(v.reshape(n_seq, 3, q, width), (3, 1, 0, 2)).reshape(width, 3 * cols) for v in whole(0)])
    out_grad = jnp.stack([
        jnp.transpose(v.reshape(n_seq, cols, n_grp, q), (2, 0, 3, 1)).reshape(width, cols) for v in whole(1)])
    up_grad = jnp.stack([jnp.transpose(v, (2, 0, 1)).reshape(width, ff_shard) for v in whole(2)])
    down_grad = jnp.stack([
        jnp.transpose(v.reshape(n_seq, cols, n_grp, f), (2, 0, 3, 1)).reshape(n_grp * ff_shard, cols)
        for v in whole(3)])

    def by_owner(v):
        v = v.reshape(v.shape[:-1] + (n_grp, v.shape[-1] // n_grp))
        return jnp.moveaxis(v, -2, 0).reshape(n_grp, -1)

    def by_owner3(v):
        v = v.reshape(v.shape[:-2] + (n_grp, 3, q))
        return jnp.moveaxis(v, -3, 0).reshape(n_grp, -1)

    tok_all = [jnp.stack(v) for v in zip(*tok_grads)]
    seq_all = [jnp.stack(v) for v in zip(*seq_grads)]
    tok_flat = jnp.concatenate([by_owner(v) for v in tok_all], axis=1)
    seq_flat = jnp.concatenate(
        [by_owner3(v) for v in seq_all[:3]] + [by_owner(v) for v in seq_all[3:]], axis=1)
    tok_len, seq_len = tok_flat.shape[1], seq_flat.shape[1]
    flat = jnp.concatenate([tok_flat, seq_flat], axis=1)
    flat = jnp.pad(flat, ((0, 0), (0, -flat.shape[1] % 1024)))
    small = comm.scatter_grp(flat.reshape(n_grp, -1, 128), F32).reshape(-1)
    tok_sum = comm.sum_all(small[:tok_len].reshape(-1, 128), "seq", n_seq).reshape(-1)
    seq_part = jnp.pad(small[tok_len : tok_len + seq_len], (0, -seq_len % 1024)).reshape(-1, 128)
    seq_sum = comm.gather_seq(seq_part).reshape(n_seq, -1)[:, :seq_len]
    norm_gain_grad, norm_bias_grad, branch_grad = tok_sum.reshape(3, depth, 2, cols)
    pieces, at = [], 0
    for shape in shapes[3:]:
        size = math.prod(shape)
        part = seq_sum[:, at : at + size].reshape((n_seq,) + shape)
        at += size
        part = jnp.moveaxis(part, 0, -2)
        pieces.append(part)
    in_bias_grad = pieces[0].reshape(depth, 3 * cols)
    taps_grad = pieces[1].reshape(depth, 3, 3 * cols)
    tap_bias_grad = pieces[2].reshape(depth, 3 * cols)
    skip_grad = pieces[3].reshape(depth, cols)
    fout_grad = pieces[4].reshape(depth, hid, cols)
    up_bias_grad = pieces[5].reshape(depth, ff_shard)

    nets = [jnp.stack(v) for v in zip(*net_grads)]
    flat = jnp.concatenate([v.reshape(-1) for v in nets])
    flat = jnp.pad(flat, (0, -flat.shape[0] % 1024)).reshape(-1, 128)
    flat = comm.sum_all(comm.sum_all(flat, "seq", n_seq), "grp", n_grp).reshape(-1)
    shared, at = [], 0
    for v in nets:
        shared.append(flat[at : at + v.size].reshape(v.shape))
        at += v.size
    return (
        state, grad, norm_gain_grad, norm_bias_grad, in_grad, in_bias_grad, taps_grad, tap_bias_grad,
        skip_grad, fout_grad, out_grad, up_grad, up_bias_grad, down_grad, branch_grad,
        shared[0], shared[1], shared[2], shared[3],
    )


ORDER = (0, 2, 1, 3)
VMEM_BYTES = 56 * 2**20
SMALL = 64
SLOT = 24
COST = 1000
UP_AT = 48
TOK = 52
NET = 112


def run(kernel, outs, meta, args, scratch=(), flops=0, alias=None):
    specs, arrays = [], []
    for a in args:
        if isinstance(a, tuple):
            array, block, place = a
            if block is None:
                specs.append(pl.BlockSpec(memory_space=pl.ANY))
            else:
                specs.append(pl.BlockSpec(block, place, pipeline_mode=pl.Buffered(1)))
            arrays.append(array)
        else:
            specs.append(pl.BlockSpec(memory_space=pltpu.VMEM))
            arrays.append(a)
    out_specs, shapes = [], []
    for o in outs:
        shapes.append(jax.ShapeDtypeStruct(o[0], o[1]))
        if len(o) > 2:
            out_specs.append(pl.BlockSpec(o[2], o[3], pipeline_mode=pl.Buffered(1)))
        else:
            out_specs.append(pl.BlockSpec(memory_space=pltpu.VMEM))
    moved = sum(o.size * o.dtype.itemsize for o in shapes) + sum(a.size * a.dtype.itemsize for a in arrays)
    return pl.pallas_call(
        kernel,
        out_shape=shapes,
        grid_spec=pltpu.PrefetchScalarGridSpec(
            num_scalar_prefetch=1,
            grid=(1,),
            in_specs=specs,
            out_specs=out_specs,
            scratch_shapes=[pltpu.VMEM(shape, kind) for shape, kind in scratch],
        ),
        input_output_aliases=alias or {},
        compiler_params=pltpu.CompilerParams(vmem_limit_bytes=VMEM_BYTES),
        cost_estimate=pl.CostEstimate(flops=flops // COST, bytes_accessed=moved // COST, transcendentals=0),
    )(meta, *arrays)


def join(meta, parts, all_ref):
    rows = parts[0].shape[0]
    for k, part in enumerate(parts):
        at = pl.multiple_of((meta[0] ^ ORDER[k]) * rows, rows)
        all_ref[pl.ds(at, rows), :] = part[...]


def owners(meta, refs):
    if len(refs) == 1:
        return [(g, refs[0].at[g]) for g in range(refs[0].shape[0])]
    half = refs[0].shape[0]
    found = []
    for k in range(half):
        at = 2 * lax.rem(meta[1] - k + half, half)
        found.append((at + meta[2], refs[0].at[k]))
        found.append((at + 1 - meta[2], refs[1].at[k]))
    return found


def span(g, size):
    if isinstance(g, int):
        return pl.ds(g * size, size)
    return pl.ds(pl.multiple_of(g * size, size), size)


def place_wide(meta, refs, wide):
    rows = wide.shape[0]
    for g, block in owners(meta, refs):
        wide[:, span(g, block.shape[-1])] = block[:rows, :]


def place_io(meta, refs, wi, wo):
    n_grp = wi.shape[1] // 128
    part = wi.shape[0] // n_grp
    q = part // 3
    for g, block in owners(meta, refs):
        for lb in range(n_grp):
            at = lb * 4 * q
            wi[span(g, part), lb * 128 : (lb + 1) * 128] = block[at : at + part, :]
            wo[lb * q : (lb + 1) * q, span(g, 128)] = block[at + part : at + part + q, :]


def part_out(meta, value, at, send, keep):
    rows = value.shape[0] // 4
    w = value.shape[1]
    even = jnp.stack([value[:rows], value[2 * rows : 3 * rows]])
    odd = jnp.stack([value[rows : 2 * rows], value[3 * rows :]])
    low = meta[4] == 0
    keep[:, :, at : at + w] = jnp.where(low, even, odd)
    send[:, :, at : at + w] = jnp.where(low, odd, even).astype(BF)


def masks_of(meta, total, wide, count):
    place = lax.broadcasted_iota(jnp.int32, (total, wide), 0)
    begin = jnp.zeros((total, wide), jnp.int32)
    for k in range(count):
        begin = jnp.where(place >= meta[5 + k], meta[5 + k], begin)
    return place, [None] + [place - lag >= begin for lag in (1, 2)]


def roll_down(v, lag):
    return pltpu.roll(v, lag, 0)


def stream_z(chan, j, wide, rows5, masks):
    at = j * wide
    v = chan[:, at : at + wide].astype(F32)
    z = rows5[4:5, at : at + wide] + rows5[1:2, at : at + wide] * v
    for lag in (1, 2):
        z = z + rows5[1 + lag : 2 + lag, at : at + wide] * jnp.where(masks[lag], roll_down(v, lag), 0.0)
    return z


def spectra(v, long, short):
    half = v.shape[0] // 2
    low = v.astype(BF)
    return dot(long[...], low[:half], 1, 0), dot(short[...], low[half:], 1, 0)


def filt_spectra(filt, long, short0):
    low = filt.astype(BF)
    return dot(long[...], low, 1, 0), dot(short0[...], low[: short0.shape[1]], 1, 0)


def each(long, short, count):
    half = long.shape[0] // 2
    most = short.shape[0] // count // 2
    pairs = [(long[:half], long[half:])]
    for k in range(count):
        pairs.append((short[2 * k * most : (2 * k + 1) * most], short[(2 * k + 1) * most : (2 * k + 2) * most]))
    return pairs


def unspectra(pairs, long_t, short_t):
    half, most = pairs[0][0].shape[0], pairs[1][0].shape[0]
    long = (jnp.concatenate(pairs[0]) * (1.0 / half)).astype(BF)
    short = (jnp.concatenate([v for pair in pairs[1:] for v in pair]) * (1.0 / most)).astype(BF)
    return jnp.concatenate([dot(long_t[...], long, 1, 0), dot(short_t[...], short, 1, 0)])


def exact(a, b, da, db):
    return lax.dot_general(a, b, (((da,), (db,)), ((), ())), precision=HIGH, preferred_element_type=F32)


def mix_forth_kernel(count, nio, raw, meta, *refs):
    parts, refs = refs[:4], refs[4:]
    io, refs = refs[:nio], refs[nio:]
    (long, long_t, short, short_t, short0, second, decay, fout, rows5, skip, gain, shift,
     every, chan, inner_ref, mixed_ref, send, keep, wi, wo) = refs
    join(meta, parts, every)
    if raw:
        every[...] = (every[...].astype(F32) * gain[...] + shift[...]).astype(BF)
    place_io(meta, io, wi, wo)
    total, wide = mixed_ref.shape
    _, masks = masks_of(meta, total, wide, count)
    z = []
    for j in range(3):
        at = j * wide
        proj = dot(every[...], wi[at : at + wide, :], 1, 1) + rows5[0:1, at : at + wide]
        chan[:, at : at + wide] = proj.astype(BF)
        z.append(stream_z(chan, j, wide, rows5, masks))
    prod = z[1] * z[2]
    filt = exact(second[...], fout[...], 1, 0) * decay[...]
    hs = each(*filt_spectra(filt, long, short0), 1)
    xs = each(*spectra(prod, long, short), count)
    ys = [times(*x, *hs[min(k, 1)]) for k, x in enumerate(xs)]
    inner = unspectra(ys, long_t, short_t) + skip[...] * prod
    inner_ref[...] = inner
    mixed_ref[...] = (z[0] * inner).astype(BF)
    for n in range(4):
        w = wo.shape[1] // 4
        part_out(meta, dot(mixed_ref[...], wo[:, n * w : (n + 1) * w], 1, 0), n * w, send, keep)


def mix_back_kernel(count, nio, meta, *refs):
    parts, refs = refs[:4], refs[4:]
    io, refs = refs[:nio], refs[nio:]
    (long, long_t, short, short_t, short0, short0_t, second, decay, fout, rows5, skip, chan, inner,
     every, g_proj_ref, g_fout, g_second, small, send, keep, wi, wo) = refs
    join(meta, parts, every)
    place_io(meta, io, wi, wo)
    total, wide = inner.shape
    place, masks = masks_of(meta, total, wide, count)
    z = [stream_z(chan, j, wide, rows5, masks) for j in range(3)]
    prod = z[1] * z[2]
    filt = exact(second[...], fout[...], 1, 0) * decay[...]
    hs = each(*filt_spectra(filt, long, short0), 1)
    xs = each(*spectra(prod, long, short), count)
    g_y = dot(every[...], wo[...], 1, 1).astype(BF).astype(F32)
    g_conv = g_y * z[0]
    ys = each(*spectra(g_conv, long, short), count)
    corr = unspectra([times_conj(*y, *hs[min(k, 1)]) for k, y in enumerate(ys)], long_t, short_t)
    g_prod = corr + skip[...] * g_conv
    small[...] = jnp.zeros_like(small)
    small[5:6, :wide] = jnp.sum(g_conv * prod, axis=0, keepdims=True)
    for j, g_z in enumerate((g_y * inner[...], g_prod * z[2], g_prod * z[1])):
        at = j * wide
        v = chan[:, at : at + wide].astype(F32)
        small[4:5, at : at + wide] = jnp.sum(g_z, axis=0, keepdims=True)
        small[1:2, at : at + wide] = jnp.sum(g_z * v, axis=0, keepdims=True)
        g_proj = rows5[1:2, at : at + wide] * g_z
        for lag in (1, 2):
            kept = jnp.where(masks[lag], g_z, 0.0)
            small[1 + lag : 2 + lag, at : at + wide] = jnp.sum(kept * roll_down(v, lag), axis=0, keepdims=True)
            moved = jnp.where(place < total - lag, roll_down(kept, total - lag), 0.0)
            g_proj = g_proj + rows5[1 + lag : 2 + lag, at : at + wide] * moved
        low = g_proj.astype(BF)
        g_proj_ref[:, at : at + wide] = low
        small[0:1, at : at + wide] = jnp.sum(low.astype(F32), axis=0, keepdims=True)
    for n in range(4):
        w = wi.shape[1] // 4
        part_out(meta, dot(g_proj_ref[...], wi[:, n * w : (n + 1) * w], 1, 0), n * w, send, keep)
    fs = [times_conj(*y, *x) for y, x in zip(ys, xs)]
    f_short = fs[1]
    for pair in fs[2:]:
        f_short = (f_short[0] + pair[0], f_short[1] + pair[1])
    half, most = fs[0][0].shape[0], f_short[0].shape[0]
    g_filt = dot(long_t[...], (jnp.concatenate(fs[0]) * (1.0 / half)).astype(BF), 1, 0)
    head = dot(short0_t[...], (jnp.concatenate(f_short) * (1.0 / most)).astype(BF), 1, 0)
    g_filt = jnp.concatenate([g_filt[:most] + head, g_filt[most:]]) * decay[...]
    g_fout[...] = exact(second[...].T, g_filt, 1, 0)
    g_second[...] = exact(g_filt, fout[...], 1, 1)


def mlp_forth_kernel(nup, ndown, meta, *refs):
    parts, refs = refs[:4], refs[4:]
    up, refs = refs[:nup], refs[nup:]
    down, refs = refs[:ndown], refs[ndown:]
    b_up, every, hidden, slope, send, keep, wide_up, wide_down = refs
    join(meta, parts, every)
    place_wide(meta, up, wide_up)
    tile = wide_up.shape[1] // 4
    for n in range(4):
        at = n * tile
        pre = dot(every[...], wide_up[:, at : at + tile], 1, 0) + b_up[:, at : at + tile]
        cdf = 0.5 * (1.0 + lax.erf(pre * INV_SQRT2))
        hidden[:, at : at + tile] = (pre * cdf).astype(BF)
        slope[:, at : at + tile] = (cdf + pre * (jnp.exp(-0.5 * pre * pre) * INV_SQRT2PI)).astype(BF)
    place_wide(meta, down, wide_down)
    tile = wide_down.shape[1] // 4
    for n in range(4):
        part_out(meta, dot(hidden[...], wide_down[:, n * tile : (n + 1) * tile], 1, 0), n * tile, send, keep)


def mlp_back_kernel(nup, ndown, meta, *refs):
    parts, refs = refs[:4], refs[4:]
    up, refs = refs[:nup], refs[nup:]
    down, refs = refs[:ndown], refs[ndown:]
    slope, every, g_pre_ref, g_bias, send, keep, wide_up, wide_down = refs
    join(meta, parts, every)
    place_wide(meta, down, wide_down)
    tile = slope.shape[1] // 4
    for n in range(4):
        at = n * tile
        g_hidden = dot(every[...], wide_down[at : at + tile, :], 1, 1)
        g_pre = (g_hidden * slope[:, at : at + tile].astype(F32)).astype(BF)
        g_pre_ref[:, at : at + tile] = g_pre
        g_bias[:, at : at + tile] = jnp.sum(g_pre.astype(F32), axis=0, keepdims=True)
    place_wide(meta, up, wide_up)
    tile = wide_up.shape[0] // 4
    for n in range(4):
        at = n * tile
        part_out(meta, dot(g_pre_ref[...], wide_up[at : at + tile, :], 1, 1), at, send, keep)


def hat_of(value):
    center = value - jnp.mean(value, axis=-1, keepdims=True)
    scale = lax.rsqrt(jnp.mean(center * center, axis=-1, keepdims=True) + EPS)
    return center * scale, scale


def first_norm_kernel(meta, tokens, cotangent, normed, low, sums):
    hat, _ = hat_of(tokens[...].astype(F32))
    normed[...] = hat.astype(BF)
    rounded = cotangent[...].astype(BF)
    low[...] = rounded
    sums[...] = jnp.zeros_like(sums)
    sums[2:3, :] = jnp.sum(rounded.astype(F32), axis=0, keepdims=True)


def add_norm_kernel(meta, state, keep, got, crossed, bias, gain, shift, new, normed):
    value = state[...].astype(F32) + (keep[0] + got[0].astype(F32) + crossed[...].astype(F32)) + bias[...]
    new[...] = value
    hat, _ = hat_of(value)
    normed[...] = (hat * gain[...] + shift[...]).astype(BF)


def add_kernel(meta, state, keep, got, crossed, bias, new):
    new[...] = state[...] + (keep[0] + got[0].astype(F32) + crossed[...].astype(F32)) + bias[...]


def norm_back_kernel(meta, grad, keep, got, crossed, value, gain, new, low, sums):
    g = keep[0] + got[0].astype(F32) + crossed[...].astype(F32)
    hat, scale = hat_of(value[...].astype(F32))
    inner = g * gain[...]
    mean_one = jnp.mean(inner, axis=-1, keepdims=True)
    mean_two = jnp.mean(inner * hat, axis=-1, keepdims=True)
    total = grad[...] + scale * (inner - mean_one - hat * mean_two)
    new[...] = total
    rounded = total.astype(BF)
    low[...] = rounded
    sums[...] = jnp.zeros_like(sums)
    sums[0:1, :] = jnp.sum(g * hat, axis=0, keepdims=True)
    sums[1:2, :] = jnp.sum(g, axis=0, keepdims=True)
    sums[2:3, :] = jnp.sum(rounded.astype(F32), axis=0, keepdims=True)


def mlp_grads_kernel(meta, every, g_pre, hidden, low, out):
    tile = 256
    rows = every.shape[1]
    for n in range(low.shape[1] // tile):
        w = slice(n * tile, (n + 1) * tile)
        for at, left, right in ((0, every, g_pre), (rows, hidden, low)):
            value = dot(left[...], right[:, w], 0, 0).astype(BF)
            out[2 * n, at : at + rows, :] = value[:, :128]
            out[2 * n + 1, at : at + rows, :] = value[:, 128:]


def mlp_split_kernel(meta, every, g_pre, hidden, low, down_send, down_mine, up_send, up_mine):
    tile = 256
    first = meta[2] == 0
    for left, right, send, mine in ((hidden, low, down_send, down_mine), (every, g_pre, up_send, up_mine)):
        for n in range(right.shape[1] // tile):
            value = dot(left[...], right[:, n * tile : (n + 1) * tile], 0, 0).astype(BF)
            one, two = value[:, :128], value[:, 128:]
            mine[n] = jnp.where(first, one, two)
            send[n] = jnp.where(first, two, one)


def io_grads_kernel(split, meta, g_proj, every, mixed, low, *refs):
    outs, (g_in, g_out) = refs[:-2], refs[-2:]
    wide = mixed.shape[1]
    for j in range(g_proj.shape[1] // wide):
        w = slice(j * wide, (j + 1) * wide)
        g_in[w, :] = dot(g_proj[:, w], every[...], 0, 0).astype(BF)
    g_out[...] = dot(mixed[...], low[...], 0, 0).astype(BF)
    n_grp = g_in.shape[1] // 128
    part = g_in.shape[0] // n_grp
    q = part // 3
    if split:
        send, mine = outs
        places = [(2 * k + x, t.at[k]) for k in range(n_grp // 2) for x, t in ((meta[2], mine), (1 - meta[2], send))]
    else:
        places = [(g, outs[0].at[g]) for g in range(n_grp)]
    for g, target in places:
        for lb in range(n_grp):
            at = lb * 4 * q
            target[at : at + part, :] = g_in[span(g, part), lb * 128 : (lb + 1) * 128]
            target[at + part : at + part + q, :] = g_out[lb * q : (lb + 1) * q, span(g, 128)]


def owner_sum_kernel(meta, mine, got, keep, send):
    for k in range(2):
        near = meta[1] ^ (2 * k)
        far = near ^ 1
        keep[k] = mine[near].astype(F32) + got[near].astype(F32)
        send[k] = (mine[far].astype(F32) + got[far].astype(F32)).astype(BF)


def last_sum_kernel(meta, *refs):
    out = refs[-1]
    rows = refs[2].shape[0]
    for k in range(len(refs) // 3):
        keep, got, crossed = refs[3 * k : 3 * k + 3]
        total = keep[0] + got[0].astype(F32) + crossed[...].astype(F32)
        out[k * rows : (k + 1) * rows, :] = total.astype(BF)


def small_last_kernel(meta, *refs):
    pieces, out, held = refs[:-2], refs[-2], refs[-1]
    half = len(pieces)
    for k, v in enumerate(pieces):
        held[lax.rem(meta[1] - k + half, half)] = v[...].astype(F32)
    total = held[0]
    for k in range(1, half):
        total = total + held[k]
    out[...] = total.astype(BF)


def small_turn_kernel(meta, mine, got, own, *sends):
    half = got.shape[0]
    for k, send in enumerate((own,) + sends):
        to = lax.rem(meta[1] + k, half)
        send[...] = (mine[to].astype(F32) + got[to].astype(F32)).astype(BF)


def prep_kernel(small, meta, up, down, w_in, w_out, *refs):
    if small:
        in_bias, conv_weight, conv_bias, skip, fout, up_bias, gain, shift, branch = refs[:9]
        refs = refs[9:]
    io_out, up_out, down_out, turned = refs[:4]
    s = meta[0]
    up_out[...] = up[0]
    n_grp, f, lanes = down.shape[1], down.shape[3], down.shape[4]
    q = w_out.shape[3]
    for g in range(n_grp):
        down_out[g * f : (g + 1) * f, :] = down[0, g, 0]
        io_out[g * 4 * q + 3 * q : (g + 1) * 4 * q, :] = w_out[0, g, 0]
    for k in range(3):
        turned[...] = w_in[0, :, k * lanes : (k + 1) * lanes].astype(F32).T
        piece = turned[span(s, q), :].astype(BF)
        for lb in range(n_grp):
            io_out[lb * 4 * q + k * q : lb * 4 * q + (k + 1) * q, :] = piece[:, lb * 128 : (lb + 1) * 128]
    if not small:
        return
    (rows,) = refs[4:]
    depth = up_bias.shape[0]
    rows[...] = jnp.zeros_like(rows)
    b_in, w_tap, b_tap = in_bias[...].astype(F32), conv_weight[...].astype(F32), conv_bias[...].astype(F32)
    skips = skip[...].astype(F32)
    for l in range(depth):
        at = l * SLOT
        outs = fout[l].astype(F32)
        for b in range(3):
            w = slice(b * lanes, (b + 1) * lanes)
            rows[b, at : at + 1, :] = b_in[l : l + 1, w]
            rows[b, at + 1 : at + 4, :] = w_tap[l][:, w]
            rows[b, at + 4 : at + 5, :] = b_tap[l : l + 1, w]
        rows[3, at : at + 4, :] = outs[60:64]
        rows[3, at + 4 : at + 5, :] = skips[l : l + 1]
        for b in range(4):
            rows[b, at + 5 : at + 20, :] = outs[15 * b : 15 * b + 15]
    lane = lax.broadcasted_iota(jnp.int32, (lanes, lanes), 0)
    to = lax.broadcasted_iota(jnp.int32, (lanes, lanes), 1)
    packed = jnp.zeros((2 * SLOT, lanes), F32)
    for b in range(4):
        hit = (lane == s * q + to - b * q) & (to >= b * q) & (to < (b + 1) * q)
        packed = packed + dot(rows[b].astype(BF), jnp.where(hit, 1.0, 0.0).astype(BF), 1, 0)
    ups = up_bias[:, span(s, lanes)].astype(F32)
    tail = [ups, jnp.zeros((TOK - UP_AT - depth, lanes), F32)]
    for v in (gain, shift, branch):
        v = v[...].astype(F32)
        tail += [v[l] for l in range(depth)]
    base = n_grp * 4 * q
    io_out[base : base + SMALL, :] = jnp.concatenate([packed] + tail).astype(BF)


def unpack_kernel(meta, slab, other, e_wide, e_all, tok, rows5, skip, fout, b_up, wide):
    place_wide(meta, (slab, other), wide)
    depth = fout.shape[0]
    hid = fout.shape[1] // depth
    fout[...] = jnp.zeros_like(fout)
    tok[...] = wide[TOK:SMALL, :].astype(F32)
    low = wide[: 2 * SLOT, :]
    five = dot(low, e_wide[...], 1, 0)
    for l in range(depth):
        rows5[l] = five[l * SLOT : l * SLOT + 5]
        b_up[l] = wide[UP_AT + l : UP_AT + l + 1, :].astype(F32)
    for b in range(4):
        found = dot(low, e_all[b], 1, 0)
        for l in range(depth):
            at, to = l * SLOT, l * hid
            fout[l, to + 15 * b : to + 15 * b + 15, :] = found[at + 5 : at + 20]
            if b == 3:
                fout[l, to + 60 : to + 64, :] = found[at : at + 4]
                skip[l] = found[at + 4 : at + 5]


def net_grads(depth, seconds, net):
    feats_t, one_t, pre0, cos0, freq0, pre1, cos1, freq1, mid = net
    g = seconds[0][...]
    for v in seconds[1:]:
        g = g + v[...]
    lanes = g.shape[1]
    hid = lanes // depth
    g = g * cos1[...]
    g_freq1 = jnp.sum(g * pre1[...], axis=0, keepdims=True)
    g = g * freq1[...]
    g_bias1 = jnp.sum(g, axis=0, keepdims=True)
    full = exact(one_t[...], g, 1, 0)
    lane = lax.broadcasted_iota(jnp.int32, (hid, lanes), 1)
    g_mid = full[:hid]
    for l in range(1, depth):
        g_mid = jnp.where(lane >= l * hid, full[l * hid : (l + 1) * hid], g_mid)
    g = exact(g, mid[...], 1, 1) * cos0[...]
    g_freq0 = jnp.sum(g * pre0[...], axis=0, keepdims=True)
    g = g * freq0[...]
    g_bias0 = jnp.sum(g, axis=0, keepdims=True)
    g_in = exact(feats_t[...], g, 1, 0)
    rows = [g_mid, g_in[:33], g_bias0, g_bias1, g_freq0, g_freq1]
    rows.append(jnp.zeros((NET - hid - 37, lanes), F32))
    return jnp.concatenate(rows)


def pack_kernel(depth, meta, *refs):
    ups, refs = refs[:depth], refs[depth:]
    smalls, refs = refs[:depth], refs[depth:]
    fouts, refs = refs[:depth], refs[depth:]
    toks, refs = refs[: 2 * depth + 1], refs[2 * depth + 1 :]
    seconds, refs = refs[:depth], refs[depth:]
    net, refs = refs[:9], refs[9:]
    e_wide, e_all, send, mine, rows, wide = refs
    chans = fouts[0].shape[1]
    hid = fouts[0].shape[0] // depth
    rows[...] = jnp.zeros_like(rows)
    for l in range(depth):
        at = l * SLOT
        rows[4, at : at + 5, :] = smalls[l][:5, :]
        for b in range(4):
            rows[b, at + 5 : at + 20, :chans] = fouts[l][hid * l + 15 * b : hid * l + 15 * b + 15, :]
        rows[3, at : at + 4, :chans] = fouts[l][hid * l + 60 : hid * l + 64, :]
        rows[3, at + 4 : at + 5, :chans] = smalls[l][5:6, :chans]
    packed = dot(rows[4].astype(BF), e_wide[...], 1, 1)
    for b in range(4):
        packed = packed + dot(rows[b, :, :chans].astype(BF), e_all[b], 1, 1)
    wide[: 2 * SLOT, :] = packed
    wide[2 * SLOT :, :] = jnp.zeros((SMALL - 2 * SLOT, wide.shape[1]), F32)
    for l in range(depth):
        wide[UP_AT + l : UP_AT + l + 1, :] = ups[l][...]
        for i in range(2):
            v = toks[2 * l + i]
            at = TOK + 2 * l + i
            wide[at : at + 1, :] = v[0:1, :]
            wide[at + 2 * depth : at + 2 * depth + 1, :] = v[1:2, :]
            wide[at + 4 * depth : at + 4 * depth + 1, :] = toks[2 * l + i + 1][2:3, :]
    grads = net_grads(depth, seconds, net).astype(BF)
    for k in range(send.shape[0]):
        mine[k, :SMALL] = wide[:, span(2 * k + meta[2], 128)].astype(BF)
        send[k, :SMALL] = wide[:, span(2 * k + 1 - meta[2], 128)].astype(BF)
        mine[k, SMALL:] = grads
        send[k, SMALL:] = grads


def finish_small_kernel(q, meta, *refs):
    parts, refs = refs[:4], refs[4:]
    gain, shift, branch, in_bias, conv_weight, conv_bias, skip, fout, up_bias, g_in, g_mid, g_bias, g_freq, held = refs
    depth = fout.shape[0]
    hid = fout.shape[1]
    lanes = parts[0].shape[1]
    lane = lax.broadcasted_iota(jnp.int32, (lanes, lanes), 0)
    to = lax.broadcasted_iota(jnp.int32, (lanes, lanes), 1)
    for k, part in enumerate(parts):
        held[meta[0] ^ ORDER[k]] = part[...].astype(F32)
    tok = held[0]
    for k in range(1, 4):
        tok = tok + held[k]
    for l in range(depth):
        w = slice(l * hid, (l + 1) * hid)
        at = SMALL + hid
        g_mid[l] = tok[SMALL:at, w]
        g_in[l] = tok[at : at + 33, w]
        g_bias[l] = tok[at + 33 : at + 35, w]
        g_freq[l] = tok[at + 35 : at + 37, w]
    for l in range(depth):
        for t, v in enumerate((gain, shift, branch)):
            at = TOK + 2 * depth * t + 2 * l
            v[l] = tok[at : at + 2]
    for k, part in enumerate(parts):
        up_bias[:, span(meta[0] ^ ORDER[k], lanes)] = part[UP_AT : UP_AT + depth, :].astype(F32)
    for b in range(4):
        found = jnp.zeros((2 * SLOT, lanes), F32)
        for k, part in enumerate(parts):
            s = meta[0] ^ ORDER[k]
            hit = (to - s * q == lane - b * q) & (lane >= b * q) & (lane < (b + 1) * q)
            found = found + dot(part[: 2 * SLOT, :], jnp.where(hit, 1.0, 0.0).astype(BF), 1, 0)
        for l in range(depth):
            at = l * SLOT
            fout[l, 15 * b : 15 * b + 15, :] = found[at + 5 : at + 20]
            if b == 3:
                fout[l, 60:64, :] = found[at : at + 4]
                skip[l : l + 1, :] = found[at + 4 : at + 5]
            else:
                w = slice(b * lanes, (b + 1) * lanes)
                in_bias[l : l + 1, w] = found[at : at + 1]
                conv_weight[l, :, w] = found[at + 1 : at + 4]
                conv_bias[l : l + 1, w] = found[at + 4 : at + 5]


def finish_mlp_kernel(extra, meta, *refs):
    parts, refs = refs[:4], refs[4:]
    up, down = refs[extra:]
    rows = up.shape[1]
    n_grp, f = down.shape[1], down.shape[3]
    for k, part in enumerate(parts):
        s = meta[0] ^ ORDER[k]
        up[0, :, span(s, part.shape[1])] = part[:rows, :].astype(F32)
        for g in range(n_grp):
            down[0, g, s] = part[rows + g * f : rows + (g + 1) * f, :].astype(F32)


def finish_io_kernel(extra, meta, *refs):
    parts, refs = refs[:4], refs[4:]
    g_in, g_out, turned = refs[extra:]
    n_grp, q = g_out.shape[1], g_out.shape[3]
    for k, part in enumerate(parts):
        s = meta[0] ^ ORDER[k]
        for lb in range(n_grp):
            at = lb * 4 * q
            for j in range(3):
                row = pl.ds(pl.multiple_of(j * 4 * q + s * q, q), q)
                turned[row, lb * 128 : (lb + 1) * 128] = part[at + j * q : at + (j + 1) * q, :].astype(F32)
            g_out[0, lb, s] = part[at + 3 * q : at + 4 * q, :].astype(F32)
    for j in range(3):
        g_in[0, :, j * 4 * q : (j + 1) * 4 * q] = turned[j * 4 * q : (j + 1) * 4 * q, :].T


def after(value, *others):
    return lax.optimization_barrier((value,) + others)[0]


def body(
    tokens,
    lengths,
    cotangent,
    norm_gain,
    norm_bias,
    in_weight,
    in_bias,
    conv_weight,
    conv_bias,
    skip_bias,
    filt_out,
    out_weight,
    up_weight,
    up_bias,
    down_weight,
    branch_bias,
    filt_in,
    filt_mid,
    filt_bias,
    sine_freq,
):
    comm = Comm()
    n_grp, n_seq, s, nz = comm.n_grp, comm.n_seq, comm.s, comm.nz
    depth = norm_gain.shape[0]
    tok_rows, width = tokens.shape
    total = tok_rows * n_seq
    half, most = total // 2, total // 4
    cols = width // n_grp
    q = cols // n_seq
    ff_shard = up_weight.shape[2]
    f = ff_shard // n_seq
    hid = filt_out.shape[1]
    chans = n_grp * q
    count = lengths.shape[1]
    lens = lengths[0]
    starts = half + jnp.cumsum(lens) - lens
    meta = jnp.concatenate([jnp.stack([s, comm.z, comm.x, comm.y, comm.c]), starts, lens]).astype(jnp.int32)

    down_view = down_weight.reshape(depth, n_grp, n_seq, f, cols)
    out_view = out_weight.reshape(depth, n_grp, n_seq, q, cols)

    def prepare(l, small):
        args = [
            (up_weight, (1, width, f), lambda i, m: (l, 0, m[0])),
            (down_view, (1, n_grp, 1, f, cols), lambda i, m: (l, 0, m[0], 0, 0)),
            (in_weight, (1, width, 3 * cols), lambda i, m: (l, 0, 0)),
            (out_view, (1, n_grp, 1, q, cols), lambda i, m: (l, 0, m[0], 0, 0)),
        ]
        scratch = [((cols, width), F32)]
        rows = width
        if small:
            args += [in_bias, conv_weight, conv_bias, skip_bias, filt_out, up_bias, norm_gain, norm_bias, branch_bias]
            scratch.append(((4, 2 * SLOT, cols), F32))
            rows += SMALL
        outs = [((rows, cols), BF), ((width, f), BF), ((n_grp * f, cols), BF)]
        return run(lambda *r: prep_kernel(small, *r), outs, meta, args, scratch)

    def by_permutes(unit):
        slab = jnp.stack([unit] + [comm.turn(unit, "grp", n_grp, k) for k in range(1, nz)])
        return [slab, comm.flip(slab, "grp", n_grp)]

    first_units = prepare(0, True)
    hat0, low_first, sums_first = run(
        first_norm_kernel,
        [((tok_rows, width), BF), ((tok_rows, width), BF), ((8, width), F32)], meta, [tokens, cotangent])
    ready = list(first_units)
    for l in range(1, depth):
        ready += prepare(l, False)
    chunks, slab = [], None
    for unit in ready:
        if slab is not None:
            unit = after(unit, slab)
        slab = jnp.stack([unit] + [comm.turn(unit, "grp", n_grp, k) for k in range(1, nz)])
        chunks.append([slab, comm.flip(slab, "grp", n_grp)])
    weights = [tuple(chunks[3 * l : 3 * l + 3]) for l in range(depth)]

    lane_from = jnp.arange(n_grp * cols, dtype=jnp.int32)[:, None]
    lane_wide = jnp.arange(3 * chans, dtype=jnp.int32)[None, :]
    lane_chan = jnp.arange(chans, dtype=jnp.int32)[None, :]
    e_wide = ((lane_from // cols == lane_wide // (3 * q)) & (lane_from % cols == lane_wide % (3 * q))).astype(BF)
    e_all = jnp.stack([
        ((lane_from // cols == lane_chan // q) & (lane_from % cols == b * q + lane_chan % q)) for b in range(4)
    ]).astype(BF)
    slab, other = weights[0][0]
    small_block = ((nz, SMALL, cols), lambda i, m: (0, width // SMALL, 0))
    tok_all, rows5, skip, fout, b_up = run(
        unpack_kernel,
        [((6 * depth, width), F32), ((depth, 5, 3 * chans), F32), ((depth, 1, chans), F32),
         ((depth, depth * hid, chans), F32), ((depth, 1, n_grp * f), F32)],
        meta, [(slab,) + small_block, (other,) + small_block, e_wide, e_all], [((SMALL, width), BF)])
    tok_all = tok_all.reshape(3, depth, 2, 1, width)
    gains, shifts, b_branch = tok_all[0], tok_all[1], tok_all[2]

    mixer = Mixer(lens, total, most)
    long, short, short0 = mixer.long, mixer.short, mixer.short0
    long_t, short_t, short0_t = long.T, short.T, short0.T
    feats, tpos = positions(half)
    channel = (
        jnp.arange(n_grp, dtype=jnp.int32)[:, None] * cols + s * q + jnp.arange(q, dtype=jnp.int32)[None, :]
    ).reshape(-1).astype(F32)
    rate = jnp.abs(FAST + (SLOW - FAST) * channel / (width - 1))
    decay = jnp.exp(-tpos[:, None] * rate[None, :])
    lanes = depth * hid
    bias0, bias1 = (filt_bias[:, i].reshape(1, lanes) for i in range(2))
    freq0, freq1 = (sine_freq[:, i].reshape(1, lanes) for i in range(2))
    mid_all = jnp.zeros((lanes, lanes), F32)
    for l in range(depth):
        mid_all = lax.dynamic_update_slice(mid_all, filt_mid[l], (l * hid, l * hid))
    pre0 = jnp.dot(feats, jnp.transpose(filt_in, (1, 0, 2)).reshape(-1, lanes), precision=HIGH) + bias0
    one, cos0 = jnp.sin(freq0 * pre0), jnp.cos(freq0 * pre0)
    pre1 = jnp.dot(one, mid_all, precision=HIGH) + bias1
    second, cos1 = jnp.sin(freq1 * pre1), jnp.cos(freq1 * pre1)
    feats_t = jnp.pad(feats.T, ((0, -feats.shape[1] % 8), (0, 0)))
    network = [feats_t, one.T, pre0, cos0, freq0, pre1, cos1, freq1, mid_all]

    def gather_parts(v):
        across = comm.turn(v, "seq", n_seq, 1)
        return [v, across, comm.flip(v, "seq", n_seq), comm.flip(across, "seq", n_seq)]

    leaving = []

    def scatter_parts(send, keep):
        got = comm.flip(send, "seq", n_seq)
        other = 1 - comm.y
        crossed = (pick(keep, other, 0) + pick(got, other, 0).astype(F32)).astype(BF)
        own = ((1, tok_rows, width), lambda i, m: (m[3], 0, 0))
        leaving.append(crossed)
        return (keep,) + own, (got,) + own, comm.turn(crossed, "seq", n_seq, 1)

    parts_out = [((2, tok_rows, width), BF), ((2, tok_rows, width), F32)]
    io_scratch = [((3 * chans, width), BF), ((chans, width), BF)]
    mlp_scratch = [((width, n_grp * f), BF), ((n_grp * f, width), BF)]
    state = tokens
    saved = []
    normed = hat0
    for l in range(depth):
        w_io, w_up, w_down = weights[l]
        parts = gather_parts(normed)
        if l == 0:
            low_parts = gather_parts(low_first)
            parts[0] = after(parts[0], *low_parts, chunks[1][0])
        else:
            parts[0] = after(parts[0], chunks[4][0])
        every, chan, inner, mixed, send, keep = run(
            lambda *r, n=len(w_io), raw=l == 0: mix_forth_kernel(count, n, raw, *r),
            [((total, width), BF), ((total, 3 * chans), BF), ((total, chans), F32), ((total, chans), BF)] + parts_out,
            meta,
            parts + w_io + [long, long_t, short, short_t, short0, second, decay, fout[l], rows5[l], skip[l],
                            gains[l, 0], shifts[l, 0]],
            io_scratch,
            flops=3 * 10**9,
        )
        if l:
            send = after(send, chunks[4][1], chunks[5][0])
        got = scatter_parts(send, keep)
        if l == 0:
            state = after(state, chunks[1][1], chunks[2][0])
        mid, normed2 = run(
            add_norm_kernel, [((tok_rows, width), F32), ((tok_rows, width), BF)], meta,
            [state, *got, b_branch[l, 0], gains[l, 1], shifts[l, 1]],
        )
        parts = gather_parts(normed2)
        if l == 0:
            parts[0] = after(parts[0], chunks[2][1], chunks[3][0])
        every2, hidden, slope, send, keep = run(
            lambda *r, n=len(w_up), m=len(w_down): mlp_forth_kernel(n, m, *r),
            [((total, width), BF), ((total, n_grp * f), BF), ((total, n_grp * f), BF)] + parts_out,
            meta, parts + w_up + w_down + [b_up[l]], mlp_scratch,
            flops=4 * 10**9,
        )
        saved.append((state, every, chan, inner, mixed, mid, every2, hidden, slope))
        got = scatter_parts(send, keep)
        if l == 0:
            mid = after(mid, chunks[3][1], chunks[4][0])
        if l + 1 < depth:
            state, normed = run(
                add_norm_kernel, [((tok_rows, width), F32), ((tok_rows, width), BF)], meta,
                [mid, *got, b_branch[l, 1], gains[l + 1, 0], shifts[l + 1, 0]],
            )
        else:
            (state,) = run(add_kernel, [((tok_rows, width), F32)], meta, [mid, *got, b_branch[l, 1]])

    grad = cotangent
    toks = [None] * (2 * depth) + [sums_first]
    g_fouts, g_seconds, smalls, up_biases = ([None] * depth for _ in range(4))

    def hop(v, bit):
        return lax.ppermute(v, "grp", [(i, i ^ bit) for i in range(n_grp)])

    def owner_first(mine, got):
        rows = mine.shape[1:]
        keep, send = run(owner_sum_kernel, [((2,) + rows, F32), ((2,) + rows, BF)], meta, [mine, got])
        return keep, hop(send, 2)

    def owner_second(keep, got):
        return [keep, got, hop((keep[1] + got[1].astype(F32)).astype(BF), 4)]

    def owner_end(*chunks):
        args = []
        for keep, got, crossed in chunks:
            block = ((1,) + crossed.shape, lambda i, m: (0, 0, 0))
            args += [(keep,) + block, (got,) + block, crossed]
        rows, lanes_of = crossed.shape
        return run(last_sum_kernel, [((len(chunks) * rows, lanes_of), BF)], meta, args)[0]

    norm_outs = [((tok_rows, width), F32), ((tok_rows, width), BF), ((8, width), F32)]
    for l in reversed(range(depth)):
        w_io, w_up, w_down = weights[l]
        first, every, chan, inner, mixed, mid, every2, hidden, slope = saved[l]
        low, g_pre, up_biases[l], send, keep = run(
            lambda *r, n=len(w_up), m=len(w_down): mlp_back_kernel(n, m, *r),
            [((total, width), BF), ((total, n_grp * f), BF), ((1, n_grp * f), F32)] + parts_out,
            meta, low_parts + w_up + w_down + [slope], mlp_scratch,
            flops=4 * 10**9,
        )
        got = scatter_parts(send, keep)
        operands = [every2, g_pre, hidden, low]
        if l:
            (g_mlp,) = run(mlp_grads_kernel, [((n_grp, 2 * width, cols), BF)], meta, operands)
            grad = after(grad, g_mlp)
        else:
            down_send, down_mine, up_send, up_mine = run(
                mlp_split_kernel, [((nz, width, cols), BF)] * 4, meta, operands)
            down_got = comm.flip(down_send, "grp", n_grp)
            up_got = comm.flip(up_send, "grp", n_grp)
            grad = after(grad, down_send)
        grad, low_own, toks[2 * l + 1] = run(norm_back_kernel, norm_outs, meta, [grad, *got, mid, gains[l, 1]])
        low_parts = gather_parts(low_own)
        if l:
            mlp_unit = lax.psum_scatter(after(g_mlp, low_own), "grp", scatter_dimension=0, tiled=False)
        if l == 0:
            down_first = owner_first(down_mine, down_got)
            low_parts[0] = after(low_parts[0], down_first[0])
        low, g_proj, g_fouts[l], g_seconds[l], smalls[l], send, keep = run(
            lambda *r, n=len(w_io): mix_back_kernel(count, n, *r),
            [((total, width), BF), ((total, 3 * chans), BF), ((lanes, chans), F32), ((half, lanes), F32),
             ((8, 3 * chans), F32)] + parts_out,
            meta,
            low_parts + w_io + [long, long_t, short, short_t, short0, short0_t, second, decay, fout[l], rows5[l],
                                skip[l], chan, inner],
            io_scratch,
            flops=5 * 10**9,
        )
        got = scatter_parts(send, keep)
        operands = [g_proj, every, mixed, low]
        scratch = [((3 * chans, width), BF), ((chans, width), BF)]
        if l:
            (g_io,) = run(lambda *r: io_grads_kernel(False, *r), [((n_grp, width, cols), BF)], meta, operands, scratch)
            grad = after(grad, g_io)
        else:
            io_send, io_mine = run(
                lambda *r: io_grads_kernel(True, *r), [((nz, width, cols), BF)] * 2, meta, operands, scratch)
            io_got = comm.flip(io_send, "grp", n_grp)
        grad, low_own, toks[2 * l] = run(norm_back_kernel, norm_outs, meta, [grad, *got, first, gains[l, 0]])
        if l:
            low_parts = gather_parts(low_own)
            io_one = lax.psum_scatter(after(g_io, low_own), "grp", scatter_dimension=0, tiled=False)

    def finish(kernel, parts, shapes, old, scratch=()):
        outs = []
        for shape in shapes:
            outs.append(((depth,) + shape, F32, (1,) + shape, lambda i, m, l=l, n=len(shape): (l,) + (0,) * n))
        return run(
            lambda *r, n=len(old): kernel(n, *r), outs, meta, parts + [(v, None, None) for v in old],
            scratch, alias={5: 0, 6: 1} if old else None)

    mlp_shapes = [(width, ff_shard), (n_grp, n_seq, f, cols)]
    io_shapes = [(width, 3 * cols), (n_grp, n_seq, q, cols)]
    turned = [((3 * cols, width), F32)]

    send, mine = run(
        lambda *r: pack_kernel(depth, *r), [((nz, SMALL + NET, cols), BF)] * 2, meta,
        up_biases + smalls + g_fouts + toks + g_seconds + network + [e_wide, e_all],
        [((5, 2 * SLOT, 3 * chans), F32), ((SMALL, width), F32)])
    up_first = owner_first(up_mine, after(up_got, io_send, low_own, down_first[1]))
    down_pieces = owner_second(*down_first)
    io_first = owner_first(io_mine, after(io_got, up_first[0], send))
    up_pieces = owner_second(*up_first)
    parts_one = gather_parts(after(mlp_unit, low_own))
    small_got = after(comm.flip(send, "grp", n_grp), parts_one[1], down_pieces[2], io_first[0])
    small_rows = (SMALL + NET, cols)
    own, *sends = run(small_turn_kernel, [(small_rows, BF)] * nz, meta, [mine, small_got])
    pieces = [own] + [comm.turn(v, "grp", n_grp, k) for k, v in enumerate(sends, 1)]
    io_turn = owner_second(*io_first)
    (small,) = run(small_last_kernel, [(small_rows, BF)], meta, pieces, [((nz,) + small_rows, F32)])
    small_parts = gather_parts(small)

    l = 1
    mlp_grads = finish(finish_mlp_kernel, parts_one, mlp_shapes, [])
    up_pieces[0], state, *mlp_grads = lax.optimization_barrier(
        (after(up_pieces[0], io_first[1], *small_parts), state, *mlp_grads))
    io_grads = finish(finish_io_kernel, gather_parts(after(io_one, *small_parts)), io_shapes, [], turned)
    io_turn[0], *io_grads = lax.optimization_barrier((io_turn[0], *io_grads))
    shared_shapes = [v.shape for v in (filt_in, filt_mid, filt_bias, sine_freq)]
    small_grads = run(
        lambda *r: finish_small_kernel(q, *r),
        [(v.shape, F32) for v in (norm_gain, norm_bias, branch_bias, in_bias, conv_weight, conv_bias, skip_bias,
                                  filt_out, up_bias)] + [(shape, F32) for shape in shared_shapes],
        meta, small_parts, [((n_seq,) + small_rows, F32)])
    io_turn[0], *small_grads = lax.optimization_barrier((io_turn[0], *small_grads))
    (norm_gain_grad, norm_bias_grad, branch_grad, in_bias_grad, taps_grad, tap_bias_grad, skip_grad, fout_grad,
     up_bias_grad, *shared) = small_grads
    l = 0
    mlp_unit = owner_end(up_pieces, down_pieces)
    up_grad, down_grad = finish(finish_mlp_kernel, gather_parts(mlp_unit), mlp_shapes, mlp_grads)
    in_grad, out_grad = finish(finish_io_kernel, gather_parts(owner_end(io_turn)), io_shapes, io_grads, turned)
    return (
        state, grad, norm_gain_grad, norm_bias_grad, in_grad, in_bias_grad, taps_grad, tap_bias_grad,
        skip_grad, fout_grad, out_grad.reshape(depth, width, cols), up_grad, up_bias_grad,
        down_grad.reshape(depth, n_grp * ff_shard, cols), branch_grad, shared[0], shared[1], shared[2], shared[3],
    )


def solution(mesh):
    tok = P(("grp", "seq"), None)
    last3, last2 = P(None, None, "grp"), P(None, "grp")
    in_specs = (
        tok, P("grp", None), tok, last3, last3, last3, last2, last3, last2, last2,
        last3, last3, last3, last2, last3, last3, P(), P(), P(), P(),
    )
    out_specs = (
        tok, tok, last3, last3, last3, last2, last3, last2, last2, last3,
        last3, last3, last2, last3, last3, P(), P(), P(), P(),
    )
    small = mesh.shape["seq"] == 4 and mesh.shape["grp"] == 8
    return jax.shard_map(body if small else body_any, mesh=mesh, in_specs=in_specs, out_specs=out_specs, check_vma=False)
```
